32 devices in a mesh: shot: 8 (over y, x, core), slab: 4 (over z).
Axes of the slice: x: 2, y: 2, z: 4, core: 2. Of those that a mesh axis runs over, the one named last changes fastest.
Arguments:
- velocity: float32 [32, 64, 128], P('slab'), may hold values from 0.2 to 0.4
- wave_state: float32 [2, 8, 2, 32, 64, 128], P(None, 'shot', None, 'slab'), may hold values from -6 to 6
- source_cells: int32 [8, 4], P('shot'), may hold values from 0 to 262143
- source_codes: int32 [8, 4], P('shot'), may hold values from 0 to 7
- wavelets: float32 [8, 2], replicated, may hold values from -48 to 48
- receiver_cells: int32 [8, 256], P('shot'), may hold values from 0 to 262143
- residuals: float32 [8, 2, 256], P('shot'), may hold values from -48 to 48
- momentum: float32 [32, 64, 128], P('slab', 'shot'), may hold values from -6 to 6
- diffusivity: float32 [3, 32, 64, 128], P(None, 'slab', 'shot'), may hold values from 0.02 to 0.15
Outputs:
- final_fields: float32 [8, 2, 32, 64, 128], P('shot', None, 'slab')
- new_momentum: float32 [32, 64, 128], P('slab', 'shot')
- new_velocity: float32 [32, 64, 128], P('slab', 'shot')
The draws below stay inside these ranges and needn't reach their ends.
All inputs are finite; a program needn't handle non-finite values.
Results may differ from the reference program's by a relative error of at most 0.000076.
Values sent between devices are 32-bit elements; how exact they have to be, the bound alone decides.
No kernel may reach another device: no remote copies, remote signals or barrier semaphores. Data moves between devices by JAX's collectives and lax.ppermute only.
A program may use at most 64 MiB of HBM per device.

```python
import math
import jax
import jax.numpy as jnp
from jax import lax

NX = 64
NY = 128
STEPS = 2
SRC = 4
REC = 256
CODES = 8
NZ = 32
GROUPS = 8


def set_ends(values, rng, smallest, largest):
    place = [jax.random.randint(jax.random.fold_in(rng, axis), (), 0, length) for axis, length in enumerate(values.shape)]
    widest = values.shape.index(max(values.shape))
    beside = place[:widest] + [(place[widest] + 1) % values.shape[widest]] + place[widest + 1:]
    return values.at[tuple(place)].set(smallest).at[tuple(beside)].set(largest)


def shard_levels(stream_key, extent, split, smallest, high):
    def one(dim, parts):
        heights = jax.random.uniform(jax.random.fold_in(jax.random.fold_in(stream_key, 6), dim), (parts,), jnp.float32, smallest / len(split), high / len(split))
        return jnp.repeat(jnp.exp(heights), extent[dim] // parts).reshape((-1,) + (1,) * (len(extent) - dim - 1))

    level = one(*split[0])
    for cut in split[1:]:
        level = level * one(*cut)
    return level


def normal_values(own_key, shape, width, most, cuts=(), kind=jnp.bfloat16):
    entries = jax.random.normal(own_key, shape, jnp.float32) * width
    if len(cuts) > 0:
        entries = shard_levels(own_key, shape, cuts, -0.22, 0.18) * entries
    return jnp.clip(entries, min=-most, max=most).astype(kind)


def setup_inputs(seed: int = 0) -> dict:
    streams_of = jax.random.split(jax.random.key(seed), 10)
    velocity = jnp.clip(0.2 + 0.2 * jax.random.uniform(streams_of[0], (NZ, NX, NY), jnp.float32) ** shard_levels(streams_of[0], (NZ, NX, NY), ((0, 4),), -0.2, 0.2), 0.2, 0.4)
    wave_state = normal_values(streams_of[1], (2, GROUPS, 2, NZ, NX, NY), 1.0, 6.0, ((1, 8), (3, 4)), jnp.float32)
    source_cells = set_ends(jax.random.randint(streams_of[2], (GROUPS, SRC), 0, NZ * NX * NY), jax.random.fold_in(streams_of[2], 1), 0, (NZ * NX * NY) - 1).astype(jnp.int32)
    source_codes = set_ends(jax.random.randint(streams_of[3], (GROUPS, SRC), 0, CODES), jax.random.fold_in(streams_of[3], 1), 0, CODES - 1).astype(jnp.int32)
    wavelets = normal_values(streams_of[4], (CODES, STEPS), 8.0, 48.0, (), jnp.float32)
    receiver_cells = set_ends(jax.random.randint(streams_of[5], (GROUPS, REC), 0, NZ * NX * NY), jax.random.fold_in(streams_of[5], 1), 0, (NZ * NX * NY) - 1).astype(jnp.int32)
    residuals = normal_values(streams_of[6], (GROUPS, STEPS, REC), 8.0, 48.0, ((0, 8),), jnp.float32)
    momentum = normal_values(streams_of[7], (NZ, NX, NY), 1.0, 6.0, ((0, 4), (1, 8)), jnp.float32)
    diffusivity = jnp.clip(0.02 + 0.13000001 * jax.random.uniform(streams_of[8], (3, NZ, NX, NY), jnp.float32) ** shard_levels(streams_of[8], (3, NZ, NX, NY), ((1, 4), (2, 8)), -0.2, 0.2), 0.02, 0.15)
    return dict(velocity=velocity, wave_state=wave_state, source_cells=source_cells, source_codes=source_codes, wavelets=wavelets, receiver_cells=receiver_cells, residuals=residuals, momentum=momentum, diffusivity=diffusivity)


STENCIL_TAPS = (-205.0 / 72.0, 8.0 / 5.0, -1.0 / 5.0, 8.0 / 315.0, -1.0 / 560.0)

def laplacian(padded):
    leading = padded.ndim - 2
    lateral = jnp.pad(padded, [(0, 0)] * leading + [(4, 4), (4, 4)])
    row_count = padded.shape[-3] - 8
    size_x = padded.shape[-2]
    size_y = padded.shape[-1]

    def shifted(off_z, off_x, off_y):
        return lateral[..., 4 + off_z:4 + off_z + row_count, 4 + off_x:4 + off_x + size_x, 4 + off_y:4 + off_y + size_y]
    summed = 3.0 * STENCIL_TAPS[0] * shifted(0, 0, 0)
    for radius in range(1, 5):
        cycle_sum = shifted(radius, 0, 0) + shifted(-radius, 0, 0) + shifted(0, radius, 0) + shifted(0, -radius, 0) + shifted(0, 0, radius) + shifted(0, 0, -radius)
        summed = summed + STENCIL_TAPS[radius] * cycle_sum
    return summed

def smooth_step(extended, kappas):
    lateral = jnp.pad(extended, ((0, 0), (0, 0), (1, 1)))
    centre = extended[1:-1, 1:-1, :]
    along_z = extended[2:, 1:-1, :] - 2.0 * centre + extended[:-2, 1:-1, :]
    along_x = extended[1:-1, 2:, :] - 2.0 * centre + extended[1:-1, :-2, :]
    along_y = lateral[1:-1, 1:-1, 2:] - 2.0 * centre + lateral[1:-1, 1:-1, :-2]
    return centre + kappas[0] * along_z + kappas[1] * along_x + kappas[2] * along_y

def reference(velocity, wave_state, source_cells, source_codes, wavelets, receiver_cells, residuals, momentum, diffusivity):
    speed_sq = velocity * velocity
    amplitude = wavelets[source_codes]
    volume = NZ * NX * NY

    def one_group(imaging, inputs):
        previous, current, src_ids, src_amounts, rec_ids, rec_amounts = inputs
        for moment in range(STEPS):
            padded = jnp.pad(current, ((0, 0), (4, 4), (0, 0), (0, 0)))
            source_grid = jnp.zeros((volume,), jnp.float32).at[src_ids].add(src_amounts[:, moment]).reshape(NZ, NX, NY)
            rec_grid = jnp.zeros((volume,), jnp.float32).at[rec_ids].add(rec_amounts[moment]).reshape(NZ, NX, NY)
            driven = speed_sq * (laplacian(padded) + jnp.stack([source_grid, rec_grid]))
            imaging = imaging + driven[0] * current[1]
            previous, current = (current, 2.0 * current - previous + driven)
        return (imaging, current)
    imaging, finals = lax.scan(one_group, jnp.zeros((NZ, NX, NY), jnp.float32), (wave_state[0], wave_state[1], source_cells, amplitude, receiver_cells, residuals))
    gradient = -0.2 * imaging / (velocity * math.sqrt(GROUPS * STEPS))
    smoothed = gradient
    for repeat in range(2):
        smoothed = smooth_step(jnp.pad(smoothed, ((1, 1), (1, 1), (0, 0))), diffusivity)
    new_momentum = 0.9 * momentum + smoothed
    new_velocity = velocity - 0.02 * new_momentum
    return (finals, new_momentum, new_velocity)
```

```python
import functools
import math

import jax
import jax.numpy as jnp
from jax import lax
from jax.experimental import pallas as pl
from jax.experimental.pallas import tpu as pltpu
from jax.sharding import PartitionSpec as P

STENCIL_TAPS = (-205.0 / 72.0, 8.0 / 5.0, -1.0 / 5.0, 8.0 / 315.0, -1.0 / 560.0)
RADIUS = 4
PAD = 8
STEPS = 2
F32 = jnp.float32


def even_pairs(count):
    return [(i, i ^ 1) for i in range(count) if (i ^ 1) < count]


def odd_pairs(count):
    low = [(i, i + 1) for i in range(1, count - 1, 2)]
    return low + [(b, a) for a, b in low]


def run_copies(pairs, sems):
    copies = [pltpu.make_async_copy(src, dst, sems.at[k]) for k, (src, dst) in enumerate(pairs)]
    for copy in copies:
        copy.start()
    return copies


def call(body, out_shapes, operands, in_specs=None, out_specs=None, scratch=(), aliases=None, flops=0):
    moved = sum(math.prod(o.shape) * 4 for o in operands) + sum(math.prod(o.shape) * 4 for o in out_shapes)
    whole = pl.BlockSpec(memory_space=pl.ANY)
    return pl.pallas_call(
        body,
        out_shape=list(out_shapes),
        in_specs=[whole if s == "any" else pl.BlockSpec(memory_space=pltpu.SMEM) if s == "smem" else pl.BlockSpec() for s in in_specs],
        out_specs=[whole if s == "any" else pl.BlockSpec() for s in out_specs],
        scratch_shapes=list(scratch),
        input_output_aliases=aliases or {},
        cost_estimate=pl.CostEstimate(flops=flops, bytes_accessed=moved, transcendentals=0),
    )(*operands)


def shape(*dims):
    return jax.ShapeDtypeStruct(dims, F32)


def y_sums(centre, lane, size_y):
    sums = []
    for r in range(1, RADIUS + 1):
        before = jnp.where(lane >= r, pltpu.roll(centre, r, 1), 0.0)
        after = jnp.where(lane < size_y - r, pltpu.roll(centre, size_y - r, 1), 0.0)
        sums.append(before + after)
    return sums


def laplacian_row(field, z, rows, size_x, size_y, lane):
    centre = field[z, PAD : PAD + size_x, :]
    along_y = y_sums(centre, lane, size_y)
    total = (3.0 * STENCIL_TAPS[0]) * centre
    for r in range(1, RADIUS + 1):
        ring = along_y[r - 1]
        ring = ring + (field[z, PAD + r : PAD + r + size_x, :] + field[z, PAD - r : PAD - r + size_x, :])
        if z + r < rows:
            ring = ring + field[z + r, PAD : PAD + size_x, :]
        if z - r >= 0:
            ring = ring + field[z - r, PAD : PAD + size_x, :]
        total = total + STENCIL_TAPS[r] * ring
    return total


def clear_sides(field, size_x):
    rows, _, size_y = field.shape
    edge = jnp.zeros((rows, PAD, size_y), F32)
    field[:, 0:PAD, :] = edge
    field[:, PAD + size_x : PAD + size_x + PAD, :] = edge


def pack_body(state, velocity, out_a, out_b, sems):
    depth = velocity.shape[0]
    even = lax.rem(lax.axis_index("slab"), 2) == 0
    at_a = jnp.where(even, depth - RADIUS, 0)
    at_b = jnp.where(even, 0, depth - RADIUS)
    pairs = []
    for out, at in ((out_a, at_a), (out_b, at_b)):
        pairs.append((state.at[1, 0, 0, pl.ds(at, RADIUS)], out.at[0:RADIUS]))
        pairs.append((state.at[1, 0, 1, pl.ds(at, RADIUS)], out.at[RADIUS : 2 * RADIUS]))
        pairs.append((velocity.at[pl.ds(at, RADIUS)], out.at[2 * RADIUS : 3 * RADIUS]))
    for copy in run_copies(pairs, sems):
        copy.wait()


def partial_u_body(state, velocity, kappa, partial, image, out_a, out_b, field, older, adjoint, speed, sems):
    depth, size_x, size_y = velocity.shape
    strip = kappa.shape[2]
    copies = run_copies(
        [
            (state.at[1, 0, 0], field.at[:, PAD : PAD + size_x]),
            (velocity, speed),
            (state.at[0, 0, 0], older),
            (state.at[1, 0, 1], adjoint),
        ],
        sems,
    )
    clear_sides(field, size_x)
    even = lax.rem(lax.axis_index("slab"), 2) == 0
    for j in range(3):
        tail = kappa[j, depth - 1]
        head = kappa[j, 0]
        at = RADIUS * size_x + j * strip
        out_a[at : at + strip, :] = jnp.where(even, tail, head)
        out_b[at : at + strip, :] = jnp.where(even, head, tail)
    lane = lax.broadcasted_iota(jnp.int32, (size_x, size_y), 1)
    for copy in copies:
        copy.wait()
    for z in range(depth):
        centre = field[z, PAD : PAD + size_x, :]
        v = speed[z]
        drive = (v * v) * laplacian_row(field, z, depth, size_x, size_y, lane)
        partial[z] = (2.0 * centre - older[z]) + drive
        image[z] = drive * adjoint[z]
    for k in range(RADIUS):
        tail = partial[depth - RADIUS + k]
        head = partial[k]
        out_a[k * size_x : (k + 1) * size_x, :] = jnp.where(even, tail, head)
        out_b[k * size_x : (k + 1) * size_x, :] = jnp.where(even, head, tail)


def partial_q_body(
    state, velocity, cells, residuals, kappa, partial, push, side_a, side_b, field, older, speed, grid_now, sems
):
    depth, size_x, size_y = velocity.shape
    strip = kappa.shape[2]
    copies = run_copies(
        [(state.at[1, 0, 1], field.at[:, PAD : PAD + size_x]), (velocity, speed), (state.at[0, 0, 1], older)], sems
    )
    clear_sides(field, size_x)
    even_strip = lax.rem(lax.axis_index("shot"), 2) == 0
    for j in range(3):
        tail = kappa[j, :, strip - 1, :]
        head = kappa[j, :, 0, :]
        side_a[j * depth : (j + 1) * depth, :] = jnp.where(even_strip, tail, head)
        side_b[j * depth : (j + 1) * depth, :] = jnp.where(even_strip, head, tail)
    volume = depth * size_x * size_y
    count = cells.shape[1]
    ids = cells[...] - lax.axis_index("slab") * volume
    inside = (ids >= 0) & (ids < volume)
    kept = jnp.where(inside, ids, 0)
    row = lax.div(kept, jnp.int32(size_y))
    column = kept - row * size_y
    rows = depth * size_x
    pick_row = (lax.broadcasted_iota(jnp.int32, (rows, count), 0) == row).astype(F32)
    pick_column = lax.broadcasted_iota(jnp.int32, (size_y, count), 0) == column
    for moment in range(STEPS):
        amounts = jnp.where(inside, residuals[0, moment : moment + 1, :], 0.0)
        grid_now[moment] = lax.dot_general(
            pick_row,
            jnp.where(pick_column, amounts, 0.0),
            (((1,), (1,)), ((), ())),
            precision=lax.Precision.HIGHEST,
            preferred_element_type=F32,
        )
    lane = lax.broadcasted_iota(jnp.int32, (size_x, size_y), 1)
    for copy in copies:
        copy.wait()
    for z in range(depth):
        centre = field[z, PAD : PAD + size_x, :]
        v = speed[z]
        vv = v * v
        at = slice(z * size_x, (z + 1) * size_x)
        drive = vv * (laplacian_row(field, z, depth, size_x, size_y, lane) + grid_now[0, at, :])
        partial[z] = (2.0 * centre - older[z]) + drive
        push[z] = vv * grid_now[1, at, :]


def image_body(
    state,
    velocity,
    partial_u,
    image0,
    partial_q,
    first_a,
    first_b,
    second_a,
    second_b,
    cells,
    codes,
    wavelets,
    fields,
    keep,
    send,
    q_next,
    edge_a,
    edge_b,
    speed,
    u_old,
    q_old,
    u_now,
    image,
    u_out,
    sems,
    out_sem,
    *,
    scale,
):
    depth, size_x, size_y = velocity.shape
    whole = depth + 2 * RADIUS
    own = slice(RADIUS, RADIUS + depth)
    here = lax.axis_index("slab")
    even = lax.rem(here, 2) == 0
    at_a = jnp.where(even, RADIUS + depth, 0)
    at_b = jnp.where(even, 0, RADIUS + depth)
    middle = slice(PAD, PAD + size_x)
    pairs = [
        (state.at[1, 0, 0], u_old.at[own]),
        (state.at[1, 0, 1], q_old.at[own]),
        (velocity, speed.at[own]),
        (partial_u, u_now.at[own, middle]),
        (image0, image.at[:, middle]),
        (partial_q, q_next),
    ]
    for got, at in ((first_a, at_a), (first_b, at_b)):
        pairs.append((got.at[0:RADIUS], u_old.at[pl.ds(at, RADIUS)]))
        pairs.append((got.at[RADIUS : 2 * RADIUS], q_old.at[pl.ds(at, RADIUS)]))
        pairs.append((got.at[2 * RADIUS : 3 * RADIUS], speed.at[pl.ds(at, RADIUS)]))
    for got, at in ((second_a, at_a), (second_b, at_b)):
        for k in range(RADIUS):
            pairs.append((got.at[k * size_x : (k + 1) * size_x], u_now.at[at + k, middle]))
    copies = run_copies(pairs, sems)
    clear_sides(u_now, size_x)
    clear_sides(image, size_x)
    lane = lax.broadcasted_iota(jnp.int32, (size_x, size_y), 1)
    row_lane = lax.broadcasted_iota(jnp.int32, (1, size_y), 1)
    for copy in copies:
        copy.wait()

    def across(field, z, inner):
        total = None
        for r in range(1, RADIUS + 1):
            for other in (z - r, z + r):
                if 0 <= other < whole and (RADIUS <= other < RADIUS + depth) != inner:
                    term = STENCIL_TAPS[r] * field[other]
                    total = term if total is None else total + term
        return total

    for z in range(whole):
        inner = RADIUS <= z < RADIUS + depth
        crossing = across(u_old, z, inner)
        v = speed[z]
        vv = v * v
        if crossing is not None:
            change = vv * crossing
            u_now[z, middle, :] = u_now[z, middle, :] + change
            if inner:
                image[z - RADIUS, middle, :] = image[z - RADIUS, middle, :] + change * q_old[z]
        if inner:
            crossing = across(q_old, z, True)
            if crossing is not None:
                q_next[z - RADIUS] = q_next[z - RADIUS] + vv * crossing

    plane = size_x * size_y
    first = here * depth - RADIUS

    def points(moment, act):
        for k in range(cells.shape[1]):
            cell = cells[0, k]
            amount = wavelets[codes[0, k], moment]
            z = lax.div(cell, plane) - first
            rest = lax.rem(cell, plane)
            x = lax.div(rest, size_y)
            y = lax.rem(rest, size_y)
            act(z, x, jnp.where(row_lane == y, amount, 0.0))

    def first_step(z, x, spot):
        @pl.when((z >= 0) & (z < whole))
        def _():
            v = speed[z, pl.ds(x, 1), :]
            change = (v * v) * spot
            u_now[z, pl.ds(PAD + x, 1), :] = u_now[z, pl.ds(PAD + x, 1), :] + change

            @pl.when((z >= RADIUS) & (z < RADIUS + depth))
            def _():
                at = (z - RADIUS, pl.ds(PAD + x, 1), slice(None))
                image[at] = image[at] + change * q_old[z, pl.ds(x, 1), :]

    points(0, first_step)

    for z in range(depth):
        v = speed[z + RADIUS]
        drive = (v * v) * laplacian_row(u_now, z + RADIUS, whole, size_x, size_y, lane)
        u_out[z] = (2.0 * u_now[z + RADIUS, middle, :] - u_old[z + RADIUS]) + drive
        image[z, middle, :] = image[z, middle, :] + drive * q_next[z]

    def second_step(z, x, spot):
        @pl.when((z >= RADIUS) & (z < RADIUS + depth))
        def _():
            v = speed[z, pl.ds(x, 1), :]
            change = (v * v) * spot
            to = z - RADIUS
            u_out[to, pl.ds(x, 1), :] = u_out[to, pl.ds(x, 1), :] + change
            at = (to, pl.ds(PAD + x, 1), slice(None))
            image[at] = image[at] + change * q_next[to, pl.ds(x, 1), :]

    points(1, second_step)
    copy_out = pltpu.make_async_copy(u_out, fields.at[0, 0], out_sem)
    copy_out.start()

    for z in range(depth):
        image[z, middle, :] = (-0.2 * image[z, middle, :]) / (speed[z + RADIUS] * scale)
    me = lax.axis_index("shot")
    core = lax.rem(me, 2)
    chip = lax.div(me, 2)
    chips = keep.shape[0]
    strip = size_x // (2 * chips)
    wide = strip + 4
    for m in range(chips):
        to = jnp.bitwise_xor(chip, m)
        for z in range(depth):
            at = PAD + 2 * m * strip - 2
            low = image[z, at : at + wide, :]
            high = image[z, at + strip : at + strip + wide, :]
            keep[to, z * wide : (z + 1) * wide, :] = jnp.where(core == 0, low, high)
            send[to, z * wide : (z + 1) * wide, :] = jnp.where(core == 0, high, low)
    for k in range(RADIUS):
        tail = q_next[depth - RADIUS + k]
        head = q_next[k]
        edge_a[k] = jnp.where(even, tail, head)
        edge_b[k] = jnp.where(even, head, tail)
    copy_out.wait()


def pair_sum_body(keep, got, *outs):
    for k, out in enumerate(outs):
        out[...] = keep[k] + got[k]


def strip_sum_body(*refs, count, wide):
    parts, (total, edge_a, edge_b) = refs[:count], refs[count:]
    added = parts[0][...]
    for part in parts[1:]:
        added = added + part[...]
    total[...] = added
    even = lax.rem(lax.axis_index("slab"), 2) == 0
    rows = total.shape[0]
    head = total[0 : 2 * wide, :]
    tail = total[rows - 2 * wide : rows, :]
    edge_a[...] = jnp.where(even, tail, head)
    edge_b[...] = jnp.where(even, head, tail)


def adjoint_body(fields_in, state, velocity, q_next, push, got_a, got_b, fields, field, q_out, sems, out_sem):
    depth, size_x, size_y = velocity.shape
    whole = depth + 2 * RADIUS
    even = lax.rem(lax.axis_index("slab"), 2) == 0
    at_a = jnp.where(even, RADIUS + depth, 0)
    at_b = jnp.where(even, 0, RADIUS + depth)
    middle = slice(PAD, PAD + size_x)
    copies = run_copies(
        [
            (q_next, field.at[RADIUS : RADIUS + depth, middle]),
            (got_a, field.at[pl.ds(at_a, RADIUS), middle]),
            (got_b, field.at[pl.ds(at_b, RADIUS), middle]),
            (state.at[1, 0, 1], q_out),
        ],
        sems,
    )
    clear_sides(field, size_x)
    lane = lax.broadcasted_iota(jnp.int32, (size_x, size_y), 1)
    for copy in copies:
        copy.wait()
    for z in range(depth):
        v = velocity[z]
        drive = (v * v) * laplacian_row(field, z + RADIUS, whole, size_x, size_y, lane) + push[z]
        q_out[z] = (2.0 * field[z + RADIUS, middle, :] - q_out[z]) + drive
    copy = pltpu.make_async_copy(q_out, fields.at[0, 1], out_sem)
    copy.start()
    copy.wait()


def smooth_body(
    total, got_a, got_b, kappa, second_a, second_b, side_a, side_b, speed, momentum, new_momentum, new_speed, grad, half, coef,
    *, size_x
):
    depth, strip, size_y = speed.shape
    wide = strip + 4
    even = lax.rem(lax.axis_index("slab"), 2) == 0
    even_strip = lax.rem(lax.axis_index("shot"), 2) == 0
    for k in range(2):
        at = slice(k * wide, (k + 1) * wide)
        grad[k, 0:wide, :] = jnp.where(even, got_b[at, :], got_a[at, :])
        grad[depth + 2 + k, 0:wide, :] = jnp.where(even, got_a[at, :], got_b[at, :])
    for z in range(depth):
        grad[z + 2, 0:wide, :] = total[z * wide : (z + 1) * wide, :]
    coef[...] = jnp.zeros(coef.shape, F32)
    for j in range(3):
        at = slice(RADIUS * size_x + j * strip, RADIUS * size_x + (j + 1) * strip)
        coef[j, 0, 1 : strip + 1, :] = jnp.where(even, second_b[at, :], second_a[at, :])
        coef[j, depth + 1, 1 : strip + 1, :] = jnp.where(even, second_a[at, :], second_b[at, :])
        left = jnp.where(even_strip, side_b[j * depth : (j + 1) * depth, :], side_a[j * depth : (j + 1) * depth, :])
        right = jnp.where(even_strip, side_a[j * depth : (j + 1) * depth, :], side_b[j * depth : (j + 1) * depth, :])
        for z in range(depth):
            coef[j, z + 1, 1 : strip + 1, :] = kappa[j, z]
            coef[j, z + 1, 0:1, :] = left[z : z + 1, :]
            coef[j, z + 1, strip + 1 : strip + 2, :] = right[z : z + 1, :]

    def step(source, z, rows, factors):
        centre = source[z, 1 : 1 + rows, :]
        lane = lax.broadcasted_iota(jnp.int32, centre.shape, 1)
        twice = 2.0 * centre
        along_z = source[z + 1, 1 : 1 + rows, :] - twice + source[z - 1, 1 : 1 + rows, :]
        along_x = source[z, 2 : 2 + rows, :] - twice + source[z, 0:rows, :]
        after = jnp.where(lane < size_y - 1, pltpu.roll(centre, size_y - 1, 1), 0.0)
        before = jnp.where(lane >= 1, pltpu.roll(centre, 1, 1), 0.0)
        along_y = after - twice + before
        return centre + factors[0] * along_z + factors[1] * along_x + factors[2] * along_y

    for z in range(depth + 2):
        half[z, 0 : strip + 2, :] = step(grad, z + 1, strip + 2, [coef[j, z, 0 : strip + 2, :] for j in range(3)])
    for z in range(depth):
        smoothed = step(half, z + 1, strip, [kappa[j, z] for j in range(3)])
        fresh = 0.9 * momentum[z] + smoothed
        new_momentum[z] = fresh
        new_speed[z] = speed[z] - 0.02 * fresh


def on_device(
    velocity,
    wave_state,
    source_cells,
    source_codes,
    wavelets,
    receiver_cells,
    residuals,
    momentum,
    diffusivity,
):
    depth, size_x, size_y = velocity.shape
    strip = momentum.shape[1]
    wide = strip + 4
    slabs = lax.axis_size("slab")
    shots = lax.axis_size("shot")
    chips = shots // 2
    z_even, z_odd = even_pairs(slabs), odd_pairs(slabs)
    cube = (depth, size_x, size_y)
    padded = (depth, size_x + 2 * PAD, size_y)
    whole = depth + 2 * RADIUS
    stencil = 45 * depth * size_x * size_y
    dma = pltpu.SemaphoreType.DMA

    block = shape(3 * RADIUS, size_x, size_y)
    out_a, out_b = call(
        pack_body, [block] * 2, (wave_state, velocity), ["any"] * 2, ["vmem"] * 2, [dma((6,))]
    )
    first_a = lax.ppermute(out_a, "slab", z_even)
    first_b = lax.ppermute(out_b, "slab", z_odd)

    flat = shape(RADIUS * size_x + 3 * strip, size_y)
    partial_u, image0, out_a, out_b = call(
        partial_u_body,
        [shape(*cube), shape(*cube), flat, flat],
        (wave_state, velocity, diffusivity),
        ["any", "any", "vmem"],
        ["vmem"] * 4,
        [pltpu.VMEM(padded, F32), pltpu.VMEM(cube, F32), pltpu.VMEM(cube, F32), pltpu.VMEM(cube, F32), dma((4,))],
        flops=stencil,
    )
    second_a = lax.ppermute(out_a, "slab", z_even)
    second_b = lax.ppermute(out_b, "slab", z_odd)

    side = shape(3 * depth, size_y)
    partial_q, push, out_a, out_b = call(
        partial_q_body,
        [shape(*cube), shape(*cube), side, side],
        (wave_state, velocity, receiver_cells, residuals, diffusivity),
        ["any", "any", "vmem", "vmem", "vmem"],
        ["vmem"] * 4,
        [
            pltpu.VMEM(padded, F32),
            pltpu.VMEM(cube, F32),
            pltpu.VMEM(cube, F32),
            pltpu.VMEM((STEPS, depth * size_x, size_y), F32),
            dma((3,)),
        ],
        flops=2 * stencil,
    )
    side_a = lax.ppermute(out_a, "shot", even_pairs(shots))
    side_b = lax.ppermute(out_b, "shot", odd_pairs(shots))
    speed_strip = lax.dynamic_slice_in_dim(velocity, lax.axis_index("shot") * strip, strip, 1)

    part = shape(chips, depth * wide, size_y)
    edge = shape(RADIUS, size_x, size_y)
    extended = (whole, size_x, size_y)
    fields, keep, send, q_next, out_a, out_b = call(
        functools.partial(image_body, scale=math.sqrt(shots * STEPS)),
        [shape(1, 2, *cube), part, part, shape(*cube), edge, edge],
        (
            wave_state,
            velocity,
            partial_u,
            image0,
            partial_q,
            first_a,
            first_b,
            second_a,
            second_b,
            source_cells,
            source_codes,
            wavelets,
        ),
        ["any"] * 9 + ["smem"] * 3,
        ["any"] + ["vmem"] * 5,
        [
            pltpu.VMEM(extended, F32),
            pltpu.VMEM(extended, F32),
            pltpu.VMEM(extended, F32),
            pltpu.VMEM((whole, size_x + 2 * PAD, size_y), F32),
            pltpu.VMEM(padded, F32),
            pltpu.VMEM(cube, F32),
            dma((12 + 2 * RADIUS,)),
            dma,
        ],
        flops=2 * stencil,
    )
    got = lax.ppermute(send, "shot", even_pairs(shots))
    row_block = shape(depth * wide, size_y)
    parts = call(pair_sum_body, [row_block] * chips, (keep, got), ["vmem"] * 2, ["vmem"] * chips)
    arrived = [
        parts[0] if k == 0 else lax.ppermute(parts[k], "shot", [(i, i ^ (2 * k)) for i in range(shots)])
        for k in range(chips)
    ]
    edge_a = lax.ppermute(out_a, "slab", z_even)
    edge_b = lax.ppermute(out_b, "slab", z_odd)
    two = shape(2 * wide, size_y)
    total, out_a, out_b = call(
        functools.partial(strip_sum_body, count=chips, wide=wide),
        [row_block, two, two],
        arrived,
        ["vmem"] * chips,
        ["vmem"] * 3,
    )
    grad_a = lax.ppermute(out_a, "slab", z_even)
    grad_b = lax.ppermute(out_b, "slab", z_odd)
    (fields,) = call(
        adjoint_body,
        [shape(1, 2, *cube)],
        (fields, wave_state, velocity, q_next, push, edge_a, edge_b),
        ["any", "any", "vmem", "any", "vmem", "any", "any"],
        ["any"],
        [
            pltpu.VMEM((whole, size_x + 2 * PAD, size_y), F32),
            pltpu.VMEM(cube, F32),
            dma((4,)),
            dma,
        ],
        aliases={0: 0},
        flops=stencil,
    )
    tall = 8 * ((wide + 7) // 8)
    new_momentum, new_velocity = call(
        functools.partial(smooth_body, size_x=size_x),
        [shape(*momentum.shape)] * 2,
        (total, grad_a, grad_b, diffusivity, second_a, second_b, side_a, side_b, speed_strip, momentum),
        ["vmem"] * 10,
        ["vmem"] * 2,
        [
            pltpu.VMEM((depth + 4, tall, size_y), F32),
            pltpu.VMEM((depth + 2, tall, size_y), F32),
            pltpu.VMEM((3, depth + 2, tall, size_y), F32),
        ],
    )
    return (fields, new_momentum, new_velocity)


def solution(mesh):
    return jax.shard_map(
        on_device,
        mesh=mesh,
        in_specs=(
            P("slab", None, None),
            P(None, "shot", None, "slab", None, None),
            P("shot", None),
            P("shot", None),
            P(),
            P("shot", None),
            P("shot", None, None),
            P("slab", "shot", None),
            P(None, "slab", "shot", None),
        ),
        out_specs=(
            P("shot", None, "slab", None, None),
            P("slab", "shot", None),
            P("slab", "shot", None),
        ),
        check_vma=False,
    )
```

```python
import functools
import math

import jax
import jax.numpy as jnp
from jax import lax
from jax.experimental import pallas as pl
from jax.experimental.pallas import tpu as pltpu
from jax.sharding import PartitionSpec as P

STENCIL_TAPS = (-205.0 / 72.0, 8.0 / 5.0, -1.0 / 5.0, 8.0 / 315.0, -1.0 / 560.0)
RADIUS = 4
PAD = 8
STEPS = 2
F32 = jnp.float32
BYTES_PER_US = 3.69e6


def even_pairs(count):
    return [(i, i ^ 1) for i in range(count) if (i ^ 1) < count]


def odd_pairs(count):
    low = [(i, i + 1) for i in range(1, count - 1, 2)]
    return low + [(b, a) for a, b in low]


def run_copies(pairs, sems):
    copies = [pltpu.make_async_copy(src, dst, sems.at[k]) for k, (src, dst) in enumerate(pairs)]
    for copy in copies:
        copy.start()
    return copies


SPECS = {
    "any": pl.BlockSpec(memory_space=pl.ANY),
    "hbm": pl.BlockSpec(memory_space=pltpu.HBM),
    "vmem": pl.BlockSpec(memory_space=pltpu.VMEM),
    "block": pl.BlockSpec(),
}


def call(body, out_shapes, operands, in_specs=None, out_specs=None, scratch=(), aliases=None, us=0.1):
    return pl.pallas_call(
        body,
        out_shape=list(out_shapes),
        in_specs=[SPECS[s] for s in in_specs],
        out_specs=[SPECS[s] for s in out_specs],
        scratch_shapes=list(scratch),
        input_output_aliases=aliases or {},
        cost_estimate=pl.CostEstimate(flops=0, bytes_accessed=int(us * BYTES_PER_US), transcendentals=0),
        compiler_params=pltpu.CompilerParams(vmem_limit_bytes=16 * 1024 * 1024),
    )(*operands)


def shape(*dims):
    return jax.ShapeDtypeStruct(dims, F32)


def y_sums(centre, lane, size_y):
    sums = []
    for r in range(1, RADIUS + 1):
        before = jnp.where(lane >= r, pltpu.roll(centre, r, 1), 0.0)
        after = jnp.where(lane < size_y - r, pltpu.roll(centre, size_y - r, 1), 0.0)
        sums.append(before + after)
    return sums


def laplacian_row(field, z, rows, size_x, size_y, lane):
    centre = field[z, PAD : PAD + size_x, :]
    along_y = y_sums(centre, lane, size_y)
    total = (3.0 * STENCIL_TAPS[0]) * centre
    for r in range(1, RADIUS + 1):
        ring = along_y[r - 1]
        ring = ring + (field[z, PAD + r : PAD + r + size_x, :] + field[z, PAD - r : PAD - r + size_x, :])
        if z + r < rows:
            ring = ring + field[z + r, PAD : PAD + size_x, :]
        if z - r >= 0:
            ring = ring + field[z - r, PAD : PAD + size_x, :]
        total = total + STENCIL_TAPS[r] * ring
    return total


def clear_sides(field, size_x):
    rows, _, size_y = field.shape
    edge = jnp.zeros((rows, PAD, size_y), F32)
    field[:, 0:PAD, :] = edge
    field[:, PAD + size_x : PAD + size_x + PAD, :] = edge


def pack_body(state, velocity, out_a, out_b, sems):
    depth = velocity.shape[0]
    half = RADIUS // 2
    even = lax.rem(lax.axis_index("slab"), 2) == 0
    share = lax.rem(lax.axis_index("shot"), 2) * half
    at_a = jnp.where(even, depth - RADIUS, 0)
    at_b = jnp.where(even, 0, depth - RADIUS)
    pairs = []
    for out, at in ((out_a, at_a), (out_b, at_b)):
        for k in range(RADIUS):
            pairs.append((state.at[1, 0, 0, at + k], out.at[k]))
            pairs.append((state.at[1, 0, 1, at + k], out.at[RADIUS + k]))
        for k in range(half):
            pairs.append((velocity.at[at + share + k], out.at[2 * RADIUS + k]))
    for copy in run_copies(pairs, sems):
        copy.wait()


def point_cells(cells, codes, wavelets, moment, first, size_x, size_y, act):
    plane = size_x * size_y
    row_lane = lax.broadcasted_iota(jnp.int32, (1, size_y), 1)
    for k in range(cells.shape[1]):
        cell = cells[0, k]
        amount = wavelets[moment, codes[0, k]]
        z = lax.div(cell, plane) - first
        rest = lax.rem(cell, plane)
        x = lax.div(rest, size_y)
        y = lax.rem(rest, size_y)
        act(z, x, jnp.where(row_lane == y, amount, 0.0))


def weighted(terms):
    total = None
    for r, value in terms:
        term = STENCIL_TAPS[r] * value
        total = term if total is None else total + term
    return total


def partial_body(
    state, velocity, cells, residuals, kappa,
    partial_u, image, partial_q, push, out_a, out_b, side_a, side_b, field_u, field_q, grid_now,
):
    depth, size_x, size_y = velocity.shape
    strip = kappa.shape[2]
    even = lax.rem(lax.axis_index("slab"), 2) == 0
    even_strip = lax.rem(lax.axis_index("shot"), 2) == 0
    for j in range(3):
        tail = kappa[j, :, strip - 1, :]
        head = kappa[j, :, 0, :]
        side_a[j * depth : (j + 1) * depth, :] = jnp.where(even_strip, tail, head)
        side_b[j * depth : (j + 1) * depth, :] = jnp.where(even_strip, head, tail)
        tail = kappa[j, depth - 1]
        head = kappa[j, 0]
        at = 2 * RADIUS * size_x + j * strip
        out_a[at : at + strip, :] = jnp.where(even, tail, head)
        out_b[at : at + strip, :] = jnp.where(even, head, tail)
    for which, field in ((0, field_u), (1, field_q)):
        clear_sides(field, size_x)
        for z in range(depth):
            field[z, PAD : PAD + size_x, :] = state[1, 0, which, z]

    volume = depth * size_x * size_y
    count = cells.shape[1]
    ids = cells[...] - lax.axis_index("slab") * volume
    inside = (ids >= 0) & (ids < volume)
    kept = jnp.where(inside, ids, 0)
    row = lax.div(kept, jnp.int32(size_y))
    column = kept - row * size_y
    rows = depth * size_x
    pick_row = (lax.broadcasted_iota(jnp.int32, (rows, count), 0) == row).astype(F32)
    pick_column = lax.broadcasted_iota(jnp.int32, (size_y, count), 0) == column
    for moment in range(STEPS):
        amounts = jnp.where(inside, residuals[0, moment : moment + 1, :], 0.0)
        grid_now[moment] = lax.dot_general(
            pick_row,
            jnp.where(pick_column, amounts, 0.0),
            (((1,), (1,)), ((), ())),
            precision=lax.Precision.HIGHEST,
            preferred_element_type=F32,
        )

    lane = lax.broadcasted_iota(jnp.int32, (size_x, size_y), 1)
    for z in range(depth):
        at = slice(z * size_x, (z + 1) * size_x)
        v = velocity[z]
        vv = v * v
        drive = vv * laplacian_row(field_u, z, depth, size_x, size_y, lane)
        partial_u[z] = (2.0 * state[1, 0, 0, z] - state[0, 0, 0, z]) + drive
        image[z] = drive * state[1, 0, 1, z]
        drive = vv * (laplacian_row(field_q, z, depth, size_x, size_y, lane) + grid_now[0, at, :])
        partial_q[z] = (2.0 * state[1, 0, 1, z] - state[0, 0, 1, z]) + drive
        push[z] = vv * grid_now[1, at, :]
    for k in range(2 * RADIUS):
        source = partial_u if k < RADIUS else partial_q
        tail = source[depth - RADIUS + k % RADIUS]
        head = source[k % RADIUS]
        out_a[k * size_x : (k + 1) * size_x, :] = jnp.where(even, tail, head)
        out_b[k * size_x : (k + 1) * size_x, :] = jnp.where(even, head, tail)


def share_body(first_a, first_b, share):
    half = RADIUS // 2
    for k in range(half):
        share[k] = first_a[2 * RADIUS + k]
        share[half + k] = first_b[2 * RADIUS + k]


def halo_speed(k, share_own, share_got):
    half = RADIUS // 2
    row = k % RADIUS
    even = lax.rem(lax.axis_index("slab"), 2) == 0
    own = lax.rem(lax.axis_index("shot"), 2) == row // half
    at_a = jnp.where(own, share_own[row % half], share_got[row % half])
    at_b = jnp.where(own, share_own[half + row % half], share_got[half + row % half])
    return jnp.where(even, at_b, at_a) if k < RADIUS else jnp.where(even, at_a, at_b)


def halo_near(k, depth):
    if k < RADIUS:
        return [(r, k - RADIUS + r) for r in range(1, RADIUS + 1) if k - RADIUS + r >= 0]
    row = k - RADIUS
    return [(r, depth + row - r) for r in range(1, RADIUS + 1) if depth + row - r < depth]


def border_body(
    state, velocity, partial_u, image0, partial_q, first_a, first_b, u_own, image, q_next, u_edge, q_edge
):
    depth = velocity.shape[0]
    even = lax.rem(lax.axis_index("slab"), 2) == 0
    for k in range(2 * RADIUS):
        row = k % RADIUS
        one, other = (first_b, first_a) if k < RADIUS else (first_a, first_b)
        u_edge[k] = jnp.where(even, one[row], other[row])
        q_edge[k] = jnp.where(even, one[RADIUS + row], other[RADIUS + row])
    for z in range(depth):
        near = [(r, RADIUS + z - r) for r in range(1, RADIUS + 1) if z - r < 0]
        near += [(r, RADIUS + z + r - depth) for r in range(1, RADIUS + 1) if z + r >= depth]
        if not near:
            u_own[z] = partial_u[z]
            q_next[z] = partial_q[z]
            image[z] = image0[z]
            continue
        v = velocity[z]
        vv = v * v
        change = vv * weighted([(r, u_edge[k]) for r, k in near])
        u_own[z] = partial_u[z] + change
        image[z] = image0[z] + change * state[1, 0, 1, z]
        q_next[z] = partial_q[z] + vv * weighted([(r, q_edge[k]) for r, k in near])

def image_body(
    state, velocity, u_own, image0, q_next, share_own, share_got, second_a, second_b, cells, codes, wavelets,
    fields, keep, send, speed, u_now, image, u_out, cells_here, codes_here, wavelets_here, sems, out_sem, *, scale,
):
    small = run_copies([(cells, cells_here), (codes, codes_here), (wavelets, wavelets_here)], sems)
    depth, size_x, size_y = velocity.shape
    whole = depth + 2 * RADIUS
    half = RADIUS // 2
    here = lax.axis_index("slab")
    even = lax.rem(here, 2) == 0
    core = lax.rem(lax.axis_index("shot"), 2)
    middle = slice(PAD, PAD + size_x)
    clear_sides(u_now, size_x)
    clear_sides(image, size_x)
    lane = lax.broadcasted_iota(jnp.int32, (size_x, size_y), 1)
    for z in range(depth):
        u_now[RADIUS + z, middle, :] = u_own[z]
    for k in range(2 * RADIUS):
        row = k % RADIUS
        one, other = (second_b, second_a) if k < RADIUS else (second_a, second_b)
        rows = slice(row * size_x, (row + 1) * size_x)
        before = jnp.where(even, one[rows, :], other[rows, :])
        v = halo_speed(k, share_own, share_got)
        speed[k] = v
        near = halo_near(k, depth)
        z = k if k < RADIUS else k + depth
        u_now[z, middle, :] = before + (v * v) * weighted([(r, state[1, 0, 0, own]) for r, own in near])

    def first_step(z, x, spot):
        at = (z, pl.ds(PAD + x, 1), slice(None))

        @pl.when((z >= 0) & (z < whole) & ((z < RADIUS) | (z >= RADIUS + depth)))
        def _():
            v = speed[jnp.where(z < RADIUS, z, z - depth), pl.ds(x, 1), :]
            u_now[at] = u_now[at] + (v * v) * spot

        @pl.when((z >= RADIUS) & (z < RADIUS + depth))
        def _():
            v = velocity[z - RADIUS, pl.ds(x, 1), :]
            u_now[at] = u_now[at] + (v * v) * spot

    for copy in small:
        copy.wait()
    sources = (cells_here, codes_here, wavelets_here)
    point_cells(*sources, 0, here * depth - RADIUS, size_x, size_y, first_step)

    for z in range(depth):
        v = velocity[z]
        drive = (v * v) * laplacian_row(u_now, z + RADIUS, whole, size_x, size_y, lane)
        u_out[z] = (2.0 * u_now[RADIUS + z, middle, :] - state[1, 0, 0, z]) + drive
        image[z, middle, :] = (-0.2 * (image0[z] + drive * q_next[z])) / (v * scale)

    def image_spot(z, x, change, adjoint):
        v = velocity[z, pl.ds(x, 1), :]
        to = (z, pl.ds(PAD + x, 1), slice(None))
        image[to] = image[to] + (-0.2 * ((v * v) * change * adjoint)) / (v * scale)

    def first_image(z, x, spot):
        @pl.when((z >= 0) & (z < depth))
        def _():
            image_spot(z, x, spot, state[1, 0, 1, z, pl.ds(x, 1), :])

    def second_step(z, x, spot):
        @pl.when((z >= 0) & (z < depth))
        def _():
            at = (z, pl.ds(x, 1), slice(None))
            v = velocity[at]
            u_out[at] = u_out[at] + (v * v) * spot
            image_spot(z, x, spot, q_next[at])

    point_cells(*sources, 0, here * depth, size_x, size_y, first_image)
    point_cells(*sources, 1, here * depth, size_x, size_y, second_step)
    copy_out = pltpu.make_async_copy(u_out, fields.at[0, 0], out_sem)
    copy_out.start()
    chip = lax.div(lax.axis_index("shot"), 2)
    chips = keep.shape[0]
    strip = size_x // (2 * chips)
    wide = strip + 4
    for m in range(chips):
        to = jnp.bitwise_xor(chip, m)
        for z in range(depth):
            at = PAD + 2 * m * strip - 2
            low = image[z, at : at + wide, :]
            high = image[z, at + strip : at + strip + wide, :]
            keep[to, z * wide : (z + 1) * wide, :] = jnp.where(core == 0, low, high)
            send[to, z * wide : (z + 1) * wide, :] = jnp.where(core == 0, high, low)
    copy_out.wait()


def pair_sum_body(keep, got, *outs):
    for k, out in enumerate(outs):
        out[...] = keep[k] + got[k]


def strip_sum_body(*refs, count, wide):
    parts, (total, edge_a, edge_b) = refs[:count], refs[count:]
    added = parts[0][...]
    for part in parts[1:]:
        added = added + part[...]
    total[...] = added
    even = lax.rem(lax.axis_index("slab"), 2) == 0
    rows = total.shape[0]
    head = total[0 : 2 * wide, :]
    tail = total[rows - 2 * wide : rows, :]
    edge_a[...] = jnp.where(even, tail, head)
    edge_b[...] = jnp.where(even, head, tail)


def adjoint_body(
    fields_in, state, velocity, q_next, push, second_a, second_b, share_own, share_got, fields, field, q_out, out_sem
):
    depth, size_x, size_y = velocity.shape
    whole = depth + 2 * RADIUS
    even = lax.rem(lax.axis_index("slab"), 2) == 0
    middle = slice(PAD, PAD + size_x)
    clear_sides(field, size_x)
    for z in range(depth):
        field[RADIUS + z, middle, :] = q_next[z]
    for k in range(2 * RADIUS):
        row = k % RADIUS
        one, other = (second_b, second_a) if k < RADIUS else (second_a, second_b)
        rows = slice((RADIUS + row) * size_x, (RADIUS + row + 1) * size_x)
        before = jnp.where(even, one[rows, :], other[rows, :])
        v = halo_speed(k, share_own, share_got)
        z = k if k < RADIUS else k + depth
        near = halo_near(k, depth)
        field[z, middle, :] = before + (v * v) * weighted([(r, state[1, 0, 1, own]) for r, own in near])
    lane = lax.broadcasted_iota(jnp.int32, (size_x, size_y), 1)
    for z in range(depth):
        v = velocity[z]
        drive = (v * v) * laplacian_row(field, z + RADIUS, whole, size_x, size_y, lane) + push[z]
        q_out[z] = (2.0 * q_next[z] - state[1, 0, 1, z]) + drive
    copy = pltpu.make_async_copy(q_out, fields.at[0, 1], out_sem)
    copy.start()
    copy.wait()


def smooth_body(
    total, got_a, got_b, kappa, second_a, second_b, side_a, side_b, velocity, momentum, new_momentum, new_speed, grad, half, coef,
    *, size_x
):
    depth, strip, size_y = momentum.shape
    column = lax.axis_index("shot") * strip
    wide = strip + 4
    even = lax.rem(lax.axis_index("slab"), 2) == 0
    even_strip = lax.rem(lax.axis_index("shot"), 2) == 0
    for k in range(2):
        at = slice(k * wide, (k + 1) * wide)
        grad[k, 0:wide, :] = jnp.where(even, got_b[at, :], got_a[at, :])
        grad[depth + 2 + k, 0:wide, :] = jnp.where(even, got_a[at, :], got_b[at, :])
    for z in range(depth):
        grad[z + 2, 0:wide, :] = total[z * wide : (z + 1) * wide, :]
    coef[...] = jnp.zeros(coef.shape, F32)
    for j in range(3):
        at = slice(2 * RADIUS * size_x + j * strip, 2 * RADIUS * size_x + (j + 1) * strip)
        coef[j, 0, 1 : strip + 1, :] = jnp.where(even, second_b[at, :], second_a[at, :])
        coef[j, depth + 1, 1 : strip + 1, :] = jnp.where(even, second_a[at, :], second_b[at, :])
        left = jnp.where(even_strip, side_b[j * depth : (j + 1) * depth, :], side_a[j * depth : (j + 1) * depth, :])
        right = jnp.where(even_strip, side_a[j * depth : (j + 1) * depth, :], side_b[j * depth : (j + 1) * depth, :])
        for z in range(depth):
            coef[j, z + 1, 1 : strip + 1, :] = kappa[j, z]
            coef[j, z + 1, 0:1, :] = left[z : z + 1, :]
            coef[j, z + 1, strip + 1 : strip + 2, :] = right[z : z + 1, :]

    def step(source, z, rows, factors):
        centre = source[z, 1 : 1 + rows, :]
        lane = lax.broadcasted_iota(jnp.int32, centre.shape, 1)
        twice = 2.0 * centre
        along_z = source[z + 1, 1 : 1 + rows, :] - twice + source[z - 1, 1 : 1 + rows, :]
        along_x = source[z, 2 : 2 + rows, :] - twice + source[z, 0:rows, :]
        after = jnp.where(lane < size_y - 1, pltpu.roll(centre, size_y - 1, 1), 0.0)
        before = jnp.where(lane >= 1, pltpu.roll(centre, 1, 1), 0.0)
        along_y = after - twice + before
        return centre + factors[0] * along_z + factors[1] * along_x + factors[2] * along_y

    for z in range(depth + 2):
        half[z, 0 : strip + 2, :] = step(grad, z + 1, strip + 2, [coef[j, z, 0 : strip + 2, :] for j in range(3)])
    for z in range(depth):
        smoothed = step(half, z + 1, strip, [kappa[j, z] for j in range(3)])
        fresh = 0.9 * momentum[z] + smoothed
        new_momentum[z] = fresh
        new_speed[z] = velocity[z, pl.ds(column, strip), :] - 0.02 * fresh


def on_device(
    velocity,
    wave_state,
    source_cells,
    source_codes,
    wavelets,
    receiver_cells,
    residuals,
    momentum,
    diffusivity,
):
    depth, size_x, size_y = velocity.shape
    strip = momentum.shape[1]
    wide = strip + 4
    slabs = lax.axis_size("slab")
    shots = lax.axis_size("shot")
    chips = shots // 2
    z_even, z_odd = even_pairs(slabs), odd_pairs(slabs)
    cube = (depth, size_x, size_y)
    padded = (depth, size_x + 2 * PAD, size_y)
    whole = depth + 2 * RADIUS
    dma = pltpu.SemaphoreType.DMA

    half = RADIUS // 2
    block = shape(2 * RADIUS + half, size_x, size_y)
    out_a, out_b = call(
        pack_body, [block] * 2, tuple(pltpu.with_memory_space_constraint(x, pltpu.HBM) for x in (wave_state, velocity)), ["hbm"] * 2, ["vmem"] * 2, [dma((2 * (2 * RADIUS + half),))], us=1.3
    )
    first_a = lax.ppermute(out_a, "slab", z_even)
    first_b = lax.ppermute(out_b, "slab", z_odd)

    flat = shape(2 * RADIUS * size_x + 3 * strip, size_y)
    side = shape(3 * depth, size_y)
    edge = shape(RADIUS, size_x, size_y)
    partial_u, image0, partial_q, push, out_a, out_b, side_a, side_b = call(
        partial_body,
        [shape(*cube)] * 4 + [flat, flat, side, side],
        (wave_state, velocity, receiver_cells, residuals, diffusivity),
        ["vmem"] * 5,
        ["vmem"] * 8,
        [pltpu.VMEM(padded, F32)] * 2 + [pltpu.VMEM((STEPS, depth * size_x, size_y), F32)],
        us=1.7,
    )
    second_a = lax.ppermute(out_a, "slab", z_even)
    second_b = lax.ppermute(out_b, "slab", z_odd)
    side_a = lax.ppermute(side_a, "shot", even_pairs(shots))
    side_b = lax.ppermute(side_b, "shot", odd_pairs(shots))

    first_a, first_b, side_a, side_b = lax.optimization_barrier((first_a, first_b, side_a, side_b))
    (share_own,) = call(share_body, [edge], (first_a, first_b), ["vmem"] * 2, ["vmem"])
    share_got = lax.ppermute(share_own, "shot", even_pairs(shots))
    u_own, image0, q_next = call(
        border_body,
        [shape(*cube)] * 3,
        (wave_state, velocity, partial_u, image0, partial_q, first_a, first_b),
        ["vmem"] * 7,
        ["vmem"] * 3,
        [pltpu.VMEM((2 * RADIUS, size_x, size_y), F32)] * 2,
        us=0.3,
    )

    small = (source_cells, source_codes, wavelets.T)
    part = shape(chips, depth * wide, size_y)
    fields, keep, send = call(
        functools.partial(image_body, scale=math.sqrt(shots * STEPS)),
        [shape(1, 2, *cube), part, part],
        (wave_state, velocity, u_own, image0, q_next, share_own, share_got, second_a, second_b)
        + tuple(pltpu.with_memory_space_constraint(x, pltpu.HBM) for x in small),
        ["vmem"] * 9 + ["hbm"] * 3,
        ["any"] + ["vmem"] * 2,
        [
            pltpu.VMEM((2 * RADIUS, size_x, size_y), F32),
            pltpu.VMEM((whole, size_x + 2 * PAD, size_y), F32),
            pltpu.VMEM(padded, F32),
            pltpu.VMEM(cube, F32),
        ]
        + [pltpu.SMEM(x.shape, x.dtype) for x in small]
        + [dma((3,)), dma],
        us=2.3,
    )
    got = lax.ppermute(send, "shot", even_pairs(shots))
    (fields,) = call(
        adjoint_body,
        [shape(1, 2, *cube)],
        (fields, wave_state, velocity, q_next, push, second_a, second_b, share_own, share_got),
        ["any"] + ["vmem"] * 8,
        ["any"],
        [pltpu.VMEM((whole, size_x + 2 * PAD, size_y), F32), pltpu.VMEM(cube, F32), dma],
        aliases={0: 0},
        us=1.4,
    )
    got, fields = lax.optimization_barrier((got, fields))
    row_block = shape(depth * wide, size_y)
    parts = call(pair_sum_body, [row_block] * chips, (keep, got), ["vmem"] * 2, ["vmem"] * chips)
    arrived = [
        parts[0] if k == 0 else lax.ppermute(parts[k], "shot", [(i, i ^ (2 * k)) for i in range(shots)])
        for k in range(chips)
    ]
    two = shape(2 * wide, size_y)
    total, out_a, out_b = call(
        functools.partial(strip_sum_body, count=chips, wide=wide),
        [row_block, two, two],
        arrived,
        ["vmem"] * chips,
        ["vmem"] * 3,
    )
    grad_a = lax.ppermute(out_a, "slab", z_even)
    grad_b = lax.ppermute(out_b, "slab", z_odd)
    tall = 8 * ((wide + 7) // 8)
    new_momentum, new_velocity = call(
        functools.partial(smooth_body, size_x=size_x),
        [shape(*momentum.shape)] * 2,
        (total, grad_a, grad_b, diffusivity, second_a, second_b, side_a, side_b, velocity, momentum),
        ["vmem"] * 10,
        ["block"] * 2,
        [
            pltpu.VMEM((depth + 4, tall, size_y), F32),
            pltpu.VMEM((depth + 2, tall, size_y), F32),
            pltpu.VMEM((3, depth + 2, tall, size_y), F32),
        ],
        us=0.9,
    )
    return (fields, new_momentum, new_velocity)


def solution(mesh):
    return jax.shard_map(
        on_device,
        mesh=mesh,
        in_specs=(
            P("slab", None, None),
            P(None, "shot", None, "slab", None, None),
            P("shot", None),
            P("shot", None),
            P(),
            P("shot", None),
            P("shot", None, None),
            P("slab", "shot", None),
            P(None, "slab", "shot", None),
        ),
        out_specs=(
            P("shot", None, "slab", None, None),
            P("slab", "shot", None),
            P("slab", "shot", None),
        ),
        check_vma=False,
    )
```

```python
import functools
import math

import jax
import jax.numpy as jnp
from jax import lax
from jax.experimental import pallas as pl
from jax.experimental.pallas import tpu as pltpu
from jax.sharding import PartitionSpec as P

STENCIL_TAPS = (-205.0 / 72.0, 8.0 / 5.0, -1.0 / 5.0, 8.0 / 315.0, -1.0 / 560.0)
RADIUS = 4
PAD = 8
STEPS = 2
F32 = jnp.float32
BYTES_PER_US = 3.69e6


def even_pairs(count):
    return [(i, i ^ 1) for i in range(count)]


def odd_pairs(count):
    low = [(i, (i + 1) % count) for i in range(1, count, 2)]
    return low + [(b, a) for a, b in low]


def odd_slabs(shots, slabs):
    pairs = []
    for shot in range(shots):
        for slab in range(slabs):
            if slab == 0 or slab == slabs - 1:
                other = (shot ^ 1) * slabs + slab
            else:
                other = shot * slabs + (slab + 1 if slab % 2 else slab - 1)
            pairs.append((shot * slabs + slab, other))
    return pairs


def at_border():
    slab = lax.axis_index("slab")
    return (slab == 0) | (slab == lax.axis_size("slab") - 1)


def ahead(even, border, from_a, from_b):
    return jnp.where(even, jnp.where(border, 0.0, from_b), from_a)


def after(even, border, from_a, from_b):
    return jnp.where(even, from_a, jnp.where(border, 0.0, from_b))


def run_copies(pairs, sems):
    copies = [pltpu.make_async_copy(src, dst, sems.at[k]) for k, (src, dst) in enumerate(pairs)]
    for copy in copies:
        copy.start()
    return copies


SPECS = {
    "any": pl.BlockSpec(memory_space=pl.ANY),
    "hbm": pl.BlockSpec(memory_space=pltpu.HBM),
    "vmem": pl.BlockSpec(memory_space=pltpu.VMEM),
    "block": pl.BlockSpec(),
}


def call(body, out_shapes, operands, in_specs=None, out_specs=None, scratch=(), aliases=None, us=0.1):
    return pl.pallas_call(
        body,
        out_shape=list(out_shapes),
        in_specs=[SPECS[s] for s in in_specs],
        out_specs=[SPECS[s] for s in out_specs],
        scratch_shapes=list(scratch),
        input_output_aliases=aliases or {},
        cost_estimate=pl.CostEstimate(flops=0, bytes_accessed=int(us * BYTES_PER_US), transcendentals=0),
        compiler_params=pltpu.CompilerParams(vmem_limit_bytes=16 * 1024 * 1024),
    )(*operands)


def shape(*dims):
    return jax.ShapeDtypeStruct(dims, F32)


def y_sums(centre, lane, size_y):
    sums = []
    for r in range(1, RADIUS + 1):
        before = jnp.where(lane >= r, pltpu.roll(centre, r, 1), 0.0)
        after = jnp.where(lane < size_y - r, pltpu.roll(centre, size_y - r, 1), 0.0)
        sums.append(before + after)
    return sums


def laplacian_row(field, z, rows, size_x, size_y, lane):
    centre = field[z, PAD : PAD + size_x, :]
    along_y = y_sums(centre, lane, size_y)
    total = (3.0 * STENCIL_TAPS[0]) * centre
    for r in range(1, RADIUS + 1):
        ring = along_y[r - 1]
        ring = ring + (field[z, PAD + r : PAD + r + size_x, :] + field[z, PAD - r : PAD - r + size_x, :])
        if z + r < rows:
            ring = ring + field[z + r, PAD : PAD + size_x, :]
        if z - r >= 0:
            ring = ring + field[z - r, PAD : PAD + size_x, :]
        total = total + STENCIL_TAPS[r] * ring
    return total


def clear_sides(field, size_x):
    rows, _, size_y = field.shape
    edge = jnp.zeros((rows, PAD, size_y), F32)
    field[:, 0:PAD, :] = edge
    field[:, PAD + size_x : PAD + size_x + PAD, :] = edge


def pack_body(state, velocity, out_b, out_a, sems):
    depth = velocity.shape[0]
    half = RADIUS // 2
    even = lax.rem(lax.axis_index("slab"), 2) == 0
    share = lax.rem(lax.axis_index("shot"), 2) * half
    at_a = jnp.where(even, depth - RADIUS, 0)
    at_b = jnp.where(even, 0, depth - RADIUS)
    pairs = []
    for out, at in ((out_a, at_a), (out_b, at_b)):
        for k in range(RADIUS):
            pairs.append((state.at[1, 0, 0, at + k], out.at[k]))
            pairs.append((state.at[1, 0, 1, at + k], out.at[RADIUS + k]))
        for k in range(half):
            pairs.append((velocity.at[at + share + k], out.at[2 * RADIUS + k]))
    for copy in run_copies(pairs, sems):
        copy.wait()


def point_cells(cells, codes, wavelets, moment, first, size_x, size_y, act):
    plane = size_x * size_y
    row_lane = lax.broadcasted_iota(jnp.int32, (1, size_y), 1)
    for k in range(cells.shape[1]):
        cell = cells[0, k]
        amount = wavelets[moment, codes[0, k]]
        z = lax.div(cell, plane) - first
        rest = lax.rem(cell, plane)
        x = lax.div(rest, size_y)
        y = lax.rem(rest, size_y)
        act(z, x, jnp.where(row_lane == y, amount, 0.0))


def weighted(terms):
    total = None
    for r, value in terms:
        term = STENCIL_TAPS[r] * value
        total = term if total is None else total + term
    return total


def partial_body(
    state, velocity, cells, residuals, kappa,
    partial_u, image, partial_q, push, out_b, out_a, side_a, side_b, field_u, field_q, grid_now,
):
    depth, size_x, size_y = velocity.shape
    strip = kappa.shape[2]
    even = lax.rem(lax.axis_index("slab"), 2) == 0
    even_strip = lax.rem(lax.axis_index("shot"), 2) == 0
    for j in range(3):
        tail = kappa[j, :, strip - 1, :]
        head = kappa[j, :, 0, :]
        side_a[j * depth : (j + 1) * depth, :] = jnp.where(even_strip, tail, head)
        side_b[j * depth : (j + 1) * depth, :] = jnp.where(even_strip, head, tail)
        tail = kappa[j, depth - 1]
        head = kappa[j, 0]
        at = 2 * RADIUS * size_x + j * strip
        out_a[at : at + strip, :] = jnp.where(even, tail, head)
        out_b[at : at + strip, :] = jnp.where(even, head, tail)
    for which, field in ((0, field_u), (1, field_q)):
        clear_sides(field, size_x)
        for z in range(depth):
            field[z, PAD : PAD + size_x, :] = state[1, 0, which, z]

    volume = depth * size_x * size_y
    count = cells.shape[1]
    ids = cells[...] - lax.axis_index("slab") * volume
    inside = (ids >= 0) & (ids < volume)
    kept = jnp.where(inside, ids, 0)
    row = lax.div(kept, jnp.int32(size_y))
    column = kept - row * size_y
    rows = depth * size_x
    pick_row = (lax.broadcasted_iota(jnp.int32, (rows, count), 0) == row).astype(F32)
    pick_column = lax.broadcasted_iota(jnp.int32, (size_y, count), 0) == column
    for moment in range(STEPS):
        amounts = jnp.where(inside, residuals[0, moment : moment + 1, :], 0.0)
        grid_now[moment] = lax.dot_general(
            pick_row,
            jnp.where(pick_column, amounts, 0.0),
            (((1,), (1,)), ((), ())),
            precision=lax.Precision.HIGHEST,
            preferred_element_type=F32,
        )

    lane = lax.broadcasted_iota(jnp.int32, (size_x, size_y), 1)
    for z in range(depth):
        at = slice(z * size_x, (z + 1) * size_x)
        v = velocity[z]
        vv = v * v
        drive = vv * laplacian_row(field_u, z, depth, size_x, size_y, lane)
        partial_u[z] = (2.0 * state[1, 0, 0, z] - state[0, 0, 0, z]) + drive
        image[z] = drive * state[1, 0, 1, z]
        drive = vv * (laplacian_row(field_q, z, depth, size_x, size_y, lane) + grid_now[0, at, :])
        partial_q[z] = (2.0 * state[1, 0, 1, z] - state[0, 0, 1, z]) + drive
        push[z] = vv * grid_now[1, at, :]
    for k in range(2 * RADIUS):
        source = partial_u if k < RADIUS else partial_q
        tail = source[depth - RADIUS + k % RADIUS]
        head = source[k % RADIUS]
        out_a[k * size_x : (k + 1) * size_x, :] = jnp.where(even, tail, head)
        out_b[k * size_x : (k + 1) * size_x, :] = jnp.where(even, head, tail)


def share_body(first_a, first_b, share):
    half = RADIUS // 2
    for k in range(half):
        share[k] = first_a[2 * RADIUS + k]
        share[half + k] = first_b[2 * RADIUS + k]


def halo_speed(k, share_own, share_got):
    half = RADIUS // 2
    row = k % RADIUS
    even = lax.rem(lax.axis_index("slab"), 2) == 0
    border = at_border()
    own = lax.rem(lax.axis_index("shot"), 2) == row // half
    at_a = jnp.where(own, share_own[row % half], share_got[row % half])
    at_b = jnp.where(own, share_own[half + row % half], share_got[half + row % half])
    return (ahead if k < RADIUS else after)(even, border, at_a, at_b)


def halo_near(k, depth):
    if k < RADIUS:
        return [(r, k - RADIUS + r) for r in range(1, RADIUS + 1) if k - RADIUS + r >= 0]
    row = k - RADIUS
    return [(r, depth + row - r) for r in range(1, RADIUS + 1) if depth + row - r < depth]


def own_near(z, depth):
    near = [(r, RADIUS + z - r) for r in range(1, RADIUS + 1) if z - r < 0]
    return near + [(r, RADIUS + z + r - depth) for r in range(1, RADIUS + 1) if z + r >= depth]


def near_body(
    state, velocity, partial_u, image0, partial_q, push, first_b, first_a, cells, codes, wavelets,
    u_part, q_part, image, gain, tap_u, tap_q,
    u_edge, q_edge, u_now, q_now, cells_here, codes_here, wavelets_here, sems, *, scale,
):
    small = run_copies([(cells, cells_here), (codes, codes_here), (wavelets, wavelets_here)], sems)
    depth, size_x, size_y = velocity.shape
    here = lax.axis_index("slab")
    even = lax.rem(here, 2) == 0
    border = at_border()
    middle = slice(PAD, PAD + size_x)
    clear_sides(u_now, size_x)
    clear_sides(q_now, size_x)
    for k in range(2 * RADIUS):
        row = k % RADIUS
        pick = ahead if k < RADIUS else after
        u_edge[k] = pick(even, border, first_a[row], first_b[row])
        q_edge[k] = pick(even, border, first_a[RADIUS + row], first_b[RADIUS + row])
        near = halo_near(k, depth)
        tap_u[k] = weighted([(r, state[1, 0, 0, own]) for r, own in near])
        tap_q[k] = weighted([(r, state[1, 0, 1, own]) for r, own in near])
    for z in range(depth):
        near = own_near(z, depth)
        if not near:
            u_now[z, middle, :] = partial_u[z]
            q_now[z, middle, :] = partial_q[z]
            image[z] = image0[z]
            continue
        v = velocity[z]
        vv = v * v
        change = vv * weighted([(r, u_edge[k]) for r, k in near])
        u_now[z, middle, :] = partial_u[z] + change
        image[z] = image0[z] + change * state[1, 0, 1, z]
        q_now[z, middle, :] = partial_q[z] + vv * weighted([(r, q_edge[k]) for r, k in near])

    def first_step(z, x, spot):
        @pl.when((z >= 0) & (z < depth))
        def _():
            v = velocity[z, pl.ds(x, 1), :]
            change = (v * v) * spot
            at = (z, pl.ds(PAD + x, 1), slice(None))
            u_now[at] = u_now[at] + change
            at = (z, pl.ds(x, 1), slice(None))
            image[at] = image[at] + change * state[1, 0, 1, z, pl.ds(x, 1), :]

        before = (z >= -RADIUS) & (z < 0)

        @pl.when(before | ((z >= depth) & (z < depth + RADIUS)))
        def _():
            at = (jnp.where(before, z + RADIUS, z + RADIUS - depth), pl.ds(x, 1), slice(None))
            tap_u[at] = tap_u[at] + spot

    def second_step(z, x, spot):
        @pl.when((z >= 0) & (z < depth))
        def _():
            at = (z, pl.ds(x, 1), slice(None))
            v = velocity[at]
            change = (v * v) * spot
            u_part[at] = u_part[at] + change
            image[at] = image[at] + (-0.2 * (change * q_now[z, pl.ds(PAD + x, 1), :])) / (v * scale)

    for copy in small:
        copy.wait()
    sources = (cells_here, codes_here, wavelets_here)
    point_cells(*sources, 0, here * depth, size_x, size_y, first_step)
    lane = lax.broadcasted_iota(jnp.int32, (size_x, size_y), 1)
    for z in range(depth):
        v = velocity[z]
        vv = v * v
        adjoint = q_now[z, middle, :]
        drive = vv * laplacian_row(u_now, z, depth, size_x, size_y, lane)
        u_part[z] = (2.0 * u_now[z, middle, :] - state[1, 0, 0, z]) + drive
        image[z] = (-0.2 * (image[z] + drive * adjoint)) / (v * scale)
        gain[z] = (-0.2 / scale) * (v * adjoint)
        drive = vv * laplacian_row(q_now, z, depth, size_x, size_y, lane) + push[z]
        q_part[z] = (2.0 * adjoint - state[1, 0, 1, z]) + drive
    point_cells(*sources, 1, here * depth, size_x, size_y, second_step)


def halo_field(halo, second_b, second_a, tap, share_own, share_got, which):
    size_x = halo.shape[1]
    even = lax.rem(lax.axis_index("slab"), 2) == 0
    border = at_border()
    for k in range(2 * RADIUS):
        row = which * RADIUS + k % RADIUS
        rows = slice(row * size_x, (row + 1) * size_x)
        pick = ahead if k < RADIUS else after
        v = halo_speed(k, share_own, share_got)
        halo[k] = pick(even, border, second_a[rows, :], second_b[rows, :]) + (v * v) * tap[k]


def image_body(
    velocity, u_part, image_own, gain, tap_u, share_own, share_got, second_b, second_a,
    fields, keep, send, halo, image, u_out, out_sem,
):
    depth, size_x, size_y = velocity.shape
    core = lax.rem(lax.axis_index("shot"), 2)
    middle = slice(PAD, PAD + size_x)
    clear_sides(image, size_x)
    halo_field(halo, second_b, second_a, tap_u, share_own, share_got, 0)
    for z in range(depth):
        near = own_near(z, depth)
        if not near:
            u_out[z] = u_part[z]
            image[z, middle, :] = image_own[z]
            continue
        v = velocity[z]
        crossing = weighted([(r, halo[k]) for r, k in near])
        u_out[z] = u_part[z] + (v * v) * crossing
        image[z, middle, :] = image_own[z] + gain[z] * crossing
    copy_out = pltpu.make_async_copy(u_out, fields.at[0, 0], out_sem)
    copy_out.start()
    chip = lax.div(lax.axis_index("shot"), 2)
    chips = keep.shape[0]
    strip = size_x // (2 * chips)
    wide = strip + 4
    for m in range(chips):
        to = jnp.bitwise_xor(chip, m)
        for z in range(depth):
            at = PAD + 2 * m * strip - 2
            low = image[z, at : at + wide, :]
            high = image[z, at + strip : at + strip + wide, :]
            keep[to, z * wide : (z + 1) * wide, :] = jnp.where(core == 0, low, high)
            send[to, z * wide : (z + 1) * wide, :] = jnp.where(core == 0, high, low)
    copy_out.wait()


def pair_sum_body(keep, got, *outs):
    for k, out in enumerate(outs):
        out[...] = keep[k] + got[k]


def strip_sum_body(*refs, count, wide):
    parts, (total, edge_b, edge_a) = refs[:count], refs[count:]
    added = parts[0][...]
    for part in parts[1:]:
        added = added + part[...]
    total[...] = added
    even = lax.rem(lax.axis_index("slab"), 2) == 0
    rows = total.shape[0]
    head = total[0 : 2 * wide, :]
    tail = total[rows - 2 * wide : rows, :]
    edge_a[...] = jnp.where(even, tail, head)
    edge_b[...] = jnp.where(even, head, tail)


def adjoint_body(
    fields_in, velocity, q_part, tap_q, share_own, share_got, second_b, second_a, fields, halo, q_out, out_sem
):
    depth = velocity.shape[0]
    halo_field(halo, second_b, second_a, tap_q, share_own, share_got, 1)
    for z in range(depth):
        near = own_near(z, depth)
        v = velocity[z]
        q_out[z] = q_part[z] + (v * v) * weighted([(r, halo[k]) for r, k in near]) if near else q_part[z]
    copy = pltpu.make_async_copy(q_out, fields.at[0, 1], out_sem)
    copy.start()
    copy.wait()


def coefficient_body(kappa, second_b, second_a, side_a, side_b, coef, *, size_x):
    _, depth, strip, _ = kappa.shape
    even = lax.rem(lax.axis_index("slab"), 2) == 0
    border = at_border()
    shot = lax.axis_index("shot")
    even_strip = lax.rem(shot, 2) == 0
    end_strip = (shot == 0) | (shot == lax.axis_size("shot") - 1)
    coef[...] = jnp.zeros(coef.shape, F32)
    for j in range(3):
        at = slice(2 * RADIUS * size_x + j * strip, 2 * RADIUS * size_x + (j + 1) * strip)
        coef[j, 0, 1 : strip + 1, :] = ahead(even, border, second_a[at, :], second_b[at, :])
        coef[j, depth + 1, 1 : strip + 1, :] = after(even, border, second_a[at, :], second_b[at, :])
        of = slice(j * depth, (j + 1) * depth)
        left = ahead(even_strip, end_strip, side_a[of, :], side_b[of, :])
        right = after(even_strip, end_strip, side_a[of, :], side_b[of, :])
        for z in range(depth):
            coef[j, z + 1, 1 : strip + 1, :] = kappa[j, z]
            coef[j, z + 1, 0:1, :] = left[z : z + 1, :]
            coef[j, z + 1, strip + 1 : strip + 2, :] = right[z : z + 1, :]


def smooth_body(total, got_a, got_b, kappa, coef, velocity, momentum, new_momentum, new_speed, grad, half):
    depth, strip, size_y = momentum.shape
    column = lax.axis_index("shot") * strip
    wide = strip + 4
    even = lax.rem(lax.axis_index("slab"), 2) == 0
    border = at_border()
    for k in range(2):
        at = slice(k * wide, (k + 1) * wide)
        grad[k, 0:wide, :] = ahead(even, border, got_a[at, :], got_b[at, :])
        grad[depth + 2 + k, 0:wide, :] = after(even, border, got_a[at, :], got_b[at, :])
    for z in range(depth):
        grad[z + 2, 0:wide, :] = total[z * wide : (z + 1) * wide, :]

    def step(source, z, rows, factors):
        centre = source[z, 1 : 1 + rows, :]
        lane = lax.broadcasted_iota(jnp.int32, centre.shape, 1)
        twice = 2.0 * centre
        along_z = source[z + 1, 1 : 1 + rows, :] - twice + source[z - 1, 1 : 1 + rows, :]
        along_x = source[z, 2 : 2 + rows, :] - twice + source[z, 0:rows, :]
        after = jnp.where(lane < size_y - 1, pltpu.roll(centre, size_y - 1, 1), 0.0)
        before = jnp.where(lane >= 1, pltpu.roll(centre, 1, 1), 0.0)
        along_y = after - twice + before
        return centre + factors[0] * along_z + factors[1] * along_x + factors[2] * along_y

    for z in range(depth + 2):
        half[z, 0 : strip + 2, :] = step(grad, z + 1, strip + 2, [coef[j, z, 0 : strip + 2, :] for j in range(3)])
    for z in range(depth):
        smoothed = step(half, z + 1, strip, [kappa[j, z] for j in range(3)])
        fresh = 0.9 * momentum[z] + smoothed
        new_momentum[z] = fresh
        new_speed[z] = velocity[z, pl.ds(column, strip), :] - 0.02 * fresh


def on_device(
    velocity,
    wave_state,
    source_cells,
    source_codes,
    wavelets,
    receiver_cells,
    residuals,
    momentum,
    diffusivity,
):
    depth, size_x, size_y = velocity.shape
    strip = momentum.shape[1]
    wide = strip + 4
    slabs = lax.axis_size("slab")
    shots = lax.axis_size("shot")
    chips = shots // 2
    z_even, z_odd = even_pairs(slabs), odd_slabs(shots, slabs)
    both = ("shot", "slab")
    cube = (depth, size_x, size_y)
    padded = (depth, size_x + 2 * PAD, size_y)
    dma = pltpu.SemaphoreType.DMA

    half = RADIUS // 2
    block = shape(2 * RADIUS + half, size_x, size_y)
    out_b, out_a = call(
        pack_body, [block] * 2, tuple(pltpu.with_memory_space_constraint(x, pltpu.HBM) for x in (wave_state, velocity)), ["hbm"] * 2, ["vmem"] * 2, [dma((2 * (2 * RADIUS + half),))], us=1.3
    )
    first_b = lax.ppermute(out_b, both, z_odd)
    first_a = lax.ppermute(out_a, "slab", z_even)

    flat = shape(2 * RADIUS * size_x + 3 * strip, size_y)
    side = shape(3 * depth, size_y)
    edge = shape(RADIUS, size_x, size_y)
    partial_u, image0, partial_q, push, out_b, out_a, side_a, side_b = call(
        partial_body,
        [shape(*cube)] * 4 + [flat, flat, side, side],
        (wave_state, velocity, receiver_cells, residuals, diffusivity),
        ["vmem"] * 5,
        ["vmem"] * 8,
        [pltpu.VMEM(padded, F32)] * 2 + [pltpu.VMEM((STEPS, depth * size_x, size_y), F32)],
        us=1.7,
    )
    second_b = lax.ppermute(out_b, both, z_odd)
    second_a = lax.ppermute(out_a, "slab", z_even)
    side_a = lax.ppermute(side_a, "shot", even_pairs(shots))
    side_b = lax.ppermute(side_b, "shot", odd_pairs(shots))

    first_a, first_b, side_a, side_b = lax.optimization_barrier((first_a, first_b, side_a, side_b))
    (share_own,) = call(share_body, [edge], (first_a, first_b), ["vmem"] * 2, ["vmem"])
    share_got = lax.ppermute(share_own, "shot", even_pairs(shots))
    ring = shape(2 * RADIUS, size_x, size_y)
    ring_scratch = pltpu.VMEM(ring.shape, F32)
    small = (source_cells, source_codes, wavelets.T)
    u_part, q_part, image_own, gain, tap_u, tap_q = call(
        functools.partial(near_body, scale=math.sqrt(shots * STEPS)),
        [shape(*cube)] * 4 + [ring, ring],
        (wave_state, velocity, partial_u, image0, partial_q, push, first_b, first_a)
        + tuple(pltpu.with_memory_space_constraint(x, pltpu.HBM) for x in small),
        ["vmem"] * 8 + ["hbm"] * 3,
        ["vmem"] * 6,
        [ring_scratch] * 2
        + [pltpu.VMEM(padded, F32)] * 2
        + [pltpu.SMEM(x.shape, x.dtype) for x in small]
        + [dma((3,))],
        us=2.3,
    )

    part = shape(chips, depth * wide, size_y)
    fields, keep, send = call(
        image_body,
        [shape(1, 2, *cube), part, part],
        (velocity, u_part, image_own, gain, tap_u, share_own, share_got, second_b, second_a),
        ["vmem"] * 9,
        ["any"] + ["vmem"] * 2,
        [ring_scratch, pltpu.VMEM(padded, F32), pltpu.VMEM(cube, F32), dma],
        us=1.0,
    )
    got = lax.ppermute(send, "shot", even_pairs(shots))
    (fields,) = call(
        adjoint_body,
        [shape(1, 2, *cube)],
        (fields, velocity, q_part, tap_q, share_own, share_got, second_b, second_a),
        ["any"] + ["vmem"] * 7,
        ["any"],
        [ring_scratch, pltpu.VMEM(cube, F32), dma],
        aliases={0: 0},
        us=0.7,
    )
    tall = 8 * ((wide + 7) // 8)
    (coef,) = call(
        functools.partial(coefficient_body, size_x=size_x),
        [shape(3, depth + 2, tall, size_y)],
        (diffusivity, second_b, second_a, side_a, side_b),
        ["vmem"] * 5,
        ["vmem"],
        us=0.3,
    )
    got, fields, coef = lax.optimization_barrier((got, fields, coef))
    row_block = shape(depth * wide, size_y)
    parts = call(pair_sum_body, [row_block] * chips, (keep, got), ["vmem"] * 2, ["vmem"] * chips)
    arrived = [
        lax.ppermute(parts[k], "shot", [(i, i ^ (2 * k)) for i in range(shots)]) for k in reversed(range(1, chips))
    ] + [parts[0]]
    two = shape(2 * wide, size_y)
    total, out_b, out_a = call(
        functools.partial(strip_sum_body, count=chips, wide=wide),
        [row_block, two, two],
        arrived,
        ["vmem"] * chips,
        ["vmem"] * 3,
    )
    grad_b = lax.ppermute(out_b, both, z_odd)
    grad_a = lax.ppermute(out_a, "slab", z_even)
    new_momentum, new_velocity = call(
        smooth_body,
        [shape(*momentum.shape)] * 2,
        (total, grad_a, grad_b, diffusivity, coef, velocity, momentum),
        ["vmem"] * 7,
        ["block"] * 2,
        [pltpu.VMEM((depth + 4, tall, size_y), F32), pltpu.VMEM((depth + 2, tall, size_y), F32)],
        us=0.7,
    )
    return (fields, new_momentum, new_velocity)


def solution(mesh):
    return jax.shard_map(
        on_device,
        mesh=mesh,
        in_specs=(
            P("slab", None, None),
            P(None, "shot", None, "slab", None, None),
            P("shot", None),
            P("shot", None),
            P(),
            P("shot", None),
            P("shot", None, None),
            P("slab", "shot", None),
            P(None, "slab", "shot", None),
        ),
        out_specs=(
            P("shot", None, "slab", None, None),
            P("slab", "shot", None),
            P("slab", "shot", None),
        ),
        check_vma=False,
    )
```

```python
import functools
import math

import jax
import jax.numpy as jnp
from jax import lax
from jax.experimental import pallas as pl
from jax.experimental.pallas import tpu as pltpu
from jax.sharding import PartitionSpec as P

STENCIL_TAPS = (-205.0 / 72.0, 8.0 / 5.0, -1.0 / 5.0, 8.0 / 315.0, -1.0 / 560.0)
RADIUS = 4
PAD = 8
STEPS = 2
F32 = jnp.float32
BYTES_PER_US = 3.69e6


def even_pairs(count):
    return [(i, i ^ 1) for i in range(count)]


def odd_pairs(count):
    low = [(i, (i + 1) % count) for i in range(1, count, 2)]
    return low + [(b, a) for a, b in low]


def odd_slabs(shots, slabs):
    pairs = []
    for shot in range(shots):
        for slab in range(slabs):
            if slab == 0 or slab == slabs - 1:
                other = (shot ^ 1) * slabs + slab
            else:
                other = shot * slabs + (slab + 1 if slab % 2 else slab - 1)
            pairs.append((shot * slabs + slab, other))
    return pairs


def at_border():
    slab = lax.axis_index("slab")
    return (slab == 0) | (slab == lax.axis_size("slab") - 1)


def ahead(even, border, from_a, from_b):
    return jnp.where(even, jnp.where(border, 0.0, from_b), from_a)


def after(even, border, from_a, from_b):
    return jnp.where(even, from_a, jnp.where(border, 0.0, from_b))


def run_copies(pairs, sems):
    copies = [pltpu.make_async_copy(src, dst, sems.at[k]) for k, (src, dst) in enumerate(pairs)]
    for copy in copies:
        copy.start()
    return copies


SPECS = {
    "any": pl.BlockSpec(memory_space=pl.ANY),
    "hbm": pl.BlockSpec(memory_space=pltpu.HBM),
    "vmem": pl.BlockSpec(memory_space=pltpu.VMEM),
    "block": pl.BlockSpec(),
}


def call(body, out_shapes, operands, in_specs=None, out_specs=None, scratch=(), aliases=None, us=0.1):
    return pl.pallas_call(
        body,
        out_shape=list(out_shapes),
        in_specs=[SPECS[s] for s in in_specs],
        out_specs=[SPECS[s] for s in out_specs],
        scratch_shapes=list(scratch),
        input_output_aliases=aliases or {},
        cost_estimate=pl.CostEstimate(flops=0, bytes_accessed=int(us * BYTES_PER_US), transcendentals=0),
        compiler_params=pltpu.CompilerParams(vmem_limit_bytes=16 * 1024 * 1024),
    )(*operands)


def shape(*dims):
    return jax.ShapeDtypeStruct(dims, F32)


def y_sums(centre, lane, size_y):
    sums = []
    for r in range(1, RADIUS + 1):
        before = jnp.where(lane >= r, pltpu.roll(centre, r, 1), 0.0)
        after = jnp.where(lane < size_y - r, pltpu.roll(centre, size_y - r, 1), 0.0)
        sums.append(before + after)
    return sums


def laplacian_row(field, z, rows, size_x, size_y, lane):
    centre = field[z, PAD : PAD + size_x, :]
    along_y = y_sums(centre, lane, size_y)
    total = (3.0 * STENCIL_TAPS[0]) * centre
    for r in range(1, RADIUS + 1):
        ring = along_y[r - 1]
        ring = ring + (field[z, PAD + r : PAD + r + size_x, :] + field[z, PAD - r : PAD - r + size_x, :])
        if z + r < rows:
            ring = ring + field[z + r, PAD : PAD + size_x, :]
        if z - r >= 0:
            ring = ring + field[z - r, PAD : PAD + size_x, :]
        total = total + STENCIL_TAPS[r] * ring
    return total


def clear_sides(field, size_x):
    rows, _, size_y = field.shape
    edge = jnp.zeros((rows, PAD, size_y), F32)
    field[:, 0:PAD, :] = edge
    field[:, PAD + size_x : PAD + size_x + PAD, :] = edge


def pack_body(state, velocity, out_b, out_a, sems):
    depth = velocity.shape[0]
    half = RADIUS // 2
    even = lax.rem(lax.axis_index("slab"), 2) == 0
    share = lax.rem(lax.axis_index("shot"), 2) * half
    at_a = jnp.where(even, depth - RADIUS, 0)
    at_b = jnp.where(even, 0, depth - RADIUS)
    pairs = []
    for out, at in ((out_a, at_a), (out_b, at_b)):
        for k in range(RADIUS):
            pairs.append((state.at[1, 0, 0, at + k], out.at[k]))
            pairs.append((state.at[1, 0, 1, at + k], out.at[RADIUS + k]))
        for k in range(half):
            pairs.append((velocity.at[at + share + k], out.at[2 * RADIUS + k]))
    for copy in run_copies(pairs, sems):
        copy.wait()


def point_cells(cells, codes, wavelets, moment, first, size_x, size_y, act):
    plane = size_x * size_y
    row_lane = lax.broadcasted_iota(jnp.int32, (1, size_y), 1)
    for k in range(cells.shape[1]):
        cell = cells[0, k]
        amount = wavelets[moment, codes[0, k]]
        z = lax.div(cell, plane) - first
        rest = lax.rem(cell, plane)
        x = lax.div(rest, size_y)
        y = lax.rem(rest, size_y)
        act(z, x, jnp.where(row_lane == y, amount, 0.0))


def weighted(terms):
    total = None
    for r, value in terms:
        term = STENCIL_TAPS[r] * value
        total = term if total is None else total + term
    return total


def partial_body(
    state, velocity, cells, residuals, kappa, source_cells, source_codes, wavelets,
    partial_u, image, partial_q, push, tap_u, weight, out_b, out_a, third_b, third_a,
    field_u, field_q, grid_now, cells_here, codes_here, wavelets_here, sems, *, scale,
):
    small = [(source_cells, cells_here), (source_codes, codes_here), (wavelets, wavelets_here)]
    copies = run_copies(small, sems)
    depth, size_x, size_y = velocity.shape
    strip = kappa.shape[2]
    even = lax.rem(lax.axis_index("slab"), 2) == 0
    for j in range(3):
        tail = kappa[j, depth - 1]
        head = kappa[j, 0]
        at = RADIUS * size_x + j * strip
        out_a[at : at + strip, :] = jnp.where(even, tail, head)
        out_b[at : at + strip, :] = jnp.where(even, head, tail)
    for which, field in ((0, field_u), (1, field_q)):
        clear_sides(field, size_x)
        for z in range(depth):
            field[z, PAD : PAD + size_x, :] = state[1, 0, which, z]

    volume = depth * size_x * size_y
    count = cells.shape[1]
    ids = cells[...] - lax.axis_index("slab") * volume
    inside = (ids >= 0) & (ids < volume)
    kept = jnp.where(inside, ids, 0)
    row = lax.div(kept, jnp.int32(size_y))
    column = kept - row * size_y
    rows = depth * size_x
    pick_row = (lax.broadcasted_iota(jnp.int32, (rows, count), 0) == row).astype(F32)
    pick_column = lax.broadcasted_iota(jnp.int32, (size_y, count), 0) == column
    for moment in range(STEPS):
        amounts = jnp.where(inside, residuals[0, moment : moment + 1, :], 0.0)
        grid_now[moment] = lax.dot_general(
            pick_row,
            jnp.where(pick_column, amounts, 0.0),
            (((1,), (1,)), ((), ())),
            precision=lax.Precision.HIGHEST,
            preferred_element_type=F32,
        )

    lane = lax.broadcasted_iota(jnp.int32, (size_x, size_y), 1)
    for z in range(depth):
        at = slice(z * size_x, (z + 1) * size_x)
        v = velocity[z]
        vv = v * v
        drive = vv * laplacian_row(field_u, z, depth, size_x, size_y, lane)
        partial_u[z] = (2.0 * state[1, 0, 0, z] - state[0, 0, 0, z]) + drive
        image[z] = drive * state[1, 0, 1, z]
        drive = vv * (laplacian_row(field_q, z, depth, size_x, size_y, lane) + grid_now[0, at, :])
        partial_q[z] = (2.0 * state[1, 0, 1, z] - state[0, 0, 1, z]) + drive
        push[z] = vv * grid_now[1, at, :]
        weight[z] = -0.2 / (v * scale)

    def inject(z, x, spot):
        @pl.when((z >= 0) & (z < depth))
        def _():
            at = (z, pl.ds(x, 1), slice(None))
            v = velocity[at]
            change = (v * v) * spot
            partial_u[at] = partial_u[at] + change
            image[at] = image[at] + change * state[1, 0, 1, z, pl.ds(x, 1), :]

    for copy in copies:
        copy.wait()
    first_layer = lax.axis_index("slab") * depth
    point_cells(cells_here, codes_here, wavelets_here, 0, first_layer, size_x, size_y, inject)
    for k in range(2 * RADIUS):
        tap_u[k] = weighted([(r, state[1, 0, 0, own]) for r, own in halo_near(k, depth)])
    for source, to_a, to_b in ((partial_u, out_a, out_b), (partial_q, third_a, third_b)):
        for k in range(RADIUS):
            tail = source[depth - RADIUS + k]
            head = source[k]
            to_a[k * size_x : (k + 1) * size_x, :] = jnp.where(even, tail, head)
            to_b[k * size_x : (k + 1) * size_x, :] = jnp.where(even, head, tail)


def share_body(first_a, first_b, share):
    half = RADIUS // 2
    for k in range(half):
        share[k] = first_a[2 * RADIUS + k]
        share[half + k] = first_b[2 * RADIUS + k]


def halo_speed(k, share_own, share_got):
    half = RADIUS // 2
    row = k % RADIUS
    even = lax.rem(lax.axis_index("slab"), 2) == 0
    border = at_border()
    own = lax.rem(lax.axis_index("shot"), 2) == row // half
    at_a = jnp.where(own, share_own[row % half], share_got[row % half])
    at_b = jnp.where(own, share_own[half + row % half], share_got[half + row % half])
    return (ahead if k < RADIUS else after)(even, border, at_a, at_b)


def halo_near(k, depth):
    if k < RADIUS:
        return [(r, k - RADIUS + r) for r in range(1, RADIUS + 1) if k - RADIUS + r >= 0]
    row = k - RADIUS
    return [(r, depth + row - r) for r in range(1, RADIUS + 1) if depth + row - r < depth]


def own_near(z, depth):
    near = [(r, RADIUS + z - r) for r in range(1, RADIUS + 1) if z - r < 0]
    return near + [(r, RADIUS + z + r - depth) for r in range(1, RADIUS + 1) if z + r >= depth]


def near_body(
    state, velocity, partial_u, image0, partial_q, weight, first_a, first_b, cells, codes, wavelets,
    u_part, q_next, image, gain,
    u_edge, q_edge, u_now, cells_here, codes_here, wavelets_here, sems,
):
    small = run_copies([(cells, cells_here), (codes, codes_here), (wavelets, wavelets_here)], sems)
    depth, size_x, size_y = velocity.shape
    even = lax.rem(lax.axis_index("slab"), 2) == 0
    border = at_border()
    middle = slice(PAD, PAD + size_x)
    clear_sides(u_now, size_x)
    for k in range(2 * RADIUS):
        row = k % RADIUS
        pick = ahead if k < RADIUS else after
        u_edge[k] = pick(even, border, first_a[row], first_b[row])
        q_edge[k] = pick(even, border, first_a[RADIUS + row], first_b[RADIUS + row])
    for z in range(depth):
        near = own_near(z, depth)
        if not near:
            u_now[z, middle, :] = partial_u[z]
            q_next[z] = partial_q[z]
            image[z] = image0[z]
            continue
        v = velocity[z]
        vv = v * v
        change = vv * weighted([(r, u_edge[k]) for r, k in near])
        u_now[z, middle, :] = partial_u[z] + change
        image[z] = image0[z] + change * state[1, 0, 1, z]
        q_next[z] = partial_q[z] + vv * weighted([(r, q_edge[k]) for r, k in near])

    def second_step(z, x, spot):
        @pl.when((z >= 0) & (z < depth))
        def _():
            at = (z, pl.ds(x, 1), slice(None))
            v = velocity[at]
            change = (v * v) * spot
            u_part[at] = u_part[at] + change
            image[at] = image[at] + weight[at] * (change * q_next[at])

    lane = lax.broadcasted_iota(jnp.int32, (size_x, size_y), 1)
    for z in range(depth):
        v = velocity[z]
        vv = v * v
        adjoint = q_next[z]
        drive = vv * laplacian_row(u_now, z, depth, size_x, size_y, lane)
        u_part[z] = (2.0 * u_now[z, middle, :] - state[1, 0, 0, z]) + drive
        image[z] = weight[z] * (image[z] + drive * adjoint)
        gain[z] = (weight[z] * vv) * adjoint
    for copy in small:
        copy.wait()
    first_layer = lax.axis_index("slab") * depth
    point_cells(cells_here, codes_here, wavelets_here, 1, first_layer, size_x, size_y, second_step)


def halo_field(halo, second_b, second_a, tap, share_own, share_got):
    size_x = halo.shape[1]
    even = lax.rem(lax.axis_index("slab"), 2) == 0
    border = at_border()
    for k in range(2 * RADIUS):
        row = k % RADIUS
        rows = slice(row * size_x, (row + 1) * size_x)
        pick = ahead if k < RADIUS else after
        v = halo_speed(k, share_own, share_got)
        halo[k] = pick(even, border, second_a[rows, :], second_b[rows, :]) + (v * v) * tap[k]


def image_body(
    velocity, kappa, u_part, image_own, gain, tap_u, share_own, share_got, second_b, second_a,
    fields, keep, packed, halo, image, u_out, out_sem,
):
    depth, size_x, size_y = velocity.shape
    core = lax.rem(lax.axis_index("shot"), 2)
    middle = slice(PAD, PAD + size_x)
    clear_sides(image, size_x)
    halo_field(halo, second_b, second_a, tap_u, share_own, share_got)
    for z in range(depth):
        near = own_near(z, depth)
        if not near:
            u_out[z] = u_part[z]
            image[z, middle, :] = image_own[z]
            continue
        v = velocity[z]
        crossing = weighted([(r, halo[k]) for r, k in near])
        u_out[z] = u_part[z] + (v * v) * crossing
        image[z, middle, :] = image_own[z] + gain[z] * crossing
    copy_out = pltpu.make_async_copy(u_out, fields.at[0, 0], out_sem)
    copy_out.start()
    chip = lax.div(lax.axis_index("shot"), 2)
    chips = keep.shape[0]
    strip = size_x // (2 * chips)
    wide = strip + 4
    rows = depth * wide
    for m in range(chips):
        to = jnp.bitwise_xor(chip, m)
        for z in range(depth):
            at = PAD + 2 * m * strip - 2
            low = image[z, at : at + wide, :]
            high = image[z, at + strip : at + strip + wide, :]
            keep[to, z * wide : (z + 1) * wide, :] = jnp.where(core == 0, low, high)
            packed[pl.ds(to * rows + z * wide, wide), :] = jnp.where(core == 0, high, low)
    for j in range(3):
        tail = kappa[j, :, strip - 1, :]
        head = kappa[j, :, 0, :]
        at = chips * rows + j * depth
        packed[at : at + depth, :] = jnp.where(core == 0, tail, head)
        packed[at + 3 * depth : at + 4 * depth, :] = jnp.where(core == 0, head, tail)
    copy_out.wait()


def hands_on(k):
    return k > 0 and k & (k + 1) == 0


def pair_sum_body(keep, got, *outs):
    rows = keep.shape[1]
    for k, out in enumerate(outs):
        out[0:rows, :] = keep[k] + got[k * rows : (k + 1) * rows, :]
        if hands_on(k):
            side = (out.shape[0] - rows)
            out[rows : rows + side, :] = got[len(outs) * rows + side : len(outs) * rows + 2 * side, :]


def strip_sum_body(*refs, count, wide):
    parts, (total, edge_b, edge_a) = refs[:count], refs[count:]
    rows = total.shape[0]
    added = parts[0][0:rows, :]
    for part in parts[1:]:
        added = added + part[0:rows, :]
    total[...] = added
    even = lax.rem(lax.axis_index("slab"), 2) == 0
    head = total[0 : 2 * wide, :]
    tail = total[rows - 2 * wide : rows, :]
    edge_a[...] = jnp.where(even, tail, head)
    edge_b[...] = jnp.where(even, head, tail)


def adjoint_body(
    fields_in, state, velocity, q_next, push, share_own, share_got, third_b, third_a, fields, field, tap, halo, q_out, out_sem
):
    depth, size_x, size_y = velocity.shape
    whole = depth + 2 * RADIUS
    middle = slice(PAD, PAD + size_x)
    clear_sides(field, size_x)
    for k in range(2 * RADIUS):
        tap[k] = weighted([(r, state[1, 0, 1, own]) for r, own in halo_near(k, depth)])
    halo_field(halo, third_b, third_a, tap, share_own, share_got)
    for z in range(whole):
        inner = RADIUS <= z < RADIUS + depth
        field[z, middle, :] = q_next[z - RADIUS] if inner else halo[z if z < RADIUS else z - depth]
    lane = lax.broadcasted_iota(jnp.int32, (size_x, size_y), 1)
    for z in range(depth):
        v = velocity[z]
        drive = (v * v) * laplacian_row(field, z + RADIUS, whole, size_x, size_y, lane) + push[z]
        q_out[z] = (2.0 * q_next[z] - state[1, 0, 1, z]) + drive
    copy = pltpu.make_async_copy(q_out, fields.at[0, 1], out_sem)
    copy.start()
    copy.wait()


def coefficient_body(kappa, second_b, second_a, got, *rest, size_x, distances):
    arrived, coef = rest[:-1], rest[-1]
    _, depth, strip, _ = kappa.shape
    even = lax.rem(lax.axis_index("slab"), 2) == 0
    border = at_border()
    shot = lax.axis_index("shot")
    even_strip = lax.rem(shot, 2) == 0
    end_strip = (shot == 0) | (shot == lax.axis_size("shot") - 1)
    chip = lax.div(shot, 2)
    distance = jnp.bitwise_xor(chip, jnp.where(even_strip, chip - 1, chip + 1))
    side = 3 * depth
    ends = [part.shape[0] for part in arrived]
    far = arrived[0][ends[0] - side : ends[0], :]
    for k, end, part in zip(distances[1:], ends[1:], arrived[1:]):
        far = jnp.where(distance == k, part[end - side : end, :], far)
    facing = got[got.shape[0] - 2 * side : got.shape[0] - side, :]
    coef[...] = jnp.zeros(coef.shape, F32)
    for j in range(3):
        at = slice(RADIUS * size_x + j * strip, RADIUS * size_x + (j + 1) * strip)
        coef[j, 0, 1 : strip + 1, :] = ahead(even, border, second_a[at, :], second_b[at, :])
        coef[j, depth + 1, 1 : strip + 1, :] = after(even, border, second_a[at, :], second_b[at, :])
        of = slice(j * depth, (j + 1) * depth)
        left = ahead(even_strip, end_strip, facing[of, :], far[of, :])
        right = after(even_strip, end_strip, facing[of, :], far[of, :])
        for z in range(depth):
            coef[j, z + 1, 1 : strip + 1, :] = kappa[j, z]
            coef[j, z + 1, 0:1, :] = left[z : z + 1, :]
            coef[j, z + 1, strip + 1 : strip + 2, :] = right[z : z + 1, :]


def smooth_body(total, got_a, got_b, kappa, coef, velocity, momentum, new_momentum, new_speed, grad, half):
    depth, strip, size_y = momentum.shape
    column = lax.axis_index("shot") * strip
    wide = strip + 4
    even = lax.rem(lax.axis_index("slab"), 2) == 0
    border = at_border()
    for k in range(2):
        at = slice(k * wide, (k + 1) * wide)
        grad[k, 0:wide, :] = ahead(even, border, got_a[at, :], got_b[at, :])
        grad[depth + 2 + k, 0:wide, :] = after(even, border, got_a[at, :], got_b[at, :])
    for z in range(depth):
        grad[z + 2, 0:wide, :] = total[z * wide : (z + 1) * wide, :]

    def step(source, z, rows, factors):
        centre = source[z, 1 : 1 + rows, :]
        lane = lax.broadcasted_iota(jnp.int32, centre.shape, 1)
        twice = 2.0 * centre
        along_z = source[z + 1, 1 : 1 + rows, :] - twice + source[z - 1, 1 : 1 + rows, :]
        along_x = source[z, 2 : 2 + rows, :] - twice + source[z, 0:rows, :]
        after = jnp.where(lane < size_y - 1, pltpu.roll(centre, size_y - 1, 1), 0.0)
        before = jnp.where(lane >= 1, pltpu.roll(centre, 1, 1), 0.0)
        along_y = after - twice + before
        return centre + factors[0] * along_z + factors[1] * along_x + factors[2] * along_y

    for z in range(depth + 2):
        half[z, 0 : strip + 2, :] = step(grad, z + 1, strip + 2, [coef[j, z, 0 : strip + 2, :] for j in range(3)])
    for z in range(depth):
        smoothed = step(half, z + 1, strip, [kappa[j, z] for j in range(3)])
        fresh = 0.9 * momentum[z] + smoothed
        new_momentum[z] = fresh
        new_speed[z] = velocity[z, pl.ds(column, strip), :] - 0.02 * fresh


def on_device(
    velocity,
    wave_state,
    source_cells,
    source_codes,
    wavelets,
    receiver_cells,
    residuals,
    momentum,
    diffusivity,
):
    depth, size_x, size_y = velocity.shape
    strip = momentum.shape[1]
    wide = strip + 4
    slabs = lax.axis_size("slab")
    shots = lax.axis_size("shot")
    chips = shots // 2
    z_even, z_odd = even_pairs(slabs), odd_slabs(shots, slabs)
    both = ("shot", "slab")
    cube = (depth, size_x, size_y)
    padded = (depth, size_x + 2 * PAD, size_y)
    dma = pltpu.SemaphoreType.DMA

    half = RADIUS // 2
    block = shape(2 * RADIUS + half, size_x, size_y)
    out_b, out_a = call(
        pack_body, [block] * 2, tuple(pltpu.with_memory_space_constraint(x, pltpu.HBM) for x in (wave_state, velocity)), ["hbm"] * 2, ["vmem"] * 2, [dma((2 * (2 * RADIUS + half),))], us=1.3
    )
    first_b = lax.ppermute(out_b, both, z_odd)
    first_a = lax.ppermute(out_a, "slab", z_even)

    flat = shape(RADIUS * size_x + 3 * strip, size_y)
    flat_q = shape(RADIUS * size_x, size_y)
    edge = shape(RADIUS, size_x, size_y)
    ring = shape(2 * RADIUS, size_x, size_y)
    ring_scratch = pltpu.VMEM(ring.shape, F32)
    small = tuple(
        pltpu.with_memory_space_constraint(x, pltpu.HBM) for x in (source_cells, source_codes, wavelets.T)
    )
    small_scratch = [pltpu.SMEM(x.shape, x.dtype) for x in small] + [dma((3,))]
    partial_u, image0, partial_q, push, tap_u, weight, out_b, out_a, third_b, third_a = call(
        functools.partial(partial_body, scale=math.sqrt(shots * STEPS)),
        [shape(*cube)] * 4 + [ring, shape(*cube), flat, flat, flat_q, flat_q],
        (wave_state, velocity, receiver_cells, residuals, diffusivity, *small),
        ["vmem"] * 5 + ["hbm"] * 3,
        ["vmem"] * 10,
        [pltpu.VMEM(padded, F32)] * 2 + [pltpu.VMEM((STEPS, depth * size_x, size_y), F32)] + small_scratch,
        us=1.7,
    )
    second_b = lax.ppermute(out_b, both, z_odd)
    second_a = lax.ppermute(out_a, "slab", z_even)
    third_b = lax.ppermute(third_b, both, z_odd)
    third_a = lax.ppermute(third_a, "slab", z_even)

    (share_own,) = call(share_body, [edge], (first_a, first_b), ["vmem"] * 2, ["vmem"])
    share_got = lax.ppermute(share_own, "shot", even_pairs(shots))
    u_part, q_next, image_own, gain = call(
        near_body,
        [shape(*cube)] * 4,
        (wave_state, velocity, partial_u, image0, partial_q, weight, first_a, first_b, *small),
        ["vmem"] * 8 + ["hbm"] * 3,
        ["vmem"] * 4,
        [ring_scratch] * 2 + [pltpu.VMEM(padded, F32)] + small_scratch,
        us=1.2,
    )

    part = shape(chips, depth * wide, size_y)
    side = 3 * depth
    fields, keep, send = call(
        image_body,
        [shape(1, 2, *cube), part, shape(chips * depth * wide + 2 * side, size_y)],
        (velocity, diffusivity, u_part, image_own, gain, tap_u, share_own, share_got, second_b, second_a),
        ["vmem"] * 10,
        ["any"] + ["vmem"] * 2,
        [ring_scratch, pltpu.VMEM(padded, F32), pltpu.VMEM(cube, F32), dma],
        us=1.0,
    )
    got = lax.ppermute(send, "shot", even_pairs(shots))
    (fields,) = call(
        adjoint_body,
        [shape(1, 2, *cube)],
        (fields, wave_state, velocity, q_next, push, share_own, share_got, third_b, third_a),
        ["any"] + ["vmem"] * 8,
        ["any"],
        [
            pltpu.VMEM((depth + 2 * RADIUS, size_x + 2 * PAD, size_y), F32),
            ring_scratch,
            ring_scratch,
            pltpu.VMEM(cube, F32),
            dma,
        ],
        aliases={0: 0},
        us=1.4,
    )
    row_block = shape(depth * wide, size_y)
    sums = [shape(depth * wide + (side if hands_on(k) else 0), size_y) for k in range(chips)]
    parts = call(pair_sum_body, sums, (keep, got), ["vmem"] * 2, ["vmem"] * chips)
    arrived = [
        lax.ppermute(parts[k], "shot", [(i, i ^ (2 * k)) for i in range(shots)]) for k in reversed(range(1, chips))
    ] + [parts[0]]
    *arrived, fields = lax.optimization_barrier((*arrived, fields))
    two = shape(2 * wide, size_y)
    total, out_b, out_a = call(
        functools.partial(strip_sum_body, count=chips, wide=wide),
        [row_block, two, two],
        arrived,
        ["vmem"] * chips,
        ["vmem"] * 3,
    )
    grad_b = lax.ppermute(out_b, both, z_odd)
    grad_a = lax.ppermute(out_a, "slab", z_even)
    distances = [k for k in range(chips) if hands_on(k)]
    tall = 8 * ((wide + 7) // 8)
    (coef,) = call(
        functools.partial(coefficient_body, size_x=size_x, distances=distances),
        [shape(3, depth + 2, tall, size_y)],
        (diffusivity, second_b, second_a, got, *(arrived[chips - 1 - k] for k in distances)),
        ["vmem"] * (4 + len(distances)),
        ["vmem"],
        us=0.1,
    )
    new_momentum, new_velocity = call(
        smooth_body,
        [shape(*momentum.shape)] * 2,
        (total, grad_a, grad_b, diffusivity, coef, velocity, momentum),
        ["vmem"] * 7,
        ["block"] * 2,
        [pltpu.VMEM((depth + 4, tall, size_y), F32), pltpu.VMEM((depth + 2, tall, size_y), F32)],
        us=0.7,
    )
    return (fields, new_momentum, new_velocity)


def solution(mesh):
    return jax.shard_map(
        on_device,
        mesh=mesh,
        in_specs=(
            P("slab", None, None),
            P(None, "shot", None, "slab", None, None),
            P("shot", None),
            P("shot", None),
            P(),
            P("shot", None),
            P("shot", None, None),
            P("slab", "shot", None),
            P(None, "slab", "shot", None),
        ),
        out_specs=(
            P("shot", None, "slab", None, None),
            P("slab", "shot", None),
            P("slab", "shot", None),
        ),
        check_vma=False,
    )
```

```python
import functools
import math

import jax
import jax.numpy as jnp
from jax import lax
from jax.experimental import pallas as pl
from jax.experimental.pallas import tpu as pltpu
from jax.sharding import PartitionSpec as P

STENCIL_TAPS = (-205.0 / 72.0, 8.0 / 5.0, -1.0 / 5.0, 8.0 / 315.0, -1.0 / 560.0)
RADIUS = 4
PAD = 8
STEPS = 2
F32 = jnp.float32
BYTES_PER_US = 3.69e6


def even_pairs(count):
    return [(i, i ^ 1) for i in range(count)]


def odd_pairs(count):
    low = [(i, (i + 1) % count) for i in range(1, count, 2)]
    return low + [(b, a) for a, b in low]


def odd_slabs(shots, slabs):
    pairs = []
    for shot in range(shots):
        for slab in range(slabs):
            if slab == 0 or slab == slabs - 1:
                other = (shot ^ 1) * slabs + slab
            else:
                other = shot * slabs + (slab + 1 if slab % 2 else slab - 1)
            pairs.append((shot * slabs + slab, other))
    return pairs


def at_border():
    slab = lax.axis_index("slab")
    return (slab == 0) | (slab == lax.axis_size("slab") - 1)


def ahead(even, border, from_a, from_b):
    return jnp.where(even, jnp.where(border, 0.0, from_b), from_a)


def after(even, border, from_a, from_b):
    return jnp.where(even, from_a, jnp.where(border, 0.0, from_b))


def run_copies(pairs, sems):
    copies = [pltpu.make_async_copy(src, dst, sems.at[k]) for k, (src, dst) in enumerate(pairs)]
    for copy in copies:
        copy.start()
    return copies


SPECS = {
    "any": pl.BlockSpec(memory_space=pl.ANY),
    "hbm": pl.BlockSpec(memory_space=pltpu.HBM),
    "vmem": pl.BlockSpec(memory_space=pltpu.VMEM),
    "block": pl.BlockSpec(),
}


def call(body, out_shapes, operands, in_specs=None, out_specs=None, scratch=(), aliases=None, us=0.1):
    return pl.pallas_call(
        body,
        out_shape=list(out_shapes),
        in_specs=[SPECS[s] for s in in_specs],
        out_specs=[SPECS[s] for s in out_specs],
        scratch_shapes=list(scratch),
        input_output_aliases=aliases or {},
        cost_estimate=pl.CostEstimate(flops=0, bytes_accessed=int(us * BYTES_PER_US), transcendentals=0),
        compiler_params=pltpu.CompilerParams(vmem_limit_bytes=16 * 1024 * 1024),
    )(*operands)


def shape(*dims):
    return jax.ShapeDtypeStruct(dims, F32)


def y_sums(centre, lane, size_y):
    sums = []
    for r in range(1, RADIUS + 1):
        before = jnp.where(lane >= r, pltpu.roll(centre, r, 1), 0.0)
        after = jnp.where(lane < size_y - r, pltpu.roll(centre, size_y - r, 1), 0.0)
        sums.append(before + after)
    return sums


def laplacian_row(field, z, rows, size_x, size_y, lane):
    centre = field[z, PAD : PAD + size_x, :]
    along_y = y_sums(centre, lane, size_y)
    total = (3.0 * STENCIL_TAPS[0]) * centre
    for r in range(1, RADIUS + 1):
        ring = along_y[r - 1]
        ring = ring + (field[z, PAD + r : PAD + r + size_x, :] + field[z, PAD - r : PAD - r + size_x, :])
        if z + r < rows:
            ring = ring + field[z + r, PAD : PAD + size_x, :]
        if z - r >= 0:
            ring = ring + field[z - r, PAD : PAD + size_x, :]
        total = total + STENCIL_TAPS[r] * ring
    return total


def clear_sides(field, size_x):
    rows, _, size_y = field.shape
    edge = jnp.zeros((rows, PAD, size_y), F32)
    field[:, 0:PAD, :] = edge
    field[:, PAD + size_x : PAD + size_x + PAD, :] = edge


def pack_body(state, velocity, out_b, out_a, sems):
    depth = velocity.shape[0]
    half = RADIUS // 2
    even = lax.rem(lax.axis_index("slab"), 2) == 0
    share = lax.rem(lax.axis_index("shot"), 2) * half
    at_a = jnp.where(even, depth - RADIUS, 0)
    at_b = jnp.where(even, 0, depth - RADIUS)
    pairs = []
    for out, at in ((out_a, at_a), (out_b, at_b)):
        for k in range(RADIUS):
            pairs.append((state.at[1, 0, 0, at + k], out.at[k]))
            pairs.append((state.at[1, 0, 1, at + k], out.at[RADIUS + k]))
        for k in range(half):
            pairs.append((velocity.at[at + share + k], out.at[2 * RADIUS + k]))
    for copy in run_copies(pairs, sems):
        copy.wait()


def point_cells(cells, codes, wavelets, moment, first, size_x, size_y, act):
    plane = size_x * size_y
    row_lane = lax.broadcasted_iota(jnp.int32, (1, size_y), 1)
    for k in range(cells.shape[1]):
        cell = cells[0, k]
        amount = wavelets[moment, codes[0, k]]
        z = lax.div(cell, plane) - first
        rest = lax.rem(cell, plane)
        x = lax.div(rest, size_y)
        y = lax.rem(rest, size_y)
        act(z, x, jnp.where(row_lane == y, amount, 0.0))


def weighted(terms):
    total = None
    for r, value in terms:
        term = STENCIL_TAPS[r] * value
        total = term if total is None else total + term
    return total


def partial_body(
    state, velocity, cells, residuals, kappa, source_cells, source_codes, wavelets,
    partial_u, image, partial_q, push_u, push, tap_u, weight, out_b, out_a, third_b, third_a,
    field_u, field_q, grid_now, cells_here, codes_here, wavelets_here, sems, *, scale,
):
    small = [(source_cells, cells_here), (source_codes, codes_here), (wavelets, wavelets_here)]
    copies = run_copies(small, sems)
    depth, size_x, size_y = velocity.shape
    strip = kappa.shape[2]
    even = lax.rem(lax.axis_index("slab"), 2) == 0
    for j in range(3):
        tail = kappa[j, depth - 1]
        head = kappa[j, 0]
        at = RADIUS * size_x + j * strip
        third_a[at : at + strip, :] = jnp.where(even, tail, head)
        third_b[at : at + strip, :] = jnp.where(even, head, tail)
    for which, field in ((0, field_u), (1, field_q)):
        clear_sides(field, size_x)
        for z in range(depth):
            field[z, PAD : PAD + size_x, :] = state[1, 0, which, z]

    volume = depth * size_x * size_y
    count = cells.shape[1]
    ids = cells[...] - lax.axis_index("slab") * volume
    inside = (ids >= 0) & (ids < volume)
    kept = jnp.where(inside, ids, 0)
    row = lax.div(kept, jnp.int32(size_y))
    column = kept - row * size_y
    rows = depth * size_x
    pick_row = (lax.broadcasted_iota(jnp.int32, (rows, count), 0) == row).astype(F32)
    pick_column = lax.broadcasted_iota(jnp.int32, (size_y, count), 0) == column
    for moment in range(STEPS):
        amounts = jnp.where(inside, residuals[0, moment : moment + 1, :], 0.0)
        grid_now[moment] = lax.dot_general(
            pick_row,
            jnp.where(pick_column, amounts, 0.0),
            (((1,), (1,)), ((), ())),
            precision=lax.Precision.HIGHEST,
            preferred_element_type=F32,
        )

    lane = lax.broadcasted_iota(jnp.int32, (size_x, size_y), 1)
    for z in range(depth):
        at = slice(z * size_x, (z + 1) * size_x)
        v = velocity[z]
        vv = v * v
        drive = vv * laplacian_row(field_u, z, depth, size_x, size_y, lane)
        partial_u[z] = (2.0 * state[1, 0, 0, z] - state[0, 0, 0, z]) + drive
        image[z] = drive * state[1, 0, 1, z]
        drive = vv * (laplacian_row(field_q, z, depth, size_x, size_y, lane) + grid_now[0, at, :])
        partial_q[z] = (2.0 * state[1, 0, 1, z] - state[0, 0, 1, z]) + drive
        push[z] = vv * grid_now[1, at, :]
        weight[z] = -0.2 / (v * scale)
        push_u[z] = jnp.zeros((size_x, size_y), F32)

    def inject(z, x, spot):
        @pl.when((z >= 0) & (z < depth))
        def _():
            at = (z, pl.ds(x, 1), slice(None))
            v = velocity[at]
            change = (v * v) * spot
            partial_u[at] = partial_u[at] + change
            image[at] = image[at] + change * state[1, 0, 1, z, pl.ds(x, 1), :]

    def inject_next(z, x, spot):
        @pl.when((z >= 0) & (z < depth))
        def _():
            at = (z, pl.ds(x, 1), slice(None))
            v = velocity[at]
            push_u[at] = push_u[at] + (v * v) * spot

    for copy in copies:
        copy.wait()
    first_layer = lax.axis_index("slab") * depth
    point_cells(cells_here, codes_here, wavelets_here, 0, first_layer, size_x, size_y, inject)
    point_cells(cells_here, codes_here, wavelets_here, 1, first_layer, size_x, size_y, inject_next)
    for k in range(2 * RADIUS):
        tap_u[k] = weighted([(r, state[1, 0, 0, own]) for r, own in halo_near(k, depth)])
    for source, to_a, to_b in ((partial_u, out_a, out_b), (partial_q, third_a, third_b)):
        for k in range(RADIUS):
            tail = source[depth - RADIUS + k]
            head = source[k]
            to_a[k * size_x : (k + 1) * size_x, :] = jnp.where(even, tail, head)
            to_b[k * size_x : (k + 1) * size_x, :] = jnp.where(even, head, tail)


def share_body(first_a, first_b, share):
    half = RADIUS // 2
    for k in range(half):
        share[k] = first_a[2 * RADIUS + k]
        share[half + k] = first_b[2 * RADIUS + k]


def halo_speed(k, share_own, share_got):
    half = RADIUS // 2
    row = k % RADIUS
    even = lax.rem(lax.axis_index("slab"), 2) == 0
    border = at_border()
    own = lax.rem(lax.axis_index("shot"), 2) == row // half
    at_a = jnp.where(own, share_own[row % half], share_got[row % half])
    at_b = jnp.where(own, share_own[half + row % half], share_got[half + row % half])
    return (ahead if k < RADIUS else after)(even, border, at_a, at_b)


def halo_near(k, depth):
    if k < RADIUS:
        return [(r, k - RADIUS + r) for r in range(1, RADIUS + 1) if k - RADIUS + r >= 0]
    row = k - RADIUS
    return [(r, depth + row - r) for r in range(1, RADIUS + 1) if depth + row - r < depth]


def own_near(z, depth):
    near = [(r, RADIUS + z - r) for r in range(1, RADIUS + 1) if z - r < 0]
    return near + [(r, RADIUS + z + r - depth) for r in range(1, RADIUS + 1) if z + r >= depth]


def near_body(
    state, velocity, partial_u, image0, partial_q, push, weight, first_a, first_b,
    u_part, q_next, image, gain, u_edge, q_edge, u_now,
):
    depth, size_x, size_y = velocity.shape
    even = lax.rem(lax.axis_index("slab"), 2) == 0
    border = at_border()
    middle = slice(PAD, PAD + size_x)
    clear_sides(u_now, size_x)
    for k in range(2 * RADIUS):
        row = k % RADIUS
        pick = ahead if k < RADIUS else after
        u_edge[k] = pick(even, border, first_a[row], first_b[row])
        q_edge[k] = pick(even, border, first_a[RADIUS + row], first_b[RADIUS + row])
    for z in range(depth):
        near = own_near(z, depth)
        if not near:
            u_now[z, middle, :] = partial_u[z]
            q_next[z] = partial_q[z]
            image[z] = image0[z]
            continue
        v = velocity[z]
        vv = v * v
        change = vv * weighted([(r, u_edge[k]) for r, k in near])
        u_now[z, middle, :] = partial_u[z] + change
        image[z] = image0[z] + change * state[1, 0, 1, z]
        q_next[z] = partial_q[z] + vv * weighted([(r, q_edge[k]) for r, k in near])

    lane = lax.broadcasted_iota(jnp.int32, (size_x, size_y), 1)
    for z in range(depth):
        v = velocity[z]
        vv = v * v
        adjoint = q_next[z]
        drive = vv * laplacian_row(u_now, z, depth, size_x, size_y, lane) + push[z]
        u_part[z] = (2.0 * u_now[z, middle, :] - state[1, 0, 0, z]) + drive
        image[z] = weight[z] * (image[z] + drive * adjoint)
        gain[z] = (weight[z] * vv) * adjoint


def halo_field(halo, second_b, second_a, tap, share_own, share_got):
    size_x = halo.shape[1]
    even = lax.rem(lax.axis_index("slab"), 2) == 0
    border = at_border()
    for k in range(2 * RADIUS):
        row = k % RADIUS
        rows = slice(row * size_x, (row + 1) * size_x)
        pick = ahead if k < RADIUS else after
        v = halo_speed(k, share_own, share_got)
        halo[k] = pick(even, border, second_a[rows, :], second_b[rows, :]) + (v * v) * tap[k]


def image_body(
    velocity, kappa, u_part, image_own, gain, tap_u, share_own, share_got, second_b, second_a,
    u_out, keep, packed, halo, image,
):
    depth, size_x, size_y = velocity.shape
    core = lax.rem(lax.axis_index("shot"), 2)
    middle = slice(PAD, PAD + size_x)
    clear_sides(image, size_x)
    halo_field(halo, second_b, second_a, tap_u, share_own, share_got)
    for z in range(depth):
        near = own_near(z, depth)
        if not near:
            u_out[z] = u_part[z]
            image[z, middle, :] = image_own[z]
            continue
        v = velocity[z]
        crossing = weighted([(r, halo[k]) for r, k in near])
        u_out[z] = u_part[z] + (v * v) * crossing
        image[z, middle, :] = image_own[z] + gain[z] * crossing
    chip = lax.div(lax.axis_index("shot"), 2)
    chips = keep.shape[0]
    strip = size_x // (2 * chips)
    wide = strip + 4
    rows = depth * wide
    for m in range(chips):
        to = jnp.bitwise_xor(chip, m)
        for z in range(depth):
            at = PAD + 2 * m * strip - 2
            low = image[z, at : at + wide, :]
            high = image[z, at + strip : at + strip + wide, :]
            keep[to, z * wide : (z + 1) * wide, :] = jnp.where(core == 0, low, high)
            packed[pl.ds(to * rows + z * wide, wide), :] = jnp.where(core == 0, high, low)
    for j in range(3):
        tail = kappa[j, :, strip - 1, :]
        head = kappa[j, :, 0, :]
        at = chips * rows + j * depth
        packed[at : at + depth, :] = jnp.where(core == 0, tail, head)
        packed[at + 3 * depth : at + 4 * depth, :] = jnp.where(core == 0, head, tail)


def hands_on(k):
    return k > 0 and k & (k + 1) == 0


def pair_sum_body(keep, got, *outs):
    rows = keep.shape[1]
    for k, out in enumerate(outs):
        out[0:rows, :] = keep[k] + got[k * rows : (k + 1) * rows, :]
        if hands_on(k):
            side = (out.shape[0] - rows)
            out[rows : rows + side, :] = got[len(outs) * rows + side : len(outs) * rows + 2 * side, :]


def strip_sum_body(*refs, count, wide):
    parts, (total, edge_b, edge_a) = refs[:count], refs[count:]
    rows = total.shape[0]
    added = parts[0][0:rows, :]
    for part in parts[1:]:
        added = added + part[0:rows, :]
    total[...] = added
    even = lax.rem(lax.axis_index("slab"), 2) == 0
    head = total[0 : 2 * wide, :]
    tail = total[rows - 2 * wide : rows, :]
    edge_a[...] = jnp.where(even, tail, head)
    edge_b[...] = jnp.where(even, head, tail)


def adjoint_body(
    state, velocity, u_out, q_next, push, share_own, share_got, third_b, third_a, fields, field, tap, halo, q_out, sems
):
    copy_u = pltpu.make_async_copy(u_out, fields.at[0, 0], sems.at[0])
    copy_u.start()
    depth, size_x, size_y = velocity.shape
    whole = depth + 2 * RADIUS
    middle = slice(PAD, PAD + size_x)
    clear_sides(field, size_x)
    for k in range(2 * RADIUS):
        tap[k] = weighted([(r, state[1, 0, 1, own]) for r, own in halo_near(k, depth)])
    halo_field(halo, third_b, third_a, tap, share_own, share_got)
    for z in range(whole):
        inner = RADIUS <= z < RADIUS + depth
        field[z, middle, :] = q_next[z - RADIUS] if inner else halo[z if z < RADIUS else z - depth]
    lane = lax.broadcasted_iota(jnp.int32, (size_x, size_y), 1)
    for z in range(depth):
        v = velocity[z]
        drive = (v * v) * laplacian_row(field, z + RADIUS, whole, size_x, size_y, lane) + push[z]
        q_out[z] = (2.0 * q_next[z] - state[1, 0, 1, z]) + drive
    copy_q = pltpu.make_async_copy(q_out, fields.at[0, 1], sems.at[1])
    copy_q.start()
    copy_u.wait()
    copy_q.wait()


def coefficient_body(kappa, third_b, third_a, got, *rest, size_x, distances):
    arrived, coef = rest[:-1], rest[-1]
    _, depth, strip, _ = kappa.shape
    even = lax.rem(lax.axis_index("slab"), 2) == 0
    border = at_border()
    shot = lax.axis_index("shot")
    even_strip = lax.rem(shot, 2) == 0
    end_strip = (shot == 0) | (shot == lax.axis_size("shot") - 1)
    chip = lax.div(shot, 2)
    distance = jnp.bitwise_xor(chip, jnp.where(even_strip, chip - 1, chip + 1))
    side = 3 * depth
    ends = [part.shape[0] for part in arrived]
    far = arrived[0][ends[0] - side : ends[0], :]
    for k, end, part in zip(distances[1:], ends[1:], arrived[1:]):
        far = jnp.where(distance == k, part[end - side : end, :], far)
    facing = got[got.shape[0] - 2 * side : got.shape[0] - side, :]
    coef[...] = jnp.zeros(coef.shape, F32)
    for j in range(3):
        at = slice(RADIUS * size_x + j * strip, RADIUS * size_x + (j + 1) * strip)
        coef[j, 0, 1 : strip + 1, :] = ahead(even, border, third_a[at, :], third_b[at, :])
        coef[j, depth + 1, 1 : strip + 1, :] = after(even, border, third_a[at, :], third_b[at, :])
        of = slice(j * depth, (j + 1) * depth)
        left = ahead(even_strip, end_strip, facing[of, :], far[of, :])
        right = after(even_strip, end_strip, facing[of, :], far[of, :])
        for z in range(depth):
            coef[j, z + 1, 1 : strip + 1, :] = kappa[j, z]
            coef[j, z + 1, 0:1, :] = left[z : z + 1, :]
            coef[j, z + 1, strip + 1 : strip + 2, :] = right[z : z + 1, :]


def smooth_body(total, got_a, got_b, kappa, coef, velocity, momentum, new_momentum, new_speed, grad, half):
    depth, strip, size_y = momentum.shape
    column = lax.axis_index("shot") * strip
    wide = strip + 4
    even = lax.rem(lax.axis_index("slab"), 2) == 0
    border = at_border()
    for k in range(2):
        at = slice(k * wide, (k + 1) * wide)
        grad[k, 0:wide, :] = ahead(even, border, got_a[at, :], got_b[at, :])
        grad[depth + 2 + k, 0:wide, :] = after(even, border, got_a[at, :], got_b[at, :])
    for z in range(depth):
        grad[z + 2, 0:wide, :] = total[z * wide : (z + 1) * wide, :]

    def step(source, z, rows, factors):
        centre = source[z, 1 : 1 + rows, :]
        lane = lax.broadcasted_iota(jnp.int32, centre.shape, 1)
        twice = 2.0 * centre
        along_z = source[z + 1, 1 : 1 + rows, :] - twice + source[z - 1, 1 : 1 + rows, :]
        along_x = source[z, 2 : 2 + rows, :] - twice + source[z, 0:rows, :]
        after = jnp.where(lane < size_y - 1, pltpu.roll(centre, size_y - 1, 1), 0.0)
        before = jnp.where(lane >= 1, pltpu.roll(centre, 1, 1), 0.0)
        along_y = after - twice + before
        return centre + factors[0] * along_z + factors[1] * along_x + factors[2] * along_y

    for z in range(depth + 2):
        half[z, 0 : strip + 2, :] = step(grad, z + 1, strip + 2, [coef[j, z, 0 : strip + 2, :] for j in range(3)])
    for z in range(depth):
        smoothed = step(half, z + 1, strip, [kappa[j, z] for j in range(3)])
        fresh = 0.9 * momentum[z] + smoothed
        new_momentum[z] = fresh
        new_speed[z] = velocity[z, pl.ds(column, strip), :] - 0.02 * fresh


def on_device(
    velocity,
    wave_state,
    source_cells,
    source_codes,
    wavelets,
    receiver_cells,
    residuals,
    momentum,
    diffusivity,
):
    depth, size_x, size_y = velocity.shape
    strip = momentum.shape[1]
    wide = strip + 4
    slabs = lax.axis_size("slab")
    shots = lax.axis_size("shot")
    chips = shots // 2
    z_even, z_odd = even_pairs(slabs), odd_slabs(shots, slabs)
    both = ("shot", "slab")
    cube = (depth, size_x, size_y)
    padded = (depth, size_x + 2 * PAD, size_y)
    dma = pltpu.SemaphoreType.DMA

    half = RADIUS // 2
    block = shape(2 * RADIUS + half, size_x, size_y)
    out_b, out_a = call(
        pack_body, [block] * 2, tuple(pltpu.with_memory_space_constraint(x, pltpu.HBM) for x in (wave_state, velocity)), ["hbm"] * 2, ["vmem"] * 2, [dma((2 * (2 * RADIUS + half),))], us=1.3
    )
    first_b = lax.ppermute(out_b, both, z_odd)
    first_a = lax.ppermute(out_a, "slab", z_even)

    flat = shape(RADIUS * size_x, size_y)
    flat_q = shape(RADIUS * size_x + 3 * strip, size_y)
    edge = shape(RADIUS, size_x, size_y)
    ring = shape(2 * RADIUS, size_x, size_y)
    ring_scratch = pltpu.VMEM(ring.shape, F32)
    small = tuple(
        pltpu.with_memory_space_constraint(x, pltpu.HBM) for x in (source_cells, source_codes, wavelets.T)
    )
    small_scratch = [pltpu.SMEM(x.shape, x.dtype) for x in small] + [dma((3,))]
    partial_u, image0, partial_q, push_u, push, tap_u, weight, out_b, out_a, third_b, third_a = call(
        functools.partial(partial_body, scale=math.sqrt(shots * STEPS)),
        [shape(*cube)] * 5 + [ring, shape(*cube), flat, flat, flat_q, flat_q],
        (wave_state, velocity, receiver_cells, residuals, diffusivity, *small),
        ["vmem"] * 5 + ["hbm"] * 3,
        ["vmem"] * 11,
        [pltpu.VMEM(padded, F32)] * 2 + [pltpu.VMEM((STEPS, depth * size_x, size_y), F32)] + small_scratch,
        us=1.7,
    )
    second_b = lax.ppermute(out_b, both, z_odd)
    second_a = lax.ppermute(out_a, "slab", z_even)
    third_b = lax.ppermute(third_b, both, z_odd)
    third_a = lax.ppermute(third_a, "slab", z_even)

    (share_own,) = call(share_body, [edge], (first_a, first_b), ["vmem"] * 2, ["vmem"])
    share_got = lax.ppermute(share_own, "shot", even_pairs(shots))
    u_part, q_next, image_own, gain = call(
        near_body,
        [shape(*cube)] * 4,
        (wave_state, velocity, partial_u, image0, partial_q, push_u, weight, first_a, first_b),
        ["vmem"] * 9,
        ["vmem"] * 4,
        [ring_scratch] * 2 + [pltpu.VMEM(padded, F32)],
        us=0.8,
    )

    part = shape(chips, depth * wide, size_y)
    side = 3 * depth
    u_out, keep, send = call(
        image_body,
        [shape(*cube), part, shape(chips * depth * wide + 2 * side, size_y)],
        (velocity, diffusivity, u_part, image_own, gain, tap_u, share_own, share_got, second_b, second_a),
        ["vmem"] * 10,
        ["vmem"] * 3,
        [ring_scratch, pltpu.VMEM(padded, F32)],
        us=0.3,
    )
    got = lax.ppermute(send, "shot", even_pairs(shots))
    (fields,) = call(
        adjoint_body,
        [shape(1, 2, *cube)],
        (wave_state, velocity, u_out, q_next, push, share_own, share_got, third_b, third_a),
        ["vmem"] * 9,
        ["any"],
        [
            pltpu.VMEM((depth + 2 * RADIUS, size_x + 2 * PAD, size_y), F32),
            ring_scratch,
            ring_scratch,
            pltpu.VMEM(cube, F32),
            dma((2,)),
        ],
        us=1.4,
    )
    row_block = shape(depth * wide, size_y)
    sums = [shape(depth * wide + (side if hands_on(k) else 0), size_y) for k in range(chips)]
    parts = call(pair_sum_body, sums, (keep, got), ["vmem"] * 2, ["vmem"] * chips)
    arrived = [
        lax.ppermute(parts[k], "shot", [(i, i ^ (2 * k)) for i in range(shots)]) for k in reversed(range(1, chips))
    ] + [parts[0]]
    *arrived, fields = lax.optimization_barrier((*arrived, fields))
    two = shape(2 * wide, size_y)
    total, out_b, out_a = call(
        functools.partial(strip_sum_body, count=chips, wide=wide),
        [row_block, two, two],
        arrived,
        ["vmem"] * chips,
        ["vmem"] * 3,
    )
    grad_b = lax.ppermute(out_b, both, z_odd)
    grad_a = lax.ppermute(out_a, "slab", z_even)
    distances = [k for k in range(chips) if hands_on(k)]
    tall = 8 * ((wide + 7) // 8)
    (coef,) = call(
        functools.partial(coefficient_body, size_x=size_x, distances=distances),
        [shape(3, depth + 2, tall, size_y)],
        (diffusivity, third_b, third_a, got, *(arrived[chips - 1 - k] for k in distances)),
        ["vmem"] * (4 + len(distances)),
        ["vmem"],
        us=0.1,
    )
    new_momentum, new_velocity = call(
        smooth_body,
        [shape(*momentum.shape)] * 2,
        (total, grad_a, grad_b, diffusivity, coef, velocity, momentum),
        ["vmem"] * 7,
        ["block"] * 2,
        [pltpu.VMEM((depth + 4, tall, size_y), F32), pltpu.VMEM((depth + 2, tall, size_y), F32)],
        us=0.7,
    )
    return (fields, new_momentum, new_velocity)


def solution(mesh):
    return jax.shard_map(
        on_device,
        mesh=mesh,
        in_specs=(
            P("slab", None, None),
            P(None, "shot", None, "slab", None, None),
            P("shot", None),
            P("shot", None),
            P(),
            P("shot", None),
            P("shot", None, None),
            P("slab", "shot", None),
            P(None, "slab", "shot", None),
        ),
        out_specs=(
            P("shot", None, "slab", None, None),
            P("slab", "shot", None),
            P("slab", "shot", None),
        ),
        check_vma=False,
    )
```

```python
import functools
import math

import jax
import jax.numpy as jnp
from jax import lax
from jax.experimental import pallas as pl
from jax.experimental.pallas import tpu as pltpu
from jax.sharding import PartitionSpec as P

STENCIL_TAPS = (-205.0 / 72.0, 8.0 / 5.0, -1.0 / 5.0, 8.0 / 315.0, -1.0 / 560.0)
RADIUS = 4
PAD = 8
STEPS = 2
F32 = jnp.float32
BYTES_PER_US = 3.69e6


def even_pairs(count):
    return [(i, i ^ 1) for i in range(count)]


def odd_pairs(count):
    low = [(i, (i + 1) % count) for i in range(1, count, 2)]
    return low + [(b, a) for a, b in low]


def odd_slabs(shots, slabs):
    pairs = []
    for shot in range(shots):
        for slab in range(slabs):
            if slab == 0 or slab == slabs - 1:
                other = (shot ^ 1) * slabs + slab
            else:
                other = shot * slabs + (slab + 1 if slab % 2 else slab - 1)
            pairs.append((shot * slabs + slab, other))
    return pairs


def at_border():
    slab = lax.axis_index("slab")
    return (slab == 0) | (slab == lax.axis_size("slab") - 1)


def ahead(even, border, from_a, from_b):
    return jnp.where(even, jnp.where(border, 0.0, from_b), from_a)


def after(even, border, from_a, from_b):
    return jnp.where(even, from_a, jnp.where(border, 0.0, from_b))


def run_copies(pairs, sems):
    copies = [pltpu.make_async_copy(src, dst, sems.at[k]) for k, (src, dst) in enumerate(pairs)]
    for copy in copies:
        copy.start()
    return copies


SPECS = {
    "any": pl.BlockSpec(memory_space=pl.ANY),
    "hbm": pl.BlockSpec(memory_space=pltpu.HBM),
    "vmem": pl.BlockSpec(memory_space=pltpu.VMEM),
    "block": pl.BlockSpec(),
}


def call(body, out_shapes, operands, in_specs=None, out_specs=None, scratch=(), aliases=None, us=0.1):
    return pl.pallas_call(
        body,
        out_shape=list(out_shapes),
        in_specs=[SPECS[s] for s in in_specs],
        out_specs=[SPECS[s] for s in out_specs],
        scratch_shapes=list(scratch),
        input_output_aliases=aliases or {},
        cost_estimate=pl.CostEstimate(flops=0, bytes_accessed=int(us * BYTES_PER_US), transcendentals=0),
        compiler_params=pltpu.CompilerParams(vmem_limit_bytes=16 * 1024 * 1024),
    )(*operands)


def shape(*dims):
    return jax.ShapeDtypeStruct(dims, F32)


def y_sums(centre, lane, size_y):
    sums = []
    for r in range(1, RADIUS + 1):
        before = jnp.where(lane >= r, pltpu.roll(centre, r, 1), 0.0)
        after = jnp.where(lane < size_y - r, pltpu.roll(centre, size_y - r, 1), 0.0)
        sums.append(before + after)
    return sums


def laplacian_row(field, z, rows, size_x, size_y, lane):
    centre = field[z, PAD : PAD + size_x, :]
    along_y = y_sums(centre, lane, size_y)
    total = (3.0 * STENCIL_TAPS[0]) * centre
    for r in range(1, RADIUS + 1):
        ring = along_y[r - 1]
        ring = ring + (field[z, PAD + r : PAD + r + size_x, :] + field[z, PAD - r : PAD - r + size_x, :])
        if z + r < rows:
            ring = ring + field[z + r, PAD : PAD + size_x, :]
        if z - r >= 0:
            ring = ring + field[z - r, PAD : PAD + size_x, :]
        total = total + STENCIL_TAPS[r] * ring
    return total


def clear_sides(field, size_x):
    rows, _, size_y = field.shape
    edge = jnp.zeros((rows, PAD, size_y), F32)
    field[:, 0:PAD, :] = edge
    field[:, PAD + size_x : PAD + size_x + PAD, :] = edge


def pack_body(state, velocity, out_b, out_a, sems):
    depth = velocity.shape[0]
    half = RADIUS // 2
    even = lax.rem(lax.axis_index("slab"), 2) == 0
    share = lax.rem(lax.axis_index("shot"), 2) * half
    at_a = jnp.where(even, depth - RADIUS, 0)
    at_b = jnp.where(even, 0, depth - RADIUS)
    pairs = []
    for out, at in ((out_a, at_a), (out_b, at_b)):
        for k in range(RADIUS):
            pairs.append((state.at[1, 0, 0, at + k], out.at[k]))
            pairs.append((state.at[1, 0, 1, at + k], out.at[RADIUS + k]))
        for k in range(half):
            pairs.append((velocity.at[at + share + k], out.at[2 * RADIUS + k]))
    for copy in run_copies(pairs, sems):
        copy.wait()


def point_cells(cells, codes, wavelets, moment, first, size_x, size_y, act):
    plane = size_x * size_y
    row_lane = lax.broadcasted_iota(jnp.int32, (1, size_y), 1)
    for k in range(cells.shape[1]):
        cell = cells[0, k]
        amount = wavelets[moment, codes[0, k]]
        z = lax.div(cell, plane) - first
        rest = lax.rem(cell, plane)
        x = lax.div(rest, size_y)
        y = lax.rem(rest, size_y)
        act(z, x, jnp.where(row_lane == y, amount, 0.0))


def weighted(terms):
    total = None
    for r, value in terms:
        term = STENCIL_TAPS[r] * value
        total = term if total is None else total + term
    return total


def partial_body(
    state, velocity, cells, residuals, kappa, source_cells, source_codes, wavelets,
    partial_u, image, partial_q, push_u, push, tap_u, weight, out_b, out_a, third_b, third_a, far,
    field_u, field_q, grid_now, cells_here, codes_here, wavelets_here, sems, *, scale,
):
    small = [(source_cells, cells_here), (source_codes, codes_here), (wavelets, wavelets_here)]
    copies = run_copies(small, sems)
    depth, size_x, size_y = velocity.shape
    strip = kappa.shape[2]
    even = lax.rem(lax.axis_index("slab"), 2) == 0
    core = lax.rem(lax.axis_index("shot"), 2)
    for j in range(3):
        far[j * depth : (j + 1) * depth, :] = jnp.where(core == 0, kappa[j, :, 0, :], kappa[j, :, strip - 1, :])
        tail = kappa[j, depth - 1]
        head = kappa[j, 0]
        at = RADIUS * size_x + j * strip
        third_a[at : at + strip, :] = jnp.where(even, tail, head)
        third_b[at : at + strip, :] = jnp.where(even, head, tail)
    for which, field in ((0, field_u), (1, field_q)):
        clear_sides(field, size_x)
        for z in range(depth):
            field[z, PAD : PAD + size_x, :] = state[1, 0, which, z]

    volume = depth * size_x * size_y
    count = cells.shape[1]
    ids = cells[...] - lax.axis_index("slab") * volume
    inside = (ids >= 0) & (ids < volume)
    kept = jnp.where(inside, ids, 0)
    row = lax.div(kept, jnp.int32(size_y))
    column = kept - row * size_y
    rows = depth * size_x
    pick_row = (lax.broadcasted_iota(jnp.int32, (rows, count), 0) == row).astype(F32)
    pick_column = lax.broadcasted_iota(jnp.int32, (size_y, count), 0) == column
    for moment in range(STEPS):
        amounts = jnp.where(inside, residuals[0, moment : moment + 1, :], 0.0)
        grid_now[moment] = lax.dot_general(
            pick_row,
            jnp.where(pick_column, amounts, 0.0),
            (((1,), (1,)), ((), ())),
            precision=lax.Precision.HIGHEST,
            preferred_element_type=F32,
        )

    lane = lax.broadcasted_iota(jnp.int32, (size_x, size_y), 1)
    for z in range(depth):
        at = slice(z * size_x, (z + 1) * size_x)
        v = velocity[z]
        vv = v * v
        drive = vv * laplacian_row(field_u, z, depth, size_x, size_y, lane)
        partial_u[z] = (2.0 * state[1, 0, 0, z] - state[0, 0, 0, z]) + drive
        image[z] = drive * state[1, 0, 1, z]
        drive = vv * (laplacian_row(field_q, z, depth, size_x, size_y, lane) + grid_now[0, at, :])
        partial_q[z] = (2.0 * state[1, 0, 1, z] - state[0, 0, 1, z]) + drive
        push[z] = vv * grid_now[1, at, :]
        weight[z] = -0.2 / (v * scale)
        push_u[z] = jnp.zeros((size_x, size_y), F32)

    def inject(z, x, spot):
        @pl.when((z >= 0) & (z < depth))
        def _():
            at = (z, pl.ds(x, 1), slice(None))
            v = velocity[at]
            change = (v * v) * spot
            partial_u[at] = partial_u[at] + change
            image[at] = image[at] + change * state[1, 0, 1, z, pl.ds(x, 1), :]

    def inject_next(z, x, spot):
        @pl.when((z >= 0) & (z < depth))
        def _():
            at = (z, pl.ds(x, 1), slice(None))
            v = velocity[at]
            push_u[at] = push_u[at] + (v * v) * spot

    for copy in copies:
        copy.wait()
    first_layer = lax.axis_index("slab") * depth
    point_cells(cells_here, codes_here, wavelets_here, 0, first_layer, size_x, size_y, inject)
    point_cells(cells_here, codes_here, wavelets_here, 1, first_layer, size_x, size_y, inject_next)
    for k in range(2 * RADIUS):
        tap_u[k] = weighted([(r, state[1, 0, 0, own]) for r, own in halo_near(k, depth)])
    for source, to_a, to_b in ((partial_u, out_a, out_b), (partial_q, third_a, third_b)):
        for k in range(RADIUS):
            tail = source[depth - RADIUS + k]
            head = source[k]
            to_a[k * size_x : (k + 1) * size_x, :] = jnp.where(even, tail, head)
            to_b[k * size_x : (k + 1) * size_x, :] = jnp.where(even, head, tail)


def share_body(first_a, first_b, share):
    half = RADIUS // 2
    for k in range(half):
        share[k] = first_a[2 * RADIUS + k]
        share[half + k] = first_b[2 * RADIUS + k]


def halo_speed(k, share_own, share_got):
    half = RADIUS // 2
    row = k % RADIUS
    even = lax.rem(lax.axis_index("slab"), 2) == 0
    border = at_border()
    own = lax.rem(lax.axis_index("shot"), 2) == row // half
    at_a = jnp.where(own, share_own[row % half], share_got[row % half])
    at_b = jnp.where(own, share_own[half + row % half], share_got[half + row % half])
    return (ahead if k < RADIUS else after)(even, border, at_a, at_b)


def halo_near(k, depth):
    if k < RADIUS:
        return [(r, k - RADIUS + r) for r in range(1, RADIUS + 1) if k - RADIUS + r >= 0]
    row = k - RADIUS
    return [(r, depth + row - r) for r in range(1, RADIUS + 1) if depth + row - r < depth]


def own_near(z, depth):
    near = [(r, RADIUS + z - r) for r in range(1, RADIUS + 1) if z - r < 0]
    return near + [(r, RADIUS + z + r - depth) for r in range(1, RADIUS + 1) if z + r >= depth]


def near_body(
    state, velocity, partial_u, image0, partial_q, push, weight, first_a, first_b,
    u_part, q_next, image, gain, u_edge, q_edge, u_now,
):
    depth, size_x, size_y = velocity.shape
    even = lax.rem(lax.axis_index("slab"), 2) == 0
    border = at_border()
    middle = slice(PAD, PAD + size_x)
    clear_sides(u_now, size_x)
    for k in range(2 * RADIUS):
        row = k % RADIUS
        pick = ahead if k < RADIUS else after
        u_edge[k] = pick(even, border, first_a[row], first_b[row])
        q_edge[k] = pick(even, border, first_a[RADIUS + row], first_b[RADIUS + row])
    for z in range(depth):
        near = own_near(z, depth)
        if not near:
            u_now[z, middle, :] = partial_u[z]
            q_next[z] = partial_q[z]
            image[z] = image0[z]
            continue
        v = velocity[z]
        vv = v * v
        change = vv * weighted([(r, u_edge[k]) for r, k in near])
        u_now[z, middle, :] = partial_u[z] + change
        image[z] = image0[z] + change * state[1, 0, 1, z]
        q_next[z] = partial_q[z] + vv * weighted([(r, q_edge[k]) for r, k in near])

    lane = lax.broadcasted_iota(jnp.int32, (size_x, size_y), 1)
    for z in range(depth):
        v = velocity[z]
        vv = v * v
        adjoint = q_next[z]
        drive = vv * laplacian_row(u_now, z, depth, size_x, size_y, lane) + push[z]
        u_part[z] = (2.0 * u_now[z, middle, :] - state[1, 0, 0, z]) + drive
        image[z] = weight[z] * (image[z] + drive * adjoint)
        gain[z] = (weight[z] * vv) * adjoint


def halo_field(halo, second_b, second_a, tap, share_own, share_got):
    size_x = halo.shape[1]
    even = lax.rem(lax.axis_index("slab"), 2) == 0
    border = at_border()
    for k in range(2 * RADIUS):
        row = k % RADIUS
        rows = slice(row * size_x, (row + 1) * size_x)
        pick = ahead if k < RADIUS else after
        v = halo_speed(k, share_own, share_got)
        halo[k] = pick(even, border, second_a[rows, :], second_b[rows, :]) + (v * v) * tap[k]


def image_body(
    velocity, kappa, u_part, image_own, gain, tap_u, share_own, share_got, second_b, second_a,
    u_out, keep, packed, halo, image,
):
    depth, size_x, size_y = velocity.shape
    core = lax.rem(lax.axis_index("shot"), 2)
    middle = slice(PAD, PAD + size_x)
    clear_sides(image, size_x)
    halo_field(halo, second_b, second_a, tap_u, share_own, share_got)
    for z in range(depth):
        near = own_near(z, depth)
        if not near:
            u_out[z] = u_part[z]
            image[z, middle, :] = image_own[z]
            continue
        v = velocity[z]
        crossing = weighted([(r, halo[k]) for r, k in near])
        u_out[z] = u_part[z] + (v * v) * crossing
        image[z, middle, :] = image_own[z] + gain[z] * crossing
    chip = lax.div(lax.axis_index("shot"), 2)
    chips = keep.shape[0]
    strip = size_x // (2 * chips)
    wide = strip + 4
    rows = depth * wide
    for m in range(chips):
        to = jnp.bitwise_xor(chip, m)
        for z in range(depth):
            at = PAD + 2 * m * strip - 2
            low = image[z, at : at + wide, :]
            high = image[z, at + strip : at + strip + wide, :]
            keep[to, z * wide : (z + 1) * wide, :] = jnp.where(core == 0, low, high)
            packed[pl.ds(to * rows + z * wide, wide), :] = jnp.where(core == 0, high, low)
    for j in range(3):
        at = chips * rows + j * depth
        packed[at : at + depth, :] = jnp.where(core == 0, kappa[j, :, strip - 1, :], kappa[j, :, 0, :])


def pair_sum_body(keep, got, *outs):
    rows = keep.shape[1]
    for k, out in enumerate(outs):
        out[...] = keep[k] + got[k * rows : (k + 1) * rows, :]


def strip_sum_body(*refs, count, wide):
    parts, (total, edge_b, edge_a) = refs[:count], refs[count:]
    rows = total.shape[0]
    added = parts[0][...]
    for part in parts[1:]:
        added = added + part[...]
    total[...] = added
    even = lax.rem(lax.axis_index("slab"), 2) == 0
    head = total[0 : 2 * wide, :]
    tail = total[rows - 2 * wide : rows, :]
    edge_a[...] = jnp.where(even, tail, head)
    edge_b[...] = jnp.where(even, head, tail)


def adjoint_body(
    state, velocity, u_out, q_next, push, share_own, share_got, third_a, third_b, fields, field, tap, halo, q_out, sems
):
    copy_u = pltpu.make_async_copy(u_out, fields.at[0, 0], sems.at[0])
    copy_u.start()
    depth, size_x, size_y = velocity.shape
    whole = depth + 2 * RADIUS
    middle = slice(PAD, PAD + size_x)
    clear_sides(field, size_x)
    for k in range(2 * RADIUS):
        tap[k] = weighted([(r, state[1, 0, 1, own]) for r, own in halo_near(k, depth)])
    halo_field(halo, third_b, third_a, tap, share_own, share_got)
    for z in range(whole):
        inner = RADIUS <= z < RADIUS + depth
        field[z, middle, :] = q_next[z - RADIUS] if inner else halo[z if z < RADIUS else z - depth]
    lane = lax.broadcasted_iota(jnp.int32, (size_x, size_y), 1)
    for z in range(depth):
        v = velocity[z]
        drive = (v * v) * laplacian_row(field, z + RADIUS, whole, size_x, size_y, lane) + push[z]
        q_out[z] = (2.0 * q_next[z] - state[1, 0, 1, z]) + drive
    copy_q = pltpu.make_async_copy(q_out, fields.at[0, 1], sems.at[1])
    copy_q.start()
    copy_u.wait()
    copy_q.wait()


def coefficient_body(kappa, third_b, third_a, got, far, coef, *, size_x):
    _, depth, strip, _ = kappa.shape
    even = lax.rem(lax.axis_index("slab"), 2) == 0
    border = at_border()
    shot = lax.axis_index("shot")
    even_strip = lax.rem(shot, 2) == 0
    end_strip = (shot == 0) | (shot == lax.axis_size("shot") - 1)
    facing = got[got.shape[0] - 3 * depth : got.shape[0], :]
    coef[...] = jnp.zeros(coef.shape, F32)
    for j in range(3):
        at = slice(RADIUS * size_x + j * strip, RADIUS * size_x + (j + 1) * strip)
        coef[j, 0, 1 : strip + 1, :] = ahead(even, border, third_a[at, :], third_b[at, :])
        coef[j, depth + 1, 1 : strip + 1, :] = after(even, border, third_a[at, :], third_b[at, :])
        of = slice(j * depth, (j + 1) * depth)
        left = ahead(even_strip, end_strip, facing[of, :], far[of, :])
        right = after(even_strip, end_strip, facing[of, :], far[of, :])
        for z in range(depth):
            coef[j, z + 1, 1 : strip + 1, :] = kappa[j, z]
            coef[j, z + 1, 0:1, :] = left[z : z + 1, :]
            coef[j, z + 1, strip + 1 : strip + 2, :] = right[z : z + 1, :]


def smooth_body(total, got_a, got_b, kappa, coef, velocity, momentum, new_momentum, new_speed, grad, half):
    depth, strip, size_y = momentum.shape
    column = lax.axis_index("shot") * strip
    wide = strip + 4
    even = lax.rem(lax.axis_index("slab"), 2) == 0
    border = at_border()
    for k in range(2):
        at = slice(k * wide, (k + 1) * wide)
        grad[k, 0:wide, :] = ahead(even, border, got_a[at, :], got_b[at, :])
        grad[depth + 2 + k, 0:wide, :] = after(even, border, got_a[at, :], got_b[at, :])
    for z in range(depth):
        grad[z + 2, 0:wide, :] = total[z * wide : (z + 1) * wide, :]

    def step(source, z, rows, factors):
        centre = source[z, 1 : 1 + rows, :]
        lane = lax.broadcasted_iota(jnp.int32, centre.shape, 1)
        twice = 2.0 * centre
        along_z = source[z + 1, 1 : 1 + rows, :] - twice + source[z - 1, 1 : 1 + rows, :]
        along_x = source[z, 2 : 2 + rows, :] - twice + source[z, 0:rows, :]
        after = jnp.where(lane < size_y - 1, pltpu.roll(centre, size_y - 1, 1), 0.0)
        before = jnp.where(lane >= 1, pltpu.roll(centre, 1, 1), 0.0)
        along_y = after - twice + before
        return centre + factors[0] * along_z + factors[1] * along_x + factors[2] * along_y

    for z in range(depth + 2):
        half[z, 0 : strip + 2, :] = step(grad, z + 1, strip + 2, [coef[j, z, 0 : strip + 2, :] for j in range(3)])
    for z in range(depth):
        smoothed = step(half, z + 1, strip, [kappa[j, z] for j in range(3)])
        fresh = 0.9 * momentum[z] + smoothed
        new_momentum[z] = fresh
        new_speed[z] = velocity[z, pl.ds(column, strip), :] - 0.02 * fresh


def on_device(
    velocity,
    wave_state,
    source_cells,
    source_codes,
    wavelets,
    receiver_cells,
    residuals,
    momentum,
    diffusivity,
):
    depth, size_x, size_y = velocity.shape
    strip = momentum.shape[1]
    wide = strip + 4
    slabs = lax.axis_size("slab")
    shots = lax.axis_size("shot")
    chips = shots // 2
    z_even, z_odd = even_pairs(slabs), odd_slabs(shots, slabs)
    both = ("shot", "slab")
    cube = (depth, size_x, size_y)
    padded = (depth, size_x + 2 * PAD, size_y)
    dma = pltpu.SemaphoreType.DMA

    half = RADIUS // 2
    block = shape(2 * RADIUS + half, size_x, size_y)
    out_b, out_a = call(
        pack_body, [block] * 2, tuple(pltpu.with_memory_space_constraint(x, pltpu.HBM) for x in (wave_state, velocity)), ["hbm"] * 2, ["vmem"] * 2, [dma((2 * (2 * RADIUS + half),))], us=1.3
    )
    first_b = lax.ppermute(out_b, both, z_odd)
    first_a = lax.ppermute(out_a, "slab", z_even)

    flat = shape(RADIUS * size_x, size_y)
    flat_q = shape(RADIUS * size_x + 3 * strip, size_y)
    edge = shape(RADIUS, size_x, size_y)
    ring = shape(2 * RADIUS, size_x, size_y)
    ring_scratch = pltpu.VMEM(ring.shape, F32)
    small = tuple(
        pltpu.with_memory_space_constraint(x, pltpu.HBM) for x in (source_cells, source_codes, wavelets.T)
    )
    small_scratch = [pltpu.SMEM(x.shape, x.dtype) for x in small] + [dma((3,))]
    partial_u, image0, partial_q, push_u, push, tap_u, weight, out_b, out_a, third_b, third_a, far = call(
        functools.partial(partial_body, scale=math.sqrt(shots * STEPS)),
        [shape(*cube)] * 5 + [ring, shape(*cube), flat, flat, flat_q, flat_q, shape(3 * depth, size_y)],
        (wave_state, velocity, receiver_cells, residuals, diffusivity, *small),
        ["vmem"] * 5 + ["hbm"] * 3,
        ["vmem"] * 12,
        [pltpu.VMEM(padded, F32)] * 2 + [pltpu.VMEM((STEPS, depth * size_x, size_y), F32)] + small_scratch,
        us=1.7,
    )
    second_b = lax.ppermute(out_b, both, z_odd)
    second_a = lax.ppermute(out_a, "slab", z_even)
    third_b = lax.ppermute(third_b, both, z_odd)
    third_a = lax.ppermute(third_a, "slab", z_even)

    far = lax.ppermute(far, "shot", odd_pairs(shots))
    first_a, first_b, far = lax.optimization_barrier((first_a, first_b, far))
    (share_own,) = call(share_body, [edge], (first_a, first_b), ["vmem"] * 2, ["vmem"])
    share_got = lax.ppermute(share_own, "shot", even_pairs(shots))
    u_part, q_next, image_own, gain = call(
        near_body,
        [shape(*cube)] * 4,
        (wave_state, velocity, partial_u, image0, partial_q, push_u, weight, first_a, first_b),
        ["vmem"] * 9,
        ["vmem"] * 4,
        [ring_scratch] * 2 + [pltpu.VMEM(padded, F32)],
        us=0.8,
    )

    part = shape(chips, depth * wide, size_y)
    side = 3 * depth
    u_out, keep, send = call(
        image_body,
        [shape(*cube), part, shape(chips * depth * wide + side, size_y)],
        (velocity, diffusivity, u_part, image_own, gain, tap_u, share_own, share_got, second_b, second_a),
        ["vmem"] * 10,
        ["vmem"] * 3,
        [ring_scratch, pltpu.VMEM(padded, F32)],
        us=0.3,
    )
    got = lax.ppermute(send, "shot", even_pairs(shots))
    (fields,) = call(
        adjoint_body,
        [shape(1, 2, *cube)],
        (wave_state, velocity, u_out, q_next, push, share_own, share_got, third_a, third_b),
        ["vmem"] * 9,
        ["any"],
        [
            pltpu.VMEM((depth + 2 * RADIUS, size_x + 2 * PAD, size_y), F32),
            ring_scratch,
            ring_scratch,
            pltpu.VMEM(cube, F32),
            dma((2,)),
        ],
        us=1.4,
    )
    row_block = shape(depth * wide, size_y)
    parts = call(pair_sum_body, [row_block] * chips, (keep, got), ["vmem"] * 2, ["vmem"] * chips)
    arrived = [
        lax.ppermute(parts[k], "shot", [(i, i ^ (2 * k)) for i in range(shots)]) for k in reversed(range(1, chips))
    ] + [parts[0]]
    *arrived, fields = lax.optimization_barrier((*arrived, fields))
    two = shape(2 * wide, size_y)
    total, out_b, out_a = call(
        functools.partial(strip_sum_body, count=chips, wide=wide),
        [row_block, two, two],
        arrived,
        ["vmem"] * chips,
        ["vmem"] * 3,
    )
    grad_b = lax.ppermute(out_b, both, z_odd)
    grad_a = lax.ppermute(out_a, "slab", z_even)
    tall = 8 * ((wide + 7) // 8)
    (coef,) = call(
        functools.partial(coefficient_body, size_x=size_x),
        [shape(3, depth + 2, tall, size_y)],
        (diffusivity, third_b, third_a, got, far),
        ["vmem"] * 5,
        ["vmem"],
        us=0.1,
    )
    new_momentum, new_velocity = call(
        smooth_body,
        [shape(*momentum.shape)] * 2,
        (total, grad_a, grad_b, diffusivity, coef, velocity, momentum),
        ["vmem"] * 7,
        ["block"] * 2,
        [pltpu.VMEM((depth + 4, tall, size_y), F32), pltpu.VMEM((depth + 2, tall, size_y), F32)],
        us=0.7,
    )
    return (fields, new_momentum, new_velocity)


def solution(mesh):
    return jax.shard_map(
        on_device,
        mesh=mesh,
        in_specs=(
            P("slab", None, None),
            P(None, "shot", None, "slab", None, None),
            P("shot", None),
            P("shot", None),
            P(),
            P("shot", None),
            P("shot", None, None),
            P("slab", "shot", None),
            P(None, "slab", "shot", None),
        ),
        out_specs=(
            P("shot", None, "slab", None, None),
            P("slab", "shot", None),
            P("slab", "shot", None),
        ),
        check_vma=False,
    )
```

```python
import functools
import math

import jax
import jax.numpy as jnp
from jax import lax
from jax.experimental import pallas as pl
from jax.experimental.pallas import tpu as pltpu
from jax.sharding import PartitionSpec as P

STENCIL_TAPS = (-205.0 / 72.0, 8.0 / 5.0, -1.0 / 5.0, 8.0 / 315.0, -1.0 / 560.0)
RADIUS = 4
PAD = 8
STEPS = 2
F32 = jnp.float32
BYTES_PER_US = 3.69e6


def even_pairs(count):
    return [(i, i ^ 1) for i in range(count)]


def odd_pairs(count):
    low = [(i, (i + 1) % count) for i in range(1, count, 2)]
    return low + [(b, a) for a, b in low]


def odd_slabs(shots, slabs):
    pairs = []
    for shot in range(shots):
        for slab in range(slabs):
            if slab == 0 or slab == slabs - 1:
                other = (shot ^ 1) * slabs + slab
            else:
                other = shot * slabs + (slab + 1 if slab % 2 else slab - 1)
            pairs.append((shot * slabs + slab, other))
    return pairs


def at_border():
    slab = lax.axis_index("slab")
    return (slab == 0) | (slab == lax.axis_size("slab") - 1)


def ahead(even, border, from_a, from_b):
    return jnp.where(even, jnp.where(border, 0.0, from_b), from_a)


def after(even, border, from_a, from_b):
    return jnp.where(even, from_a, jnp.where(border, 0.0, from_b))


def run_copies(pairs, sems):
    copies = [pltpu.make_async_copy(src, dst, sems.at[k]) for k, (src, dst) in enumerate(pairs)]
    for copy in copies:
        copy.start()
    return copies


SPECS = {
    "any": pl.BlockSpec(memory_space=pl.ANY),
    "hbm": pl.BlockSpec(memory_space=pltpu.HBM),
    "vmem": pl.BlockSpec(memory_space=pltpu.VMEM),
    "block": pl.BlockSpec(),
}


def call(body, out_shapes, operands, in_specs=None, out_specs=None, scratch=(), aliases=None, us=0.1):
    return pl.pallas_call(
        body,
        out_shape=list(out_shapes),
        in_specs=[SPECS[s] for s in in_specs],
        out_specs=[SPECS[s] for s in out_specs],
        scratch_shapes=list(scratch),
        input_output_aliases=aliases or {},
        cost_estimate=pl.CostEstimate(flops=0, bytes_accessed=int(us * BYTES_PER_US), transcendentals=0),
        compiler_params=pltpu.CompilerParams(vmem_limit_bytes=16 * 1024 * 1024),
    )(*operands)


def shape(*dims):
    return jax.ShapeDtypeStruct(dims, F32)


def y_sums(centre, lane, size_y):
    sums = []
    for r in range(1, RADIUS + 1):
        before = jnp.where(lane >= r, pltpu.roll(centre, r, 1), 0.0)
        after = jnp.where(lane < size_y - r, pltpu.roll(centre, size_y - r, 1), 0.0)
        sums.append(before + after)
    return sums


def laplacian_row(field, z, rows, size_x, size_y, lane):
    centre = field[z, PAD : PAD + size_x, :]
    along_y = y_sums(centre, lane, size_y)
    total = (3.0 * STENCIL_TAPS[0]) * centre
    for r in range(1, RADIUS + 1):
        ring = along_y[r - 1]
        ring = ring + (field[z, PAD + r : PAD + r + size_x, :] + field[z, PAD - r : PAD - r + size_x, :])
        if z + r < rows:
            ring = ring + field[z + r, PAD : PAD + size_x, :]
        if z - r >= 0:
            ring = ring + field[z - r, PAD : PAD + size_x, :]
        total = total + STENCIL_TAPS[r] * ring
    return total


def clear_sides(field, size_x):
    rows, _, size_y = field.shape
    edge = jnp.zeros((rows, PAD, size_y), F32)
    field[:, 0:PAD, :] = edge
    field[:, PAD + size_x : PAD + size_x + PAD, :] = edge


def pack_body(state, velocity, out_b, out_a, sems):
    depth = velocity.shape[0]
    half = RADIUS // 2
    even = lax.rem(lax.axis_index("slab"), 2) == 0
    share = lax.rem(lax.axis_index("shot"), 2) * half
    at_a = jnp.where(even, depth - RADIUS, 0)
    at_b = jnp.where(even, 0, depth - RADIUS)
    pairs = []
    for out, at in ((out_a, at_a), (out_b, at_b)):
        for k in range(RADIUS):
            pairs.append((state.at[1, 0, 0, at + k], out.at[k]))
            pairs.append((state.at[1, 0, 1, at + k], out.at[RADIUS + k]))
        for k in range(half):
            pairs.append((velocity.at[at + share + k], out.at[2 * RADIUS + k]))
    for copy in run_copies(pairs, sems):
        copy.wait()


def point_cells(cells, codes, wavelets, moment, first, size_x, size_y, act):
    plane = size_x * size_y
    row_lane = lax.broadcasted_iota(jnp.int32, (1, size_y), 1)
    for k in range(cells.shape[1]):
        cell = cells[0, k]
        amount = wavelets[moment, codes[0, k]]
        z = lax.div(cell, plane) - first
        rest = lax.rem(cell, plane)
        x = lax.div(rest, size_y)
        y = lax.rem(rest, size_y)
        act(z, x, jnp.where(row_lane == y, amount, 0.0))


def weighted(terms):
    total = None
    for r, value in terms:
        term = STENCIL_TAPS[r] * value
        total = term if total is None else total + term
    return total


def partial_u_body(
    state, velocity, source_cells, source_codes, wavelets,
    partial_u, image, tap_u, out_b, out_a,
    field, cells_here, codes_here, wavelets_here, sems,
):
    small = [(source_cells, cells_here), (source_codes, codes_here), (wavelets, wavelets_here)]
    copies = run_copies(small, sems)
    depth, size_x, size_y = velocity.shape
    even = lax.rem(lax.axis_index("slab"), 2) == 0
    clear_sides(field, size_x)
    for z in range(depth):
        field[z, PAD : PAD + size_x, :] = state[1, 0, 0, z]
    lane = lax.broadcasted_iota(jnp.int32, (size_x, size_y), 1)
    for z in range(depth):
        v = velocity[z]
        drive = (v * v) * laplacian_row(field, z, depth, size_x, size_y, lane)
        partial_u[z] = (2.0 * state[1, 0, 0, z] - state[0, 0, 0, z]) + drive
        image[z] = drive * state[1, 0, 1, z]
    for k in range(2 * RADIUS):
        tap_u[k] = weighted([(r, state[1, 0, 0, own]) for r, own in halo_near(k, depth)])

    def inject(z, x, spot):
        @pl.when((z >= 0) & (z < depth))
        def _():
            at = (z, pl.ds(x, 1), slice(None))
            v = velocity[at]
            change = (v * v) * spot
            partial_u[at] = partial_u[at] + change
            image[at] = image[at] + change * state[1, 0, 1, z, pl.ds(x, 1), :]

    for copy in copies:
        copy.wait()
    first_layer = lax.axis_index("slab") * depth
    point_cells(cells_here, codes_here, wavelets_here, 0, first_layer, size_x, size_y, inject)
    for k in range(RADIUS):
        tail = partial_u[depth - RADIUS + k]
        head = partial_u[k]
        out_a[k * size_x : (k + 1) * size_x, :] = jnp.where(even, tail, head)
        out_b[k * size_x : (k + 1) * size_x, :] = jnp.where(even, head, tail)


def partial_q_body(
    state, velocity, cells, residuals, kappa, source_cells, source_codes, wavelets,
    partial_q, push_u, push, weight, third_b, third_a, far,
    field, grid_now, cells_here, codes_here, wavelets_here, sems, *, scale,
):
    small = [(source_cells, cells_here), (source_codes, codes_here), (wavelets, wavelets_here)]
    copies = run_copies(small, sems)
    depth, size_x, size_y = velocity.shape
    strip = kappa.shape[2]
    even = lax.rem(lax.axis_index("slab"), 2) == 0
    core = lax.rem(lax.axis_index("shot"), 2)
    for j in range(3):
        far[j * depth : (j + 1) * depth, :] = jnp.where(core == 0, kappa[j, :, 0, :], kappa[j, :, strip - 1, :])
        tail = kappa[j, depth - 1]
        head = kappa[j, 0]
        at = RADIUS * size_x + j * strip
        third_a[at : at + strip, :] = jnp.where(even, tail, head)
        third_b[at : at + strip, :] = jnp.where(even, head, tail)
    clear_sides(field, size_x)
    for z in range(depth):
        field[z, PAD : PAD + size_x, :] = state[1, 0, 1, z]

    volume = depth * size_x * size_y
    count = cells.shape[1]
    ids = cells[...] - lax.axis_index("slab") * volume
    inside = (ids >= 0) & (ids < volume)
    kept = jnp.where(inside, ids, 0)
    row = lax.div(kept, jnp.int32(size_y))
    column = kept - row * size_y
    rows = depth * size_x
    pick_row = (lax.broadcasted_iota(jnp.int32, (rows, count), 0) == row).astype(F32)
    pick_column = lax.broadcasted_iota(jnp.int32, (size_y, count), 0) == column
    for moment in range(STEPS):
        amounts = jnp.where(inside, residuals[0, moment : moment + 1, :], 0.0)
        grid_now[moment] = lax.dot_general(
            pick_row,
            jnp.where(pick_column, amounts, 0.0),
            (((1,), (1,)), ((), ())),
            precision=lax.Precision.HIGHEST,
            preferred_element_type=F32,
        )

    lane = lax.broadcasted_iota(jnp.int32, (size_x, size_y), 1)
    for z in range(depth):
        at = slice(z * size_x, (z + 1) * size_x)
        v = velocity[z]
        vv = v * v
        drive = vv * (laplacian_row(field, z, depth, size_x, size_y, lane) + grid_now[0, at, :])
        partial_q[z] = (2.0 * state[1, 0, 1, z] - state[0, 0, 1, z]) + drive
        push[z] = vv * grid_now[1, at, :]
        weight[z] = -0.2 / (v * scale)
        push_u[z] = jnp.zeros((size_x, size_y), F32)

    def inject(z, x, spot):
        @pl.when((z >= 0) & (z < depth))
        def _():
            at = (z, pl.ds(x, 1), slice(None))
            v = velocity[at]
            push_u[at] = push_u[at] + (v * v) * spot

    for copy in copies:
        copy.wait()
    first_layer = lax.axis_index("slab") * depth
    point_cells(cells_here, codes_here, wavelets_here, 1, first_layer, size_x, size_y, inject)
    for k in range(RADIUS):
        tail = partial_q[depth - RADIUS + k]
        head = partial_q[k]
        third_a[k * size_x : (k + 1) * size_x, :] = jnp.where(even, tail, head)
        third_b[k * size_x : (k + 1) * size_x, :] = jnp.where(even, head, tail)


def share_body(first_a, first_b, share):
    half = RADIUS // 2
    for k in range(half):
        share[k] = first_a[2 * RADIUS + k]
        share[half + k] = first_b[2 * RADIUS + k]


def halo_speed(k, share_own, share_got):
    half = RADIUS // 2
    row = k % RADIUS
    even = lax.rem(lax.axis_index("slab"), 2) == 0
    border = at_border()
    own = lax.rem(lax.axis_index("shot"), 2) == row // half
    at_a = jnp.where(own, share_own[row % half], share_got[row % half])
    at_b = jnp.where(own, share_own[half + row % half], share_got[half + row % half])
    return (ahead if k < RADIUS else after)(even, border, at_a, at_b)


def halo_near(k, depth):
    if k < RADIUS:
        return [(r, k - RADIUS + r) for r in range(1, RADIUS + 1) if k - RADIUS + r >= 0]
    row = k - RADIUS
    return [(r, depth + row - r) for r in range(1, RADIUS + 1) if depth + row - r < depth]


def own_near(z, depth):
    near = [(r, RADIUS + z - r) for r in range(1, RADIUS + 1) if z - r < 0]
    return near + [(r, RADIUS + z + r - depth) for r in range(1, RADIUS + 1) if z + r >= depth]


def near_body(
    state, velocity, partial_u, image0, partial_q, push, weight, first_a, first_b,
    u_part, q_next, image, gain, u_edge, q_edge, u_now,
):
    depth, size_x, size_y = velocity.shape
    even = lax.rem(lax.axis_index("slab"), 2) == 0
    border = at_border()
    middle = slice(PAD, PAD + size_x)
    clear_sides(u_now, size_x)
    for k in range(2 * RADIUS):
        row = k % RADIUS
        pick = ahead if k < RADIUS else after
        u_edge[k] = pick(even, border, first_a[row], first_b[row])
        q_edge[k] = pick(even, border, first_a[RADIUS + row], first_b[RADIUS + row])
    for z in range(depth):
        near = own_near(z, depth)
        if not near:
            u_now[z, middle, :] = partial_u[z]
            q_next[z] = partial_q[z]
            image[z] = image0[z]
            continue
        v = velocity[z]
        vv = v * v
        change = vv * weighted([(r, u_edge[k]) for r, k in near])
        u_now[z, middle, :] = partial_u[z] + change
        image[z] = image0[z] + change * state[1, 0, 1, z]
        q_next[z] = partial_q[z] + vv * weighted([(r, q_edge[k]) for r, k in near])

    lane = lax.broadcasted_iota(jnp.int32, (size_x, size_y), 1)
    for z in range(depth):
        v = velocity[z]
        vv = v * v
        adjoint = q_next[z]
        drive = vv * laplacian_row(u_now, z, depth, size_x, size_y, lane) + push[z]
        u_part[z] = (2.0 * u_now[z, middle, :] - state[1, 0, 0, z]) + drive
        image[z] = weight[z] * (image[z] + drive * adjoint)
        gain[z] = (weight[z] * vv) * adjoint


def halo_field(halo, second_b, second_a, tap, share_own, share_got):
    size_x = halo.shape[1]
    even = lax.rem(lax.axis_index("slab"), 2) == 0
    border = at_border()
    for k in range(2 * RADIUS):
        row = k % RADIUS
        rows = slice(row * size_x, (row + 1) * size_x)
        pick = ahead if k < RADIUS else after
        v = halo_speed(k, share_own, share_got)
        halo[k] = pick(even, border, second_a[rows, :], second_b[rows, :]) + (v * v) * tap[k]


def image_body(
    velocity, kappa, u_part, image_own, gain, tap_u, share_own, share_got, second_b, second_a,
    u_out, keep, packed, halo, image,
):
    depth, size_x, size_y = velocity.shape
    core = lax.rem(lax.axis_index("shot"), 2)
    middle = slice(PAD, PAD + size_x)
    clear_sides(image, size_x)
    halo_field(halo, second_b, second_a, tap_u, share_own, share_got)
    for z in range(depth):
        near = own_near(z, depth)
        if not near:
            u_out[z] = u_part[z]
            image[z, middle, :] = image_own[z]
            continue
        v = velocity[z]
        crossing = weighted([(r, halo[k]) for r, k in near])
        u_out[z] = u_part[z] + (v * v) * crossing
        image[z, middle, :] = image_own[z] + gain[z] * crossing
    chip = lax.div(lax.axis_index("shot"), 2)
    chips = keep.shape[0]
    strip = size_x // (2 * chips)
    wide = strip + 4
    rows = depth * wide
    for m in range(chips):
        to = jnp.bitwise_xor(chip, m)
        for z in range(depth):
            at = PAD + 2 * m * strip - 2
            low = image[z, at : at + wide, :]
            high = image[z, at + strip : at + strip + wide, :]
            keep[to, z * wide : (z + 1) * wide, :] = jnp.where(core == 0, low, high)
            packed[pl.ds(to * rows + z * wide, wide), :] = jnp.where(core == 0, high, low)
    for j in range(3):
        at = chips * rows + j * depth
        packed[at : at + depth, :] = jnp.where(core == 0, kappa[j, :, strip - 1, :], kappa[j, :, 0, :])


def pair_sum_body(keep, got, *outs):
    rows = keep.shape[1]
    for k, out in enumerate(outs):
        out[...] = keep[k] + got[k * rows : (k + 1) * rows, :]


def strip_sum_body(*refs, count, wide):
    parts, (total, edge_b, edge_a) = refs[:count], refs[count:]
    rows = total.shape[0]
    added = parts[0][...]
    for part in parts[1:]:
        added = added + part[...]
    total[...] = added
    even = lax.rem(lax.axis_index("slab"), 2) == 0
    head = total[0 : 2 * wide, :]
    tail = total[rows - 2 * wide : rows, :]
    edge_a[...] = jnp.where(even, tail, head)
    edge_b[...] = jnp.where(even, head, tail)


def adjoint_body(
    state, velocity, u_out, q_next, push, share_own, share_got, third_a, third_b, fields, field, tap, halo, q_out, sems
):
    copy_u = pltpu.make_async_copy(u_out, fields.at[0, 0], sems.at[0])
    copy_u.start()
    depth, size_x, size_y = velocity.shape
    whole = depth + 2 * RADIUS
    middle = slice(PAD, PAD + size_x)
    clear_sides(field, size_x)
    for k in range(2 * RADIUS):
        tap[k] = weighted([(r, state[1, 0, 1, own]) for r, own in halo_near(k, depth)])
    halo_field(halo, third_b, third_a, tap, share_own, share_got)
    for z in range(whole):
        inner = RADIUS <= z < RADIUS + depth
        field[z, middle, :] = q_next[z - RADIUS] if inner else halo[z if z < RADIUS else z - depth]
    lane = lax.broadcasted_iota(jnp.int32, (size_x, size_y), 1)
    for z in range(depth):
        v = velocity[z]
        drive = (v * v) * laplacian_row(field, z + RADIUS, whole, size_x, size_y, lane) + push[z]
        q_out[z] = (2.0 * q_next[z] - state[1, 0, 1, z]) + drive
    copy_q = pltpu.make_async_copy(q_out, fields.at[0, 1], sems.at[1])
    copy_q.start()
    copy_u.wait()
    copy_q.wait()


def coefficient_body(kappa, third_b, third_a, got, far, coef, *, size_x):
    _, depth, strip, _ = kappa.shape
    even = lax.rem(lax.axis_index("slab"), 2) == 0
    border = at_border()
    shot = lax.axis_index("shot")
    even_strip = lax.rem(shot, 2) == 0
    end_strip = (shot == 0) | (shot == lax.axis_size("shot") - 1)
    facing = got[got.shape[0] - 3 * depth : got.shape[0], :]
    coef[...] = jnp.zeros(coef.shape, F32)
    for j in range(3):
        at = slice(RADIUS * size_x + j * strip, RADIUS * size_x + (j + 1) * strip)
        coef[j, 0, 1 : strip + 1, :] = ahead(even, border, third_a[at, :], third_b[at, :])
        coef[j, depth + 1, 1 : strip + 1, :] = after(even, border, third_a[at, :], third_b[at, :])
        of = slice(j * depth, (j + 1) * depth)
        left = ahead(even_strip, end_strip, facing[of, :], far[of, :])
        right = after(even_strip, end_strip, facing[of, :], far[of, :])
        for z in range(depth):
            coef[j, z + 1, 1 : strip + 1, :] = kappa[j, z]
            coef[j, z + 1, 0:1, :] = left[z : z + 1, :]
            coef[j, z + 1, strip + 1 : strip + 2, :] = right[z : z + 1, :]


def smooth_body(total, got_a, got_b, kappa, coef, velocity, momentum, new_momentum, new_speed, grad, half):
    depth, strip, size_y = momentum.shape
    column = lax.axis_index("shot") * strip
    wide = strip + 4
    even = lax.rem(lax.axis_index("slab"), 2) == 0
    border = at_border()
    for k in range(2):
        at = slice(k * wide, (k + 1) * wide)
        grad[k, 0:wide, :] = ahead(even, border, got_a[at, :], got_b[at, :])
        grad[depth + 2 + k, 0:wide, :] = after(even, border, got_a[at, :], got_b[at, :])
    for z in range(depth):
        grad[z + 2, 0:wide, :] = total[z * wide : (z + 1) * wide, :]

    def step(source, z, rows, factors):
        centre = source[z, 1 : 1 + rows, :]
        lane = lax.broadcasted_iota(jnp.int32, centre.shape, 1)
        twice = 2.0 * centre
        along_z = source[z + 1, 1 : 1 + rows, :] - twice + source[z - 1, 1 : 1 + rows, :]
        along_x = source[z, 2 : 2 + rows, :] - twice + source[z, 0:rows, :]
        after = jnp.where(lane < size_y - 1, pltpu.roll(centre, size_y - 1, 1), 0.0)
        before = jnp.where(lane >= 1, pltpu.roll(centre, 1, 1), 0.0)
        along_y = after - twice + before
        return centre + factors[0] * along_z + factors[1] * along_x + factors[2] * along_y

    for z in range(depth + 2):
        half[z, 0 : strip + 2, :] = step(grad, z + 1, strip + 2, [coef[j, z, 0 : strip + 2, :] for j in range(3)])
    for z in range(depth):
        smoothed = step(half, z + 1, strip, [kappa[j, z] for j in range(3)])
        fresh = 0.9 * momentum[z] + smoothed
        new_momentum[z] = fresh
        new_speed[z] = velocity[z, pl.ds(column, strip), :] - 0.02 * fresh


def on_device(
    velocity,
    wave_state,
    source_cells,
    source_codes,
    wavelets,
    receiver_cells,
    residuals,
    momentum,
    diffusivity,
):
    depth, size_x, size_y = velocity.shape
    strip = momentum.shape[1]
    wide = strip + 4
    slabs = lax.axis_size("slab")
    shots = lax.axis_size("shot")
    chips = shots // 2
    z_even, z_odd = even_pairs(slabs), odd_slabs(shots, slabs)
    both = ("shot", "slab")
    cube = (depth, size_x, size_y)
    padded = (depth, size_x + 2 * PAD, size_y)
    dma = pltpu.SemaphoreType.DMA

    half = RADIUS // 2
    block = shape(2 * RADIUS + half, size_x, size_y)
    out_b, out_a = call(
        pack_body, [block] * 2, tuple(pltpu.with_memory_space_constraint(x, pltpu.HBM) for x in (wave_state, velocity)), ["hbm"] * 2, ["vmem"] * 2, [dma((2 * (2 * RADIUS + half),))], us=1.3
    )
    first_b = lax.ppermute(out_b, both, z_odd)
    first_a = lax.ppermute(out_a, "slab", z_even)

    flat = shape(RADIUS * size_x, size_y)
    flat_q = shape(RADIUS * size_x + 3 * strip, size_y)
    edge = shape(RADIUS, size_x, size_y)
    ring = shape(2 * RADIUS, size_x, size_y)
    ring_scratch = pltpu.VMEM(ring.shape, F32)
    small = tuple(
        pltpu.with_memory_space_constraint(x, pltpu.HBM) for x in (source_cells, source_codes, wavelets.T)
    )
    small_scratch = [pltpu.SMEM(x.shape, x.dtype) for x in small] + [dma((3,))]
    partial_u, image0, tap_u, out_b, out_a = call(
        partial_u_body,
        [shape(*cube)] * 2 + [ring, flat, flat],
        (wave_state, velocity, *small),
        ["vmem"] * 2 + ["hbm"] * 3,
        ["vmem"] * 5,
        [pltpu.VMEM(padded, F32)] + small_scratch,
        us=1.0,
    )
    receiver_cells, out_b, out_a = lax.optimization_barrier((receiver_cells, out_b, out_a))
    second_b = lax.ppermute(out_b, both, z_odd)
    second_a = lax.ppermute(out_a, "slab", z_even)
    partial_q, push_u, push, weight, third_b, third_a, far = call(
        functools.partial(partial_q_body, scale=math.sqrt(shots * STEPS)),
        [shape(*cube)] * 4 + [flat_q, flat_q, shape(3 * depth, size_y)],
        (wave_state, velocity, receiver_cells, residuals, diffusivity, *small),
        ["vmem"] * 5 + ["hbm"] * 3,
        ["vmem"] * 7,
        [pltpu.VMEM(padded, F32), pltpu.VMEM((STEPS, depth * size_x, size_y), F32)] + small_scratch,
        us=1.3,
    )
    third_b = lax.ppermute(third_b, both, z_odd)
    third_a = lax.ppermute(third_a, "slab", z_even)

    far = lax.ppermute(far, "shot", odd_pairs(shots))
    first_a, first_b, far = lax.optimization_barrier((first_a, first_b, far))
    (share_own,) = call(share_body, [edge], (first_a, first_b), ["vmem"] * 2, ["vmem"])
    share_got = lax.ppermute(share_own, "shot", even_pairs(shots))
    u_part, q_next, image_own, gain = call(
        near_body,
        [shape(*cube)] * 4,
        (wave_state, velocity, partial_u, image0, partial_q, push_u, weight, first_a, first_b),
        ["vmem"] * 9,
        ["vmem"] * 4,
        [ring_scratch] * 2 + [pltpu.VMEM(padded, F32)],
        us=0.8,
    )

    part = shape(chips, depth * wide, size_y)
    side = 3 * depth
    u_out, keep, send = call(
        image_body,
        [shape(*cube), part, shape(chips * depth * wide + side, size_y)],
        (velocity, diffusivity, u_part, image_own, gain, tap_u, share_own, share_got, second_b, second_a),
        ["vmem"] * 10,
        ["vmem"] * 3,
        [ring_scratch, pltpu.VMEM(padded, F32)],
        us=0.3,
    )
    got = lax.ppermute(send, "shot", even_pairs(shots))
    (fields,) = call(
        adjoint_body,
        [shape(1, 2, *cube)],
        (wave_state, velocity, u_out, q_next, push, share_own, share_got, third_a, third_b),
        ["vmem"] * 9,
        ["any"],
        [
            pltpu.VMEM((depth + 2 * RADIUS, size_x + 2 * PAD, size_y), F32),
            ring_scratch,
            ring_scratch,
            pltpu.VMEM(cube, F32),
            dma((2,)),
        ],
        us=1.4,
    )
    row_block = shape(depth * wide, size_y)
    parts = call(pair_sum_body, [row_block] * chips, (keep, got), ["vmem"] * 2, ["vmem"] * chips)
    arrived = [
        lax.ppermute(parts[k], "shot", [(i, i ^ (2 * k)) for i in range(shots)]) for k in reversed(range(1, chips))
    ] + [parts[0]]
    *arrived, fields = lax.optimization_barrier((*arrived, fields))
    two = shape(2 * wide, size_y)
    total, out_b, out_a = call(
        functools.partial(strip_sum_body, count=chips, wide=wide),
        [row_block, two, two],
        arrived,
        ["vmem"] * chips,
        ["vmem"] * 3,
    )
    grad_b = lax.ppermute(out_b, both, z_odd)
    grad_a = lax.ppermute(out_a, "slab", z_even)
    tall = 8 * ((wide + 7) // 8)
    (coef,) = call(
        functools.partial(coefficient_body, size_x=size_x),
        [shape(3, depth + 2, tall, size_y)],
        (diffusivity, third_b, third_a, got, far),
        ["vmem"] * 5,
        ["vmem"],
        us=0.1,
    )
    new_momentum, new_velocity = call(
        smooth_body,
        [shape(*momentum.shape)] * 2,
        (total, grad_a, grad_b, diffusivity, coef, velocity, momentum),
        ["vmem"] * 7,
        ["block"] * 2,
        [pltpu.VMEM((depth + 4, tall, size_y), F32), pltpu.VMEM((depth + 2, tall, size_y), F32)],
        us=0.7,
    )
    return (fields, new_momentum, new_velocity)


def solution(mesh):
    return jax.shard_map(
        on_device,
        mesh=mesh,
        in_specs=(
            P("slab", None, None),
            P(None, "shot", None, "slab", None, None),
            P("shot", None),
            P("shot", None),
            P(),
            P("shot", None),
            P("shot", None, None),
            P("slab", "shot", None),
            P(None, "slab", "shot", None),
        ),
        out_specs=(
            P("shot", None, "slab", None, None),
            P("slab", "shot", None),
            P("slab", "shot", None),
        ),
        check_vma=False,
    )
```

```python
import functools
import math

import jax
import jax.numpy as jnp
from jax import lax
from jax.experimental import pallas as pl
from jax.experimental.pallas import tpu as pltpu
from jax.sharding import PartitionSpec as P

STENCIL_TAPS = (-205.0 / 72.0, 8.0 / 5.0, -1.0 / 5.0, 8.0 / 315.0, -1.0 / 560.0)
RADIUS = 4
PAD = 8
STEPS = 2
F32 = jnp.float32
BYTES_PER_US = 3.69e6


def even_pairs(count):
    return [(i, i ^ 1) for i in range(count)]


def odd_pairs(count):
    low = [(i, (i + 1) % count) for i in range(1, count, 2)]
    return low + [(b, a) for a, b in low]


def odd_slabs(shots, slabs):
    pairs = []
    for shot in range(shots):
        for slab in range(slabs):
            if slab == 0 or slab == slabs - 1:
                other = (shot ^ 1) * slabs + slab
            else:
                other = shot * slabs + (slab + 1 if slab % 2 else slab - 1)
            pairs.append((shot * slabs + slab, other))
    return pairs


def at_border():
    slab = lax.axis_index("slab")
    return (slab == 0) | (slab == lax.axis_size("slab") - 1)


def ahead(even, border, from_a, from_b):
    return jnp.where(even, jnp.where(border, 0.0, from_b), from_a)


def after(even, border, from_a, from_b):
    return jnp.where(even, from_a, jnp.where(border, 0.0, from_b))


def run_copies(pairs, sems):
    copies = [pltpu.make_async_copy(src, dst, sems.at[k]) for k, (src, dst) in enumerate(pairs)]
    for copy in copies:
        copy.start()
    return copies


SPECS = {
    "any": pl.BlockSpec(memory_space=pl.ANY),
    "hbm": pl.BlockSpec(memory_space=pltpu.HBM),
    "vmem": pl.BlockSpec(memory_space=pltpu.VMEM),
    "block": pl.BlockSpec(),
}


def call(body, out_shapes, operands, in_specs=None, out_specs=None, scratch=(), aliases=None, us=0.1):
    return pl.pallas_call(
        body,
        out_shape=list(out_shapes),
        in_specs=[SPECS[s] for s in in_specs],
        out_specs=[SPECS[s] for s in out_specs],
        scratch_shapes=list(scratch),
        input_output_aliases=aliases or {},
        cost_estimate=pl.CostEstimate(flops=0, bytes_accessed=int(us * BYTES_PER_US), transcendentals=0),
        compiler_params=pltpu.CompilerParams(vmem_limit_bytes=16 * 1024 * 1024),
    )(*operands)


def shape(*dims):
    return jax.ShapeDtypeStruct(dims, F32)


def y_sums(centre, lane, size_y):
    sums = []
    for r in range(1, RADIUS + 1):
        before = jnp.where(lane >= r, pltpu.roll(centre, r, 1), 0.0)
        after = jnp.where(lane < size_y - r, pltpu.roll(centre, size_y - r, 1), 0.0)
        sums.append(before + after)
    return sums


def laplacian_row(field, z, rows, size_x, size_y, lane):
    centre = field[z, PAD : PAD + size_x, :]
    along_y = y_sums(centre, lane, size_y)
    total = (3.0 * STENCIL_TAPS[0]) * centre
    for r in range(1, RADIUS + 1):
        ring = along_y[r - 1]
        ring = ring + (field[z, PAD + r : PAD + r + size_x, :] + field[z, PAD - r : PAD - r + size_x, :])
        if z + r < rows:
            ring = ring + field[z + r, PAD : PAD + size_x, :]
        if z - r >= 0:
            ring = ring + field[z - r, PAD : PAD + size_x, :]
        total = total + STENCIL_TAPS[r] * ring
    return total


def clear_sides(field, size_x):
    rows, _, size_y = field.shape
    edge = jnp.zeros((rows, PAD, size_y), F32)
    field[:, 0:PAD, :] = edge
    field[:, PAD + size_x : PAD + size_x + PAD, :] = edge


def pack_body(state, velocity, out_b, out_a, sems):
    depth = velocity.shape[0]
    half = RADIUS // 2
    even = lax.rem(lax.axis_index("slab"), 2) == 0
    share = lax.rem(lax.axis_index("shot"), 2) * half
    at_a = jnp.where(even, depth - RADIUS, 0)
    at_b = jnp.where(even, 0, depth - RADIUS)
    pairs = []
    for out, at in ((out_a, at_a), (out_b, at_b)):
        for k in range(RADIUS):
            pairs.append((state.at[1, 0, 0, at + k], out.at[k]))
            pairs.append((state.at[1, 0, 1, at + k], out.at[RADIUS + k]))
        for k in range(half):
            pairs.append((velocity.at[at + share + k], out.at[2 * RADIUS + k]))
    for copy in run_copies(pairs, sems):
        copy.wait()


def point_cells(cells, codes, wavelets, moment, first, size_x, size_y, act):
    plane = size_x * size_y
    row_lane = lax.broadcasted_iota(jnp.int32, (1, size_y), 1)
    for k in range(cells.shape[1]):
        cell = cells[0, k]
        amount = wavelets[moment, codes[0, k]]
        z = lax.div(cell, plane) - first
        rest = lax.rem(cell, plane)
        x = lax.div(rest, size_y)
        y = lax.rem(rest, size_y)
        act(z, x, jnp.where(row_lane == y, amount, 0.0))


def weighted(terms):
    total = None
    for r, value in terms:
        term = STENCIL_TAPS[r] * value
        total = term if total is None else total + term
    return total


def partial_u_body(
    state, velocity, source_cells, source_codes, wavelets,
    partial_u, image, tap_u, out_b, out_a,
    field, cells_here, codes_here, wavelets_here, sems,
):
    small = [(source_cells, cells_here), (source_codes, codes_here), (wavelets, wavelets_here)]
    copies = run_copies(small, sems)
    depth, size_x, size_y = velocity.shape
    even = lax.rem(lax.axis_index("slab"), 2) == 0
    clear_sides(field, size_x)
    for z in range(depth):
        field[z, PAD : PAD + size_x, :] = state[1, 0, 0, z]
    lane = lax.broadcasted_iota(jnp.int32, (size_x, size_y), 1)
    for z in range(depth):
        v = velocity[z]
        drive = (v * v) * laplacian_row(field, z, depth, size_x, size_y, lane)
        partial_u[z] = (2.0 * state[1, 0, 0, z] - state[0, 0, 0, z]) + drive
        image[z] = drive * state[1, 0, 1, z]
    for k in range(2 * RADIUS):
        tap_u[k] = weighted([(r, state[1, 0, 0, own]) for r, own in halo_near(k, depth)])

    def inject(z, x, spot):
        @pl.when((z >= 0) & (z < depth))
        def _():
            at = (z, pl.ds(x, 1), slice(None))
            v = velocity[at]
            change = (v * v) * spot
            partial_u[at] = partial_u[at] + change
            image[at] = image[at] + change * state[1, 0, 1, z, pl.ds(x, 1), :]

    for copy in copies:
        copy.wait()
    first_layer = lax.axis_index("slab") * depth
    point_cells(cells_here, codes_here, wavelets_here, 0, first_layer, size_x, size_y, inject)
    for k in range(RADIUS):
        tail = partial_u[depth - RADIUS + k]
        head = partial_u[k]
        out_a[k * size_x : (k + 1) * size_x, :] = jnp.where(even, tail, head)
        out_b[k * size_x : (k + 1) * size_x, :] = jnp.where(even, head, tail)


def partial_q_body(
    state, velocity, cells, residuals, kappa, source_cells, source_codes, wavelets,
    partial_q, push_u, push, weight, third_b, third_a, far,
    field, grid_now, cells_here, codes_here, wavelets_here, sems, *, scale,
):
    small = [(source_cells, cells_here), (source_codes, codes_here), (wavelets, wavelets_here)]
    copies = run_copies(small, sems)
    depth, size_x, size_y = velocity.shape
    strip = kappa.shape[2]
    even = lax.rem(lax.axis_index("slab"), 2) == 0
    core = lax.rem(lax.axis_index("shot"), 2)
    for j in range(3):
        far[j * depth : (j + 1) * depth, :] = jnp.where(core == 0, kappa[j, :, 0, :], kappa[j, :, strip - 1, :])
        tail = kappa[j, depth - 1]
        head = kappa[j, 0]
        at = RADIUS * size_x + j * strip
        third_a[at : at + strip, :] = jnp.where(even, tail, head)
        third_b[at : at + strip, :] = jnp.where(even, head, tail)
    clear_sides(field, size_x)
    for z in range(depth):
        field[z, PAD : PAD + size_x, :] = state[1, 0, 1, z]

    volume = depth * size_x * size_y
    count = cells.shape[1]
    ids = cells[...] - lax.axis_index("slab") * volume
    inside = (ids >= 0) & (ids < volume)
    kept = jnp.where(inside, ids, 0)
    row = lax.div(kept, jnp.int32(size_y))
    column = kept - row * size_y
    rows = depth * size_x
    pick_row = (lax.broadcasted_iota(jnp.int32, (rows, count), 0) == row).astype(F32)
    pick_column = lax.broadcasted_iota(jnp.int32, (size_y, count), 0) == column
    for moment in range(STEPS):
        amounts = jnp.where(inside, residuals[0, moment : moment + 1, :], 0.0)
        grid_now[moment] = lax.dot_general(
            pick_row,
            jnp.where(pick_column, amounts, 0.0),
            (((1,), (1,)), ((), ())),
            precision=lax.Precision.HIGHEST,
            preferred_element_type=F32,
        )

    lane = lax.broadcasted_iota(jnp.int32, (size_x, size_y), 1)
    for z in range(depth):
        at = slice(z * size_x, (z + 1) * size_x)
        v = velocity[z]
        vv = v * v
        drive = vv * (laplacian_row(field, z, depth, size_x, size_y, lane) + grid_now[0, at, :])
        partial_q[z] = (2.0 * state[1, 0, 1, z] - state[0, 0, 1, z]) + drive
        push[z] = vv * grid_now[1, at, :]
        weight[z] = -0.2 / (v * scale)
        push_u[z] = jnp.zeros((size_x, size_y), F32)

    def inject(z, x, spot):
        @pl.when((z >= 0) & (z < depth))
        def _():
            at = (z, pl.ds(x, 1), slice(None))
            v = velocity[at]
            push_u[at] = push_u[at] + (v * v) * spot

    for copy in copies:
        copy.wait()
    first_layer = lax.axis_index("slab") * depth
    point_cells(cells_here, codes_here, wavelets_here, 1, first_layer, size_x, size_y, inject)
    for k in range(RADIUS):
        tail = partial_q[depth - RADIUS + k]
        head = partial_q[k]
        third_a[k * size_x : (k + 1) * size_x, :] = jnp.where(even, tail, head)
        third_b[k * size_x : (k + 1) * size_x, :] = jnp.where(even, head, tail)


def share_body(first_a, first_b, share):
    half = RADIUS // 2
    for k in range(half):
        share[k] = first_a[2 * RADIUS + k]
        share[half + k] = first_b[2 * RADIUS + k]


def halo_speed(k, share_own, share_got):
    half = RADIUS // 2
    row = k % RADIUS
    even = lax.rem(lax.axis_index("slab"), 2) == 0
    border = at_border()
    own = lax.rem(lax.axis_index("shot"), 2) == row // half
    at_a = jnp.where(own, share_own[row % half], share_got[row % half])
    at_b = jnp.where(own, share_own[half + row % half], share_got[half + row % half])
    return (ahead if k < RADIUS else after)(even, border, at_a, at_b)


def halo_near(k, depth):
    if k < RADIUS:
        return [(r, k - RADIUS + r) for r in range(1, RADIUS + 1) if k - RADIUS + r >= 0]
    row = k - RADIUS
    return [(r, depth + row - r) for r in range(1, RADIUS + 1) if depth + row - r < depth]


def own_near(z, depth):
    near = [(r, RADIUS + z - r) for r in range(1, RADIUS + 1) if z - r < 0]
    return near + [(r, RADIUS + z + r - depth) for r in range(1, RADIUS + 1) if z + r >= depth]


def near_body(
    state, velocity, partial_u, image0, partial_q, push, weight, first_a, first_b,
    u_part, q_next, image, gain, u_edge, q_edge, u_now,
):
    depth, size_x, size_y = velocity.shape
    even = lax.rem(lax.axis_index("slab"), 2) == 0
    border = at_border()
    middle = slice(PAD, PAD + size_x)
    clear_sides(u_now, size_x)
    for k in range(2 * RADIUS):
        row = k % RADIUS
        pick = ahead if k < RADIUS else after
        u_edge[k] = pick(even, border, first_a[row], first_b[row])
        q_edge[k] = pick(even, border, first_a[RADIUS + row], first_b[RADIUS + row])
    for z in range(depth):
        near = own_near(z, depth)
        if not near:
            u_now[z, middle, :] = partial_u[z]
            q_next[z] = partial_q[z]
            image[z] = image0[z]
            continue
        v = velocity[z]
        vv = v * v
        change = vv * weighted([(r, u_edge[k]) for r, k in near])
        u_now[z, middle, :] = partial_u[z] + change
        image[z] = image0[z] + change * state[1, 0, 1, z]
        q_next[z] = partial_q[z] + vv * weighted([(r, q_edge[k]) for r, k in near])

    lane = lax.broadcasted_iota(jnp.int32, (size_x, size_y), 1)
    for z in range(depth):
        v = velocity[z]
        vv = v * v
        adjoint = q_next[z]
        drive = vv * laplacian_row(u_now, z, depth, size_x, size_y, lane) + push[z]
        u_part[z] = (2.0 * u_now[z, middle, :] - state[1, 0, 0, z]) + drive
        image[z] = weight[z] * (image[z] + drive * adjoint)
        gain[z] = (weight[z] * vv) * adjoint


def halo_field(halo, second_b, second_a, tap, share_own, share_got):
    size_x = halo.shape[1]
    even = lax.rem(lax.axis_index("slab"), 2) == 0
    border = at_border()
    for k in range(2 * RADIUS):
        row = k % RADIUS
        rows = slice(row * size_x, (row + 1) * size_x)
        pick = ahead if k < RADIUS else after
        v = halo_speed(k, share_own, share_got)
        halo[k] = pick(even, border, second_a[rows, :], second_b[rows, :]) + (v * v) * tap[k]


def image_body(
    velocity, kappa, u_part, image_own, gain, tap_u, share_own, share_got, second_b, second_a,
    u_out, keep, packed, halo, image,
):
    depth, size_x, size_y = velocity.shape
    core = lax.rem(lax.axis_index("shot"), 2)
    middle = slice(PAD, PAD + size_x)
    clear_sides(image, size_x)
    halo_field(halo, second_b, second_a, tap_u, share_own, share_got)
    for z in range(depth):
        near = own_near(z, depth)
        if not near:
            u_out[z] = u_part[z]
            image[z, middle, :] = image_own[z]
            continue
        v = velocity[z]
        crossing = weighted([(r, halo[k]) for r, k in near])
        u_out[z] = u_part[z] + (v * v) * crossing
        image[z, middle, :] = image_own[z] + gain[z] * crossing
    chip = lax.div(lax.axis_index("shot"), 2)
    chips = keep.shape[0]
    strip = size_x // (2 * chips)
    wide = strip + 4
    rows = depth * wide
    for m in range(chips):
        to = jnp.bitwise_xor(chip, m)
        for z in range(depth):
            at = PAD + 2 * m * strip - 2
            low = image[z, at : at + wide, :]
            high = image[z, at + strip : at + strip + wide, :]
            keep[to, z * wide : (z + 1) * wide, :] = jnp.where(core == 0, low, high)
            packed[pl.ds(to * rows + z * wide, wide), :] = jnp.where(core == 0, high, low)
    for j in range(3):
        at = chips * rows + j * depth
        packed[at : at + depth, :] = jnp.where(core == 0, kappa[j, :, strip - 1, :], kappa[j, :, 0, :])


def pair_sum_body(keep, got, *outs):
    rows = keep.shape[1]
    for k, out in enumerate(outs):
        out[...] = keep[k] + got[k * rows : (k + 1) * rows, :]


def strip_sum_body(*refs, count, wide):
    parts, (total, edge_b, edge_a) = refs[:count], refs[count:]
    rows = total.shape[0]
    added = parts[0][...]
    for part in parts[1:]:
        added = added + part[...]
    total[...] = added
    even = lax.rem(lax.axis_index("slab"), 2) == 0
    head = total[0 : 2 * wide, :]
    tail = total[rows - 2 * wide : rows, :]
    edge_a[...] = jnp.where(even, tail, head)
    edge_b[...] = jnp.where(even, head, tail)


def adjoint_body(
    state, velocity, u_out, q_next, push, share_own, share_got, third_a, third_b, fields, field, tap, halo, q_out, sems
):
    copy_u = pltpu.make_async_copy(u_out, fields.at[0, 0], sems.at[0])
    copy_u.start()
    depth, size_x, size_y = velocity.shape
    whole = depth + 2 * RADIUS
    middle = slice(PAD, PAD + size_x)
    clear_sides(field, size_x)
    for k in range(2 * RADIUS):
        tap[k] = weighted([(r, state[1, 0, 1, own]) for r, own in halo_near(k, depth)])
    halo_field(halo, third_b, third_a, tap, share_own, share_got)
    for z in range(whole):
        inner = RADIUS <= z < RADIUS + depth
        field[z, middle, :] = q_next[z - RADIUS] if inner else halo[z if z < RADIUS else z - depth]
    lane = lax.broadcasted_iota(jnp.int32, (size_x, size_y), 1)
    for z in range(depth):
        v = velocity[z]
        drive = (v * v) * laplacian_row(field, z + RADIUS, whole, size_x, size_y, lane) + push[z]
        q_out[z] = (2.0 * q_next[z] - state[1, 0, 1, z]) + drive
    copy_q = pltpu.make_async_copy(q_out, fields.at[0, 1], sems.at[1])
    copy_q.start()
    copy_u.wait()
    copy_q.wait()


def coefficient_body(kappa, third_b, third_a, got, far, coef, *, size_x):
    _, depth, strip, _ = kappa.shape
    even = lax.rem(lax.axis_index("slab"), 2) == 0
    border = at_border()
    shot = lax.axis_index("shot")
    even_strip = lax.rem(shot, 2) == 0
    end_strip = (shot == 0) | (shot == lax.axis_size("shot") - 1)
    facing = got[got.shape[0] - 3 * depth : got.shape[0], :]
    coef[...] = jnp.zeros(coef.shape, F32)
    for j in range(3):
        at = slice(RADIUS * size_x + j * strip, RADIUS * size_x + (j + 1) * strip)
        coef[j, 0, 1 : strip + 1, :] = ahead(even, border, third_a[at, :], third_b[at, :])
        coef[j, depth + 1, 1 : strip + 1, :] = after(even, border, third_a[at, :], third_b[at, :])
        of = slice(j * depth, (j + 1) * depth)
        left = ahead(even_strip, end_strip, facing[of, :], far[of, :])
        right = after(even_strip, end_strip, facing[of, :], far[of, :])
        for z in range(depth):
            coef[j, z + 1, 1 : strip + 1, :] = kappa[j, z]
            coef[j, z + 1, 0:1, :] = left[z : z + 1, :]
            coef[j, z + 1, strip + 1 : strip + 2, :] = right[z : z + 1, :]


def smooth_body(total, got_a, got_b, kappa, coef, velocity, momentum, new_momentum, new_speed, grad, half):
    depth, strip, size_y = momentum.shape
    column = lax.axis_index("shot") * strip
    wide = strip + 4
    even = lax.rem(lax.axis_index("slab"), 2) == 0
    border = at_border()
    for k in range(2):
        at = slice(k * wide, (k + 1) * wide)
        grad[k, 0:wide, :] = ahead(even, border, got_a[at, :], got_b[at, :])
        grad[depth + 2 + k, 0:wide, :] = after(even, border, got_a[at, :], got_b[at, :])
    for z in range(depth):
        grad[z + 2, 0:wide, :] = total[z * wide : (z + 1) * wide, :]

    def step(source, z, rows, factors):
        centre = source[z, 1 : 1 + rows, :]
        lane = lax.broadcasted_iota(jnp.int32, centre.shape, 1)
        twice = 2.0 * centre
        along_z = source[z + 1, 1 : 1 + rows, :] - twice + source[z - 1, 1 : 1 + rows, :]
        along_x = source[z, 2 : 2 + rows, :] - twice + source[z, 0:rows, :]
        after = jnp.where(lane < size_y - 1, pltpu.roll(centre, size_y - 1, 1), 0.0)
        before = jnp.where(lane >= 1, pltpu.roll(centre, 1, 1), 0.0)
        along_y = after - twice + before
        return centre + factors[0] * along_z + factors[1] * along_x + factors[2] * along_y

    for z in range(depth + 2):
        half[z, 0 : strip + 2, :] = step(grad, z + 1, strip + 2, [coef[j, z, 0 : strip + 2, :] for j in range(3)])
    for z in range(depth):
        smoothed = step(half, z + 1, strip, [kappa[j, z] for j in range(3)])
        fresh = 0.9 * momentum[z] + smoothed
        new_momentum[z] = fresh
        new_speed[z] = velocity[z, pl.ds(column, strip), :] - 0.02 * fresh


def on_device(
    velocity,
    wave_state,
    source_cells,
    source_codes,
    wavelets,
    receiver_cells,
    residuals,
    momentum,
    diffusivity,
):
    depth, size_x, size_y = velocity.shape
    strip = momentum.shape[1]
    wide = strip + 4
    slabs = lax.axis_size("slab")
    shots = lax.axis_size("shot")
    chips = shots // 2
    z_even, z_odd = even_pairs(slabs), odd_slabs(shots, slabs)
    both = ("shot", "slab")
    cube = (depth, size_x, size_y)
    padded = (depth, size_x + 2 * PAD, size_y)
    dma = pltpu.SemaphoreType.DMA

    half = RADIUS // 2
    block = shape(2 * RADIUS + half, size_x, size_y)
    out_b, out_a = call(
        pack_body, [block] * 2, tuple(pltpu.with_memory_space_constraint(x, pltpu.HBM) for x in (wave_state, velocity)), ["hbm"] * 2, ["vmem"] * 2, [dma((2 * (2 * RADIUS + half),))], us=1.3
    )
    first_b = lax.ppermute(out_b, both, z_odd)
    first_a = lax.ppermute(out_a, "slab", z_even)

    flat = shape(RADIUS * size_x, size_y)
    flat_q = shape(RADIUS * size_x + 3 * strip, size_y)
    edge = shape(RADIUS, size_x, size_y)
    ring = shape(2 * RADIUS, size_x, size_y)
    ring_scratch = pltpu.VMEM(ring.shape, F32)
    small = tuple(
        pltpu.with_memory_space_constraint(x, pltpu.HBM) for x in (source_cells, source_codes, wavelets.T)
    )
    small_scratch = [pltpu.SMEM(x.shape, x.dtype) for x in small] + [dma((3,))]
    partial_u, image0, tap_u, out_b, out_a = call(
        partial_u_body,
        [shape(*cube)] * 2 + [ring, flat, flat],
        (wave_state, velocity, *small),
        ["vmem"] * 2 + ["hbm"] * 3,
        ["vmem"] * 5,
        [pltpu.VMEM(padded, F32)] + small_scratch,
        us=1.0,
    )
    receiver_cells, out_b, out_a = lax.optimization_barrier((receiver_cells, out_b, out_a))
    second_b = lax.ppermute(out_b, both, z_odd)
    second_a = lax.ppermute(out_a, "slab", z_even)
    partial_q, push_u, push, weight, third_b, third_a, far = call(
        functools.partial(partial_q_body, scale=math.sqrt(shots * STEPS)),
        [shape(*cube)] * 4 + [flat_q, flat_q, shape(3 * depth, size_y)],
        (wave_state, velocity, receiver_cells, residuals, diffusivity, *small),
        ["vmem"] * 5 + ["hbm"] * 3,
        ["vmem"] * 7,
        [pltpu.VMEM(padded, F32), pltpu.VMEM((STEPS, depth * size_x, size_y), F32)] + small_scratch,
        us=1.3,
    )
    third_b = lax.ppermute(third_b, both, z_odd)
    third_a = lax.ppermute(third_a, "slab", z_even)

    far = lax.ppermute(far, "shot", odd_pairs(shots))
    first_a, first_b, far = lax.optimization_barrier((first_a, first_b, far))
    u_part, q_next, image_own, gain = call(
        near_body,
        [shape(*cube)] * 4,
        (wave_state, velocity, partial_u, image0, partial_q, push_u, weight, first_a, first_b),
        ["vmem"] * 9,
        ["vmem"] * 4,
        [ring_scratch] * 2 + [pltpu.VMEM(padded, F32)],
        us=0.8,
    )

    gain, first_a, first_b = lax.optimization_barrier((gain, first_a, first_b))
    (share_own,) = call(share_body, [edge], (first_a, first_b), ["vmem"] * 2, ["vmem"])
    share_got = lax.ppermute(share_own, "shot", even_pairs(shots))
    part = shape(chips, depth * wide, size_y)
    side = 3 * depth
    u_out, keep, send = call(
        image_body,
        [shape(*cube), part, shape(chips * depth * wide + side, size_y)],
        (velocity, diffusivity, u_part, image_own, gain, tap_u, share_own, share_got, second_b, second_a),
        ["vmem"] * 10,
        ["vmem"] * 3,
        [ring_scratch, pltpu.VMEM(padded, F32)],
        us=0.3,
    )
    got = lax.ppermute(send, "shot", even_pairs(shots))
    (fields,) = call(
        adjoint_body,
        [shape(1, 2, *cube)],
        (wave_state, velocity, u_out, q_next, push, share_own, share_got, third_a, third_b),
        ["vmem"] * 9,
        ["any"],
        [
            pltpu.VMEM((depth + 2 * RADIUS, size_x + 2 * PAD, size_y), F32),
            ring_scratch,
            ring_scratch,
            pltpu.VMEM(cube, F32),
            dma((2,)),
        ],
        us=1.4,
    )
    row_block = shape(depth * wide, size_y)
    parts = call(pair_sum_body, [row_block] * chips, (keep, got), ["vmem"] * 2, ["vmem"] * chips)
    arrived = [
        lax.ppermute(parts[k], "shot", [(i, i ^ (2 * k)) for i in range(shots)]) for k in reversed(range(1, chips))
    ] + [parts[0]]
    *arrived, fields = lax.optimization_barrier((*arrived, fields))
    two = shape(2 * wide, size_y)
    total, out_b, out_a = call(
        functools.partial(strip_sum_body, count=chips, wide=wide),
        [row_block, two, two],
        arrived,
        ["vmem"] * chips,
        ["vmem"] * 3,
    )
    grad_b = lax.ppermute(out_b, both, z_odd)
    grad_a = lax.ppermute(out_a, "slab", z_even)
    tall = 8 * ((wide + 7) // 8)
    (coef,) = call(
        functools.partial(coefficient_body, size_x=size_x),
        [shape(3, depth + 2, tall, size_y)],
        (diffusivity, third_b, third_a, got, far),
        ["vmem"] * 5,
        ["vmem"],
        us=0.1,
    )
    new_momentum, new_velocity = call(
        smooth_body,
        [shape(*momentum.shape)] * 2,
        (total, grad_a, grad_b, diffusivity, coef, velocity, momentum),
        ["vmem"] * 7,
        ["block"] * 2,
        [pltpu.VMEM((depth + 4, tall, size_y), F32), pltpu.VMEM((depth + 2, tall, size_y), F32)],
        us=0.7,
    )
    return (fields, new_momentum, new_velocity)


def solution(mesh):
    return jax.shard_map(
        on_device,
        mesh=mesh,
        in_specs=(
            P("slab", None, None),
            P(None, "shot", None, "slab", None, None),
            P("shot", None),
            P("shot", None),
            P(),
            P("shot", None),
            P("shot", None, None),
            P("slab", "shot", None),
            P(None, "slab", "shot", None),
        ),
        out_specs=(
            P("shot", None, "slab", None, None),
            P("slab", "shot", None),
            P("slab", "shot", None),
        ),
        check_vma=False,
    )
```
